32 devices in a mesh: seq: 8 (over y, x, core), fsdp: 4 (over z).
Axes of the slice: x: 2, y: 2, z: 4, core: 2. Of those that a mesh axis runs over, the one named last changes fastest.
Arguments:
- tokens: bfloat16 [2, 4, 1024, 2048], P(None, 'fsdp', 'seq'), may hold values from -6 to 6
- ln_gain: bfloat16 [2048], P(('seq', 'fsdp')), may hold values from 0.5 to 1.5
- ln_bias: bfloat16 [2048], P(('seq', 'fsdp')), may hold values from -1.75 to 1.75
- w_qkv: bfloat16 [2048, 6144], P(('seq', 'fsdp')), may hold values from -0.125 to 0.125
- b_qkv: bfloat16 [6144], P(('seq', 'fsdp')), may hold values from -1.75 to 1.75
- w_out: bfloat16 [2048, 2048], P(('seq', 'fsdp')), may hold values from -2 to 2
- b_out: bfloat16 [2048], P(('seq', 'fsdp')), may hold values from -1.75 to 1.75
- w_fc1: bfloat16 [2048, 8192], P(('seq', 'fsdp')), may hold values from -0.125 to 0.125
- b_fc1: bfloat16 [8192], P(('seq', 'fsdp')), may hold values from -3 to 3
- w_fc2: bfloat16 [8192, 2048], P(('seq', 'fsdp')), may hold values from -0.0625 to 0.0625
- b_fc2: bfloat16 [2048], P(('seq', 'fsdp')), may hold values from -1.75 to 1.75
- piece_starts: int32 [2, 4, 2], P(None, 'fsdp'), may hold values from 0 to 768, as said below
- cotangent: bfloat16 [2, 4, 1024, 2048], P(None, 'fsdp', 'seq'), may hold values from -6 to 6
Outputs:
- activations: bfloat16 [2, 4, 1024, 2048], P(None, 'fsdp', 'seq')
- input_grad: float32 [2, 4, 1024, 2048], P(None, 'fsdp', 'seq')
- grad_ln_gain: float32 [2048], P(('seq', 'fsdp'))
- grad_ln_bias: float32 [2048], P(('seq', 'fsdp'))
- grad_w_qkv: float32 [2048, 6144], P(('seq', 'fsdp'))
- grad_b_qk: float32 [4096], P(('seq', 'fsdp'))
- grad_b_v: float32 [2048], P(('seq', 'fsdp'))
- grad_w_out: float32 [2048, 2048], P(('seq', 'fsdp'))
- grad_b_out: float32 [2048], P(('seq', 'fsdp'))
- grad_w_fc1: float32 [2048, 8192], P(('seq', 'fsdp'))
- grad_b_fc1: float32 [8192], P(('seq', 'fsdp'))
- grad_w_fc2: float32 [8192, 2048], P(('seq', 'fsdp'))
- grad_b_fc2: float32 [2048], P(('seq', 'fsdp'))
The draws below stay inside these ranges and needn't reach their ends.
Inputs may be any that keep to these rules, and one draw needn't show every extreme that they name: `piece_starts`: in each sequence the 2 pieces are disjoint and in increasing order; piece p starts in [p * 512, (p + 1) * 512 - 256].
All inputs are finite; a program needn't handle non-finite values.
Results may differ from the reference program's by a relative error of at most 0.015.
Values may be sent and summed in bfloat16 or wider, within the bound.
A program may use at most 512 MiB of HBM per device.

```python
import math
import jax
import jax.numpy as jnp
from jax import lax

D = 2048
HEADS = 32
HEAD_DIM = 64
FF = 8192
ROT = 32
IMG = 256
PIECES = 2
MB = 2
SEQLEN = 1024
GROUPS = 4


def draw_piece_starts(key, part):
    segment = SEQLEN // PIECES
    offsets = jax.random.randint(key, (MB, GROUPS, PIECES), 0, segment - IMG + 1)
    starts = offsets + segment * jnp.arange(PIECES, dtype=jnp.int32)[None, None, :]
    starts = starts.at[0, 0, 0].set(0)
    starts = starts.at[MB - 1, GROUPS - 1, PIECES - 1].set(SEQLEN - IMG)
    return starts.astype(jnp.int32)


def with_spikes(values, own_key, source, target, blocks, factor):
    def block_of(dim):
        return (jnp.arange(values.shape[dim]) // (values.shape[dim] // blocks)).reshape((-1,) + (1,) * (values.ndim - 1 - dim))

    first = jax.random.permutation(own_key, blocks)[block_of(target)]
    other_side = (block_of(target) + blocks // 2) % blocks
    return jnp.where((block_of(source) == first) | (block_of(source) == other_side), factor * values, values)


def level_of(own_key, extent, cuts, low, largest):
    def one(axis_at, blocks):
        draws = jax.random.uniform(jax.random.fold_in(jax.random.fold_in(own_key, 6), axis_at), (blocks,), jnp.float32, low / len(cuts), largest / len(cuts))
        return jnp.repeat(jnp.exp(draws), extent[axis_at] // blocks).reshape((-1,) + (1,) * (len(extent) - axis_at - 1))

    level = one(*cuts[0])
    for cut in cuts[1:]:
        level = level * one(*cut)
    return level


def normal_values(key, extent, scale, reach, cuts=(), kind=jnp.bfloat16):
    result = jax.random.normal(key, extent, jnp.float32) * scale
    if len(cuts) > 0:
        result = level_of(key, extent, cuts, -0.22, 0.18) * result
    return jnp.clip(result, min=-reach, max=reach).astype(kind)


def gaussian_with(rng, extent, deviation, most, split, heavy, held_as=jnp.bfloat16):
    values = deviation * jax.random.normal(rng, extent, jnp.float32)
    if split:
        values = values * level_of(rng, extent, split, -0.22, 0.18)
    return jnp.clip(with_spikes(values, jax.random.fold_in(rng, 3), *heavy), -most, most).astype(held_as)


def setup_inputs(seed: int = 0) -> dict:
    splits = jax.random.split(jax.random.key(seed), 14)
    tokens = gaussian_with(splits[0], (MB, GROUPS, SEQLEN, D), 1.0, 6.0, ((1, 4), (2, 8)), (2, 3, 8, 2.0))
    ln_gain = jnp.clip(1.0 + 0.1 * jax.random.normal(splits[1], (D,), jnp.float32), 0.5, 1.5).astype(jnp.bfloat16)
    ln_bias = normal_values(splits[2], (D,), 0.3, 1.75, ((0, 32),))
    w_qkv = normal_values(splits[3], (D, 3 * D), D ** -0.5, 0.125, ((0, 32),))
    b_qkv = normal_values(splits[4], (3 * D,), 0.3, 1.75, ((0, 32),))
    w_out = normal_values(splits[5], (D, D), (max(1, 4 * D // SEQLEN)) ** -0.5, 2.0, ((0, 32),))
    b_out = normal_values(splits[6], (D,), 0.3, 1.75, ((0, 32),))
    w_fc1 = normal_values(splits[7], (D, FF), D ** -0.5, 0.125, ((0, 32),))
    b_fc1 = normal_values(splits[8], (FF,), 0.5, 3.0, ((0, 32),))
    w_fc2 = normal_values(splits[9], (FF, D), FF ** -0.5, 0.0625, ((0, 32),))
    b_fc2 = normal_values(splits[10], (D,), 0.3, 1.75, ((0, 32),))
    piece_starts = draw_piece_starts(jax.random.fold_in(splits[13], 71), 0)
    cotangent = gaussian_with(splits[12], (MB, GROUPS, SEQLEN, D), 1.0, 6.0, ((1, 4), (2, 8)), (2, 3, 8, 2.0))
    return dict(tokens=tokens, ln_gain=ln_gain, ln_bias=ln_bias, w_qkv=w_qkv, b_qkv=b_qkv, w_out=w_out, b_out=b_out, w_fc1=w_fc1, b_fc1=b_fc1, w_fc2=w_fc2, b_fc2=b_fc2, piece_starts=piece_starts, cotangent=cotangent)


EPSILON = 1e-05
HIGH = lax.Precision.HIGHEST

@jax.custom_vjp
def low(v):
    return lax.optimization_barrier(v.astype(jnp.bfloat16)).astype(jnp.float32)

@jax.custom_vjp
def low_back(v):
    return v

def low_keep(v):
    return (low(v), None)

def low_pass(kept, grad):
    return (grad,)

def back_keep(v):
    return (v, None)

def back_low(kept, grad):
    return (low(grad),)
low.defvjp(low_keep, low_pass)
low_back.defvjp(back_keep, back_low)

def matmul(left, right):
    return jnp.dot(left, right, precision=HIGH, preferred_element_type=jnp.float32)

def layer_norm(values, ln_scale, ln_shift):
    center = values - lax.optimization_barrier(jnp.mean(values, axis=-1, keepdims=True))
    spread = lax.optimization_barrier(jnp.mean(center * center, axis=-1, keepdims=True))
    return center * lax.rsqrt(spread + EPSILON) * ln_scale + ln_shift

def rotate(values, positions):
    half_dims = ROT // 2
    frequency = 10000.0 ** (-2.0 * jnp.arange(half_dims, dtype=jnp.float32) / ROT)
    angles = positions.astype(jnp.float32)[:, None] * frequency[None, :]
    cosine = jnp.cos(angles)[:, None, :]
    sine_part = jnp.sin(angles)[:, None, :]
    front_part = values[..., :half_dims]
    back_part = values[..., half_dims:ROT]
    return jnp.concatenate([front_part * cosine - back_part * sine_part, back_part * cosine + front_part * sine_part, values[..., ROT:]], axis=-1)

def piece_index(positions, starts):
    inside = (positions[:, None] >= starts[None, :]) & (positions[:, None] < starts[None, :] + IMG)
    labels = jnp.arange(1, PIECES + 1, dtype=jnp.int32)
    return (lax.optimization_barrier(jnp.sum(jnp.where(inside, labels[None, :], 0), axis=1)) - 1).astype(jnp.int32)

def visible(query_pos, query_piece, key_pos, key_piece):
    causal = key_pos[None, :] <= query_pos[:, None]
    same_piece = (query_piece[:, None] == key_piece[None, :]) & (query_piece[:, None] >= 0)
    return causal | same_piece

def one_sequence(params, sequence_pair):
    tokens_seq, starts = sequence_pair
    ln_scale, ln_shift, wide_qkv, bias_qkv, wide_out, bias_out, wide_fc1, bias_fc1, wide_fc2, bias_fc2 = params
    positions = jnp.arange(SEQLEN, dtype=jnp.int32)
    normed = low(layer_norm(tokens_seq, ln_scale, ln_shift))
    projected = low_back(matmul(normed, wide_qkv) + bias_qkv)
    queries = low(rotate(projected[:, :D].reshape(SEQLEN, HEADS, HEAD_DIM), positions))
    key_rows = low(rotate(projected[:, D:2 * D].reshape(SEQLEN, HEADS, HEAD_DIM), positions))
    value_rows = low(projected[:, 2 * D:].reshape(SEQLEN, HEADS, HEAD_DIM))
    pieces = piece_index(positions, starts)
    score_scale = 1.0 / math.sqrt(HEAD_DIM)
    block_rows = math.gcd(SEQLEN, 512)
    block_count = SEQLEN // block_rows

    def attend(block_args):
        query_block, query_pos, query_piece = block_args
        scores = jnp.einsum('qhd,khd->hqk', query_block, key_rows, precision=HIGH) * score_scale
        scores = low_back(scores)
        allowed = visible(query_pos, query_piece, positions, pieces)
        scores = jnp.where(allowed[None], scores, -1e+30)
        row_max = lax.optimization_barrier(jnp.max(scores, axis=-1, keepdims=True))
        weights = jnp.exp(scores - row_max)
        weights = low(weights / lax.optimization_barrier(jnp.sum(weights, axis=-1, keepdims=True)))
        return jnp.einsum('hqk,khd->qhd', weights, value_rows, precision=HIGH)
    attended = lax.map(jax.checkpoint(attend), (queries.reshape(block_count, block_rows, HEADS, HEAD_DIM), positions.reshape(block_count, block_rows), pieces.reshape(block_count, block_rows)))
    mixed_heads = low(low_back(attended.reshape(SEQLEN, D)))
    attn_branch = matmul(mixed_heads, wide_out) + bias_out
    hidden_pre = low_back(matmul(normed, wide_fc1) + bias_fc1)
    hidden = low(jax.nn.gelu(hidden_pre, approximate=True))
    return tokens_seq + attn_branch + matmul(hidden, wide_fc2) + bias_fc2

def reference(tokens, ln_gain, ln_bias, w_qkv, b_qkv, w_out, b_out, w_fc1, b_fc1, w_fc2, b_fc2, piece_starts, cotangent):
    params = (ln_gain.astype(jnp.float32), ln_bias.astype(jnp.float32), w_qkv.astype(jnp.float32), b_qkv.astype(jnp.float32), w_out.astype(jnp.float32), b_out.astype(jnp.float32), w_fc1.astype(jnp.float32), b_fc1.astype(jnp.float32), w_fc2.astype(jnp.float32), b_fc2.astype(jnp.float32))
    inputs = tokens.astype(jnp.float32).reshape(MB * GROUPS, SEQLEN, D)
    starts = piece_starts.reshape(MB * GROUPS, PIECES).astype(jnp.int32)

    def forward(layer_in, layer_params):
        return lax.map(jax.checkpoint(lambda sequence_pair: one_sequence(layer_params, sequence_pair)), (layer_in, starts))
    output, pullback = jax.vjp(forward, inputs, params)
    grad_in, grad_params = pullback(cotangent.astype(jnp.float32).reshape(MB * GROUPS, SEQLEN, D))
    bias_grad = grad_params[3]
    return (output.reshape(tokens.shape).astype(jnp.bfloat16), grad_in.reshape(tokens.shape), grad_params[0], grad_params[1], grad_params[2], bias_grad[:2 * D], bias_grad[2 * D:], grad_params[4], grad_params[5], grad_params[6], grad_params[7], grad_params[8], grad_params[9])
```

```python
import functools
import math

import jax
import jax.numpy as jnp
from jax import lax
from jax.experimental import pallas as pl
from jax.experimental.pallas import tpu as pltpu
from jax.sharding import PartitionSpec as P

HEADS = 32
HEAD_DIM = 64
ROT = 32
IMG = 256
PIECES = 2
EPSILON = 1e-05
BF = jnp.bfloat16
F32 = jnp.float32
SCALE = 1.0 / math.sqrt(HEAD_DIM)
LANES = 2 * HEAD_DIM


def swap(value, bit):
    size = lax.axis_size("seq")
    return lax.ppermute(value, "seq", [(i, i ^ bit) for i in range(size)])


def gather_seq(rows):
    size = lax.axis_size("seq")
    count = size.bit_length() - 1
    micro, length, width = rows.shape
    half = width // 2
    wide = []
    bits = list(range(1, count))
    for part, order in ((rows[..., :half], bits), (rows[..., half:], bits[::-1])):
        held = part.reshape((micro,) + (1,) * (count - 1) + (length, half))
        for bit in order:
            other = swap(held, 1 << bit)
            held = jnp.concatenate([held, other], axis=count - bit)
        wide.append(held.reshape(micro, size // 2, length, half))
    both = [jnp.stack([part, swap(part, 1)], axis=2) for part in wide]
    return jnp.concatenate(both, axis=-1).reshape(micro, size, length, width)


def scatter_seq(terms):
    size = lax.axis_size("seq")
    count = size.bit_length() - 1
    micro, _, length, width = terms.shape
    half = width // 2
    pairs = terms.reshape(micro, size // 2, 2, length, width)
    bits = list(range(1, count))
    sums = []
    for cols, order in ((slice(0, half), bits), (slice(half, width), bits[::-1])):
        held = pairs[:, :, 0, :, cols].astype(F32) + swap(pairs[:, :, 1, :, cols], 1).astype(F32)
        held = held.reshape((micro,) + (2,) * (count - 1) + (length, half))
        for bit in order:
            axis = count - bit
            held = held.astype(BF)
            away = lax.slice_in_dim(held, 1, 2, axis=axis)
            kept = lax.slice_in_dim(held, 0, 1, axis=axis)
            held = kept.astype(F32) + swap(away, 1 << bit).astype(F32)
        sums.append(held.reshape(micro, length, half))
    return jnp.concatenate(sums, axis=-1)


def gather_fsdp(mine, place):
    size = lax.axis_size("fsdp")
    at = lax.axis_index("fsdp")
    right = [mine]
    left = [mine]
    for step in range(1, size):
        right.append(
            lax.ppermute(right[-1], "fsdp", [(i, i + 1) for i in range(step - 1, size - 1)])
        )
        left.append(lax.ppermute(left[-1], "fsdp", [(i + 1, i) for i in range(0, size - step)]))
    out = place(None, mine, at)
    for step in range(1, size):
        piece = jnp.where(at >= step, right[step], left[size - step])
        out = place(out, piece, lax.rem(at - step + size, size))
    return out


def scatter_fsdp(chunk):
    size = lax.axis_size("fsdp")
    at = lax.axis_index("fsdp")
    right = left = None
    for step in range(1, size):
        going = chunk(jnp.minimum(size - step + at, size - 1))
        coming = chunk(jnp.maximum(step - size + at, 0))
        if step > 1:
            going = (going.astype(F32) + right.astype(F32)).astype(BF)
            coming = (coming.astype(F32) + left.astype(F32)).astype(BF)
        right = lax.ppermute(going, "fsdp", [(i, i + 1) for i in range(min(step, size - 1))])
        left = lax.ppermute(
            coming, "fsdp", [(size - 1 - i, size - 2 - i) for i in range(min(step, size - 1))]
        )
    return chunk(at).astype(F32) + right.astype(F32) + left.astype(F32)


def by_index(blocks):
    me = lax.axis_index("seq")
    shape = blocks.shape
    for bit in range(shape[0].bit_length() - 1):
        split = blocks.reshape((-1, 2, 1 << bit) + shape[1:])
        blocks = jnp.where((me >> bit) & 1 == 1, split[:, ::-1], split).reshape(shape)
    return blocks


def gather_small(vector):
    size, depth = lax.axis_size("seq"), lax.axis_size("fsdp")
    held = vector[None]
    for bit in range(size.bit_length() - 1):
        held = jnp.concatenate([held, swap(held, 1 << bit)], axis=0)
    deep = [held] + [
        lax.ppermute(held, "fsdp", [(i, (i + step) % depth) for i in range(depth)])
        for step in range(1, depth)
    ]
    deep = jnp.stack(deep[::-1] * 2, axis=1)
    start = depth - 1 - lax.axis_index("fsdp")
    return by_index(lax.dynamic_slice_in_dim(deep, start, depth, 1))


def scatter_small(terms):
    size, depth = lax.axis_size("seq"), lax.axis_size("fsdp")
    held = by_index(terms)
    for bit in reversed(range(size.bit_length() - 1)):
        n = held.shape[0] // 2
        held = held[:n] + swap(held[n:], 1 << bit)
    at = lax.axis_index("fsdp")
    held = held[0]
    total = lax.dynamic_index_in_dim(held, at, 0, keepdims=False)
    for step in range(1, depth):
        away = lax.dynamic_index_in_dim(held, (at + step) % depth, 0, keepdims=False)
        total = total + lax.ppermute(
            away, "fsdp", [(i, (i + step) % depth) for i in range(depth)]
        )
    return total


def attention_kernel(
    blocks,
    length,
    me_ref,
    starts_ref,
    cos_ref,
    sin_ref,
    q_ref,
    k_ref,
    v_ref,
    do_ref,
    mixed_ref,
    dq_ref,
    dk_ref,
    dv_ref,
    q_s,
    k_s,
    v_s,
    do_s,
    dk_s,
    dv_s,
    bias_s,
):
    micro = pl.program_id(0)
    me = me_ref[0]
    total = blocks * length
    tile = 256
    lane = lax.broadcasted_iota(jnp.int32, (1, LANES), 1)
    low_lane = (lane % HEAD_DIM) < (ROT // 2)

    def turn(value, cosine, sine):
        other = jnp.where(
            low_lane,
            pltpu.roll(value, LANES - ROT // 2, 1),
            pltpu.roll(value, ROT // 2, 1),
        )
        return value * cosine + other * sine

    for block in range(blocks):
        source = me ^ block
        at = slice(block * length, (block + 1) * length)
        cosine, sine = cos_ref[at, :], sin_ref[at, :]
        q_s[at, :] = (turn(q_ref[0, source], cosine, sine)).astype(BF) * jnp.asarray(SCALE, BF)
        k_s[at, :] = turn(k_ref[0, source], cosine, sine).astype(BF)
        v_s[at, :] = v_ref[0, source].astype(BF)
        do_s[at, :] = do_ref[0, source]
    dk_s[...] = jnp.zeros_like(dk_s)
    dv_s[...] = jnp.zeros_like(dv_s)

    def label(positions):
        found = jnp.full(positions.shape, -1, jnp.int32)
        for piece in range(PIECES):
            start = starts_ref[micro, piece]
            found = jnp.where((positions >= start) & (positions < start + IMG), piece, found)
        return found

    for first in range(0, total, tile):
        last = min(total, first + tile + IMG)
        qpos = first + lax.broadcasted_iota(jnp.int32, (tile, 1), 0)
        kpos = first + lax.broadcasted_iota(jnp.int32, (1, last - first), 1)
        qlab, klab = label(qpos), label(kpos)
        allowed = (kpos <= qpos) | ((qlab == klab) & (qlab >= 0))
        bias_s[:, : last - first] = jnp.where(allowed, 0.0, -1e30)
        rows = slice(first, first + tile)
        keys = k_s[:last, :]
        values = v_s[:last, :]
        mixed = jnp.zeros((tile, LANES), F32)
        dq = jnp.zeros((tile, LANES), F32)
        for head in range(LANES // HEAD_DIM):
            mine = (lane // HEAD_DIM) == head
            q = jnp.where(mine, q_s[rows, :], 0)
            do = jnp.where(mine, do_s[rows, :], 0)
            dims = (((1,), (1,)), ((), ()))
            s = lax.dot_general(q, keys, dims, preferred_element_type=F32)
            if first:
                s = jnp.concatenate(
                    [s[:, :first], s[:, first:] + bias_s[:, : last - first]], axis=1
                )
            else:
                s = s + bias_s[:, : last - first]
            p = jnp.exp(s - jnp.max(s, axis=1, keepdims=True))
            p = p * (1.0 / jnp.sum(p, axis=1, keepdims=True))
            probs = p.astype(BF)
            att = jnp.dot(probs, values, preferred_element_type=F32)
            mixed = jnp.where(mine, att, mixed)
            dp = lax.dot_general(do, values, dims, preferred_element_type=F32)
            delta = jnp.sum(p * dp, axis=1, keepdims=True)
            ds = (p * (dp - delta)).astype(BF)
            dq = jnp.where(mine, jnp.dot(ds, keys, preferred_element_type=F32), dq)
            over = (((0,), (0,)), ((), ()))
            dk_s[:last, :] += lax.dot_general(ds, q, over, preferred_element_type=F32)
            dv_s[:last, :] += lax.dot_general(probs, do, over, preferred_element_type=F32)
        dq = dq * SCALE
        for part in range(tile // length):
            block = first // length + part
            here = slice(part * length, (part + 1) * length)
            at = slice(block * length, (block + 1) * length)
            mixed_ref[0, me ^ block] = mixed[here].astype(BF)
            dq_ref[0, me ^ block] = turn(dq[here], cos_ref[at, :], -sin_ref[at, :]).astype(BF)
    for block in range(blocks):
        at = slice(block * length, (block + 1) * length)
        dk_ref[0, me ^ block] = turn(dk_s[at, :], cos_ref[at, :], -sin_ref[at, :]).astype(BF)
        dv_ref[0, me ^ block] = dv_s[at, :].astype(BF)


def attention(starts, projected, mixed_grad):
    micro, blocks, length, cols = mixed_grad.shape
    total = blocks * length
    groups = cols // LANES
    half = ROT // 2
    frequency = 10000.0 ** (-2.0 * jnp.arange(half, dtype=F32) / ROT)
    angles = jnp.arange(total, dtype=jnp.int32).astype(F32)[:, None] * frequency[None, :]
    cosine, sine = jnp.cos(angles), jnp.sin(angles)
    ones = jnp.ones((total, HEAD_DIM - ROT), F32)
    cosine = jnp.concatenate([cosine, cosine, ones] * 2, axis=1)
    sine = jnp.concatenate([-sine, sine, 0 * ones] * 2, axis=1)

    def spec(offset):
        return pl.BlockSpec(
            (1, blocks, length, LANES), lambda m, g, offset=offset: (m, 0, 0, offset * groups + g)
        )

    table = pl.BlockSpec((total, LANES), lambda m, g: (0, 0))
    shape = jax.ShapeDtypeStruct(mixed_grad.shape, BF)
    return pl.pallas_call(
        functools.partial(attention_kernel, blocks, length),
        grid=(micro, groups),
        in_specs=[
            pl.BlockSpec(memory_space=pltpu.SMEM),
            pl.BlockSpec(memory_space=pltpu.SMEM),
            table,
            table,
            spec(0),
            spec(1),
            spec(2),
            spec(0),
        ],
        out_specs=[spec(0)] * 4,
        out_shape=[shape] * 4,
        scratch_shapes=[pltpu.VMEM((total, LANES), BF)] * 4
        + [pltpu.VMEM((total, LANES), F32)] * 2
        + [pltpu.VMEM((256, 512), F32)],
        compiler_params=pltpu.CompilerParams(vmem_limit_bytes=48 * 1024 * 1024),
        cost_estimate=pl.CostEstimate(
            flops=micro * groups * 40 * total * total * HEAD_DIM,
            bytes_accessed=micro * groups * total * LANES * 22,
            transcendentals=micro * groups * 2 * total * total,
        ),
    )(lax.axis_index("seq")[None], starts, cosine, sine, projected, projected, projected, mixed_grad)


def gelu_tanh(values):
    return jax.nn.gelu(values, approximate=True)


def layer_norm(values, gain, shift):
    center = values - jnp.mean(values, axis=-1, keepdims=True)
    spread = jnp.mean(center * center, axis=-1, keepdims=True)
    return center * lax.rsqrt(spread + EPSILON) * gain + shift


def per_device(
    tokens,
    ln_gain,
    ln_bias,
    w_qkv,
    b_qkv,
    w_out,
    b_out,
    w_fc1,
    b_fc1,
    w_fc2,
    b_fc2,
    piece_starts,
    cotangent,
):
    size, depth = lax.axis_size("seq"), lax.axis_size("fsdp")
    me = lax.axis_index("seq")
    micro, _, length, width = tokens.shape
    rows = width // (size * depth)
    hidden_rows = w_fc2.shape[0]
    cols = width // size
    units = hidden_rows * depth
    tokens = tokens[:, 0]
    upstream = cotangent[:, 0]

    smalls = [ln_gain, ln_bias, b_qkv, b_out, b_fc1, b_fc2]
    sizes = [v.shape[0] for v in smalls]
    small = gather_small(jnp.concatenate(smalls)).astype(F32)
    full = []
    start = 0
    for count in sizes:
        full.append(small[:, :, start : start + count].reshape(-1))
        start += count
    gain, shift, bias_qkv, bias_out, bias_one, bias_two = full

    def to_columns(weight, parts):
        split = weight.reshape(rows, parts, size, -1).transpose(2, 0, 1, 3)
        split = split.reshape(size, rows, -1)
        return lax.all_to_all(split, "seq", 0, 0, tiled=True)

    def place_columns(buffer, piece, origin):
        if buffer is None:
            buffer = jnp.zeros((size, depth) + piece.shape[1:], piece.dtype)
        return lax.dynamic_update_slice_in_dim(buffer, piece[:, None], origin, 1)

    def place_rows(buffer, piece, origin):
        if buffer is None:
            buffer = jnp.zeros((depth,) + piece.shape, piece.dtype)
        return lax.dynamic_update_slice_in_dim(buffer, piece[None], origin, 0)

    all_tokens = gather_seq(tokens)
    my_out = gather_fsdp(w_out, place_rows).reshape(cols, width)
    my_qkv = gather_fsdp(to_columns(w_qkv, 3), place_columns).reshape(width, 3 * cols)
    all_up = gather_seq(upstream)
    my_one = gather_fsdp(to_columns(w_fc1, 1), place_columns).reshape(width, units)
    my_two = gather_fsdp(w_fc2, place_rows).reshape(units, width)

    count = micro * size * length
    bias_qkv = lax.dynamic_slice_in_dim(bias_qkv.reshape(3, width), me * cols, cols, 1).reshape(-1)
    bias_one = lax.dynamic_slice_in_dim(bias_one, me * units, units, 0)

    normed = layer_norm(all_tokens.astype(F32), gain, shift).astype(BF).reshape(count, width)
    up = all_up.reshape(count, width)

    def contract_last(left, right):
        return lax.dot_general(left, right, (((1,), (1,)), ((), ())), preferred_element_type=F32)

    def contract_first(left, right):
        return lax.dot_general(left, right, (((0,), (0,)), ((), ())), preferred_element_type=F32)

    projected = jnp.dot(normed, my_qkv, preferred_element_type=F32) + bias_qkv
    mixed_grad = contract_last(up, my_out).astype(BF)
    mixed, dq, dk, dv = attention(
        piece_starts[:, 0],
        projected.reshape(micro, size, length, 3 * cols),
        mixed_grad.reshape(micro, size, length, cols),
    )
    mixed = mixed.reshape(count, cols)
    projected_grad = jnp.concatenate([dq, dk, dv], axis=-1).reshape(count, 3 * cols)

    pre = jnp.dot(normed, my_one, preferred_element_type=F32) + bias_one
    hidden, back = jax.vjp(gelu_tanh, pre)
    hidden = hidden.astype(BF)
    pre_grad = back(contract_last(up, my_two))[0].astype(BF)

    terms = jnp.dot(mixed, my_out, preferred_element_type=F32)
    terms = terms + jnp.dot(hidden, my_two, preferred_element_type=F32)
    sums = scatter_seq(terms.astype(BF).reshape(micro, size, length, width))
    activations = (tokens.astype(F32) + sums + (bias_out + bias_two)).astype(BF)

    grad_terms = contract_last(projected_grad, my_qkv) + contract_last(pre_grad, my_one)
    normed_grad = scatter_seq(grad_terms.astype(BF).reshape(micro, size, length, width))
    _, norm_back = jax.vjp(layer_norm, tokens.astype(F32), gain, shift)
    input_grad, gain_grad, shift_grad = norm_back(normed_grad)
    input_grad = input_grad + upstream.astype(F32)

    def scatter_rows(grad):
        grad = grad.astype(BF).reshape(depth, -1, width)
        return scatter_fsdp(lambda o: lax.dynamic_index_in_dim(grad, o, 0, keepdims=False))

    def scatter_columns(grad, parts):
        grad = grad.astype(BF).reshape(size, depth, rows, -1)
        mine = scatter_fsdp(lambda o: lax.dynamic_index_in_dim(grad, o, 1, keepdims=False))
        mine = lax.all_to_all(mine.astype(BF), "seq", 0, 0, tiled=True).astype(F32)
        mine = mine.reshape(size, rows, parts, -1).transpose(1, 2, 0, 3)
        return mine.reshape(rows, -1)

    grad_two = scatter_rows(contract_first(hidden, up))
    grad_out = scatter_rows(contract_first(mixed, up))
    grad_one = scatter_columns(contract_first(normed, pre_grad), 1)
    grad_qkv = scatter_columns(contract_first(normed, projected_grad), 3)

    def put(values, extent, at):
        return lax.dynamic_update_slice_in_dim(jnp.zeros(extent, F32), values, at, -1)

    bqkv = jnp.sum(projected_grad.astype(F32), axis=0).reshape(3, cols)
    bqkv = put(bqkv, (3, width), me * cols)
    bone = put(jnp.sum(pre_grad.astype(F32), axis=0), (size * units,), me * units)
    btwo = jnp.sum(upstream.astype(F32), axis=(0, 1))
    packed = [gain_grad, shift_grad, bqkv[:2], bqkv[2], bone, btwo]
    packed = [v.reshape(size, depth, -1) for v in packed]
    summed = scatter_small(jnp.concatenate(packed, axis=-1))
    parts = []
    start = 0
    for v in packed:
        parts.append(summed[start : start + v.shape[-1]])
        start += v.shape[-1]
    return (
        activations[:, None],
        input_grad[:, None],
        parts[0],
        parts[1],
        grad_qkv,
        parts[2],
        parts[3],
        grad_out,
        parts[5],
        grad_one,
        parts[4],
        grad_two,
        parts[5],
    )


def solution(mesh):
    both = ("seq", "fsdp")
    row = P(both)
    matrix = P(both, None)
    tokens = P(None, "fsdp", "seq", None)
    weights = (row, row, matrix, row, matrix, row, matrix, row, matrix, row)
    grads = (row, row, matrix, row, row, matrix, row, matrix, row, matrix, row)
    return jax.shard_map(
        per_device,
        mesh=mesh,
        in_specs=(tokens,) + weights + (P(None, "fsdp", None), tokens),
        out_specs=(tokens, tokens) + grads,
        check_vma=False,
    )
```

```python
import functools
import math

import jax
import jax.numpy as jnp
from jax import lax
from jax.experimental import pallas as pl
from jax.experimental.pallas import tpu as pltpu
from jax.sharding import PartitionSpec as P

HEADS = 32
HEAD_DIM = 64
ROT = 32
IMG = 256
PIECES = 2
EPSILON = 1e-05
BF = jnp.bfloat16
F32 = jnp.float32
SCALE = 1.0 / math.sqrt(HEAD_DIM)
LANES = 2 * HEAD_DIM


def swap(value, bit):
    size = lax.axis_size("seq")
    return lax.ppermute(value, "seq", [(i, i ^ bit) for i in range(size)])


def scatter_seq(terms):
    size = lax.axis_size("seq")
    me = lax.axis_index("seq")
    count = size.bit_length() - 1
    micro, _, length, width = terms.shape
    half = width // 2
    bits = list(range(1, count))

    def exchange(held, bit, axis):
        held = held.astype(BF)
        mine = (me >> bit) & 1
        away = lax.dynamic_index_in_dim(held, 1 - mine, axis, keepdims=False)
        kept = lax.dynamic_index_in_dim(held, mine, axis, keepdims=False)
        return kept.astype(F32) + swap(away, 1 << bit).astype(F32)

    sums = []
    for cols, order in ((slice(0, half), bits), (slice(half, width), bits[::-1])):
        held = terms[..., cols].reshape((micro,) + (2,) * count + (length, half))
        left = list(range(count))[::-1]
        for bit in [0] + order:
            held = exchange(held, bit, 1 + left.index(bit))
            left.remove(bit)
        sums.append(held)
    return jnp.concatenate(sums, axis=-1)


def by_index(blocks):
    me = lax.axis_index("seq")
    shape = blocks.shape
    for bit in range(shape[0].bit_length() - 1):
        split = blocks.reshape((-1, 2, 1 << bit) + shape[1:])
        blocks = jnp.where((me >> bit) & 1 == 1, split[:, ::-1], split).reshape(shape)
    return blocks


def scatter_small(terms):
    size, depth = lax.axis_size("seq"), lax.axis_size("fsdp")
    held = by_index(terms)
    for bit in reversed(range(size.bit_length() - 1)):
        n = held.shape[0] // 2
        held = held[:n] + swap(held[n:], 1 << bit)
    at = lax.axis_index("fsdp")
    held = held[0]
    total = lax.dynamic_index_in_dim(held, at, 0, keepdims=False)
    for step in range(1, depth):
        away = lax.dynamic_index_in_dim(held, (at + step) % depth, 0, keepdims=False)
        total = total + lax.ppermute(
            away, "fsdp", [(i, (i + step) % depth) for i in range(depth)]
        )
    return total


def attention_kernel(
    blocks,
    length,
    starts_ref,
    cos_ref,
    sin_ref,
    q_ref,
    k_ref,
    v_ref,
    do_ref,
    mixed_ref,
    dq_ref,
    dk_ref,
    dv_ref,
    q_s,
    k_s,
    v_s,
    do_s,
    dk_s,
    dv_s,
    bias_s,
):
    micro = pl.program_id(0)
    total = blocks * length
    tile = 256
    lane = lax.broadcasted_iota(jnp.int32, (1, LANES), 1)
    low_lane = (lane % HEAD_DIM) < (ROT // 2)

    def turn(value, cosine, sine):
        other = jnp.where(
            low_lane,
            pltpu.roll(value, LANES - ROT // 2, 1),
            pltpu.roll(value, ROT // 2, 1),
        )
        return value * cosine + other * sine

    for block in range(blocks):
        source = block
        at = slice(block * length, (block + 1) * length)
        cosine, sine = cos_ref[at, :], sin_ref[at, :]
        q_s[at, :] = (turn(q_ref[0, source], cosine, sine)).astype(BF) * jnp.asarray(SCALE, BF)
        k_s[at, :] = turn(k_ref[0, source], cosine, sine).astype(BF)
        v_s[at, :] = v_ref[0, source].astype(BF)
        do_s[at, :] = do_ref[0, source]
    dk_s[...] = jnp.zeros_like(dk_s)
    dv_s[...] = jnp.zeros_like(dv_s)

    def label(positions):
        found = jnp.full(positions.shape, -1, jnp.int32)
        for piece in range(PIECES):
            start = starts_ref[micro, piece]
            found = jnp.where((positions >= start) & (positions < start + IMG), piece, found)
        return found

    for first in range(0, total, tile):
        last = min(total, first + tile + IMG)
        qpos = first + lax.broadcasted_iota(jnp.int32, (tile, 1), 0)
        kpos = first + lax.broadcasted_iota(jnp.int32, (1, last - first), 1)
        qlab, klab = label(qpos), label(kpos)
        allowed = (kpos <= qpos) | ((qlab == klab) & (qlab >= 0))
        bias_s[:, : last - first] = jnp.where(allowed, 0.0, -1e30)
        rows = slice(first, first + tile)
        keys = k_s[:last, :]
        values = v_s[:last, :]
        mixed = jnp.zeros((tile, LANES), F32)
        dq = jnp.zeros((tile, LANES), F32)
        for head in range(LANES // HEAD_DIM):
            mine = (lane // HEAD_DIM) == head
            q = jnp.where(mine, q_s[rows, :], 0)
            do = jnp.where(mine, do_s[rows, :], 0)
            dims = (((1,), (1,)), ((), ()))
            s = lax.dot_general(q, keys, dims, preferred_element_type=F32)
            if first:
                s = jnp.concatenate(
                    [s[:, :first], s[:, first:] + bias_s[:, : last - first]], axis=1
                )
            else:
                s = s + bias_s[:, : last - first]
            p = jnp.exp(s - jnp.max(s, axis=1, keepdims=True))
            p = p * (1.0 / jnp.sum(p, axis=1, keepdims=True))
            probs = p.astype(BF)
            att = jnp.dot(probs, values, preferred_element_type=F32)
            mixed = jnp.where(mine, att, mixed)
            dp = lax.dot_general(do, values, dims, preferred_element_type=F32)
            delta = jnp.sum(p * dp, axis=1, keepdims=True)
            ds = (p * (dp - delta)).astype(BF)
            dq = jnp.where(mine, jnp.dot(ds, keys, preferred_element_type=F32), dq)
            over = (((0,), (0,)), ((), ()))
            dk_s[:last, :] += lax.dot_general(ds, q, over, preferred_element_type=F32)
            dv_s[:last, :] += lax.dot_general(probs, do, over, preferred_element_type=F32)
        dq = dq * SCALE
        for part in range(tile // length):
            block = first // length + part
            here = slice(part * length, (part + 1) * length)
            at = slice(block * length, (block + 1) * length)
            mixed_ref[0, block] = mixed[here].astype(BF)
            dq_ref[0, block] = turn(dq[here], cos_ref[at, :], -sin_ref[at, :]).astype(BF)
    for block in range(blocks):
        at = slice(block * length, (block + 1) * length)
        dk_ref[0, block] = turn(dk_s[at, :], cos_ref[at, :], -sin_ref[at, :]).astype(BF)
        dv_ref[0, block] = dv_s[at, :].astype(BF)


def attention(starts, projected, mixed_grad):
    micro, blocks, length, cols = mixed_grad.shape
    total = blocks * length
    groups = cols // LANES
    half = ROT // 2
    frequency = 10000.0 ** (-2.0 * jnp.arange(half, dtype=F32) / ROT)
    angles = jnp.arange(total, dtype=jnp.int32).astype(F32)[:, None] * frequency[None, :]
    cosine, sine = jnp.cos(angles), jnp.sin(angles)
    ones = jnp.ones((total, HEAD_DIM - ROT), F32)
    cosine = jnp.concatenate([cosine, cosine, ones] * 2, axis=1)
    sine = jnp.concatenate([-sine, sine, 0 * ones] * 2, axis=1)

    def spec(offset):
        return pl.BlockSpec(
            (1, blocks, length, LANES), lambda m, g, offset=offset: (m, 0, 0, offset * groups + g)
        )

    table = pl.BlockSpec((total, LANES), lambda m, g: (0, 0))
    shape = jax.ShapeDtypeStruct(mixed_grad.shape, BF)
    return pl.pallas_call(
        functools.partial(attention_kernel, blocks, length),
        grid=(micro, groups),
        in_specs=[
            pl.BlockSpec(memory_space=pltpu.SMEM),
            table,
            table,
            spec(0),
            spec(1),
            spec(2),
            spec(0),
        ],
        out_specs=[spec(0)] * 4,
        out_shape=[shape] * 4,
        scratch_shapes=[pltpu.VMEM((total, LANES), BF)] * 4
        + [pltpu.VMEM((total, LANES), F32)] * 2
        + [pltpu.VMEM((256, 512), F32)],
        compiler_params=pltpu.CompilerParams(vmem_limit_bytes=48 * 1024 * 1024),
        cost_estimate=pl.CostEstimate(
            flops=micro * groups * 40 * total * total * HEAD_DIM,
            bytes_accessed=micro * groups * total * LANES * 22,
            transcendentals=micro * groups * 2 * total * total,
        ),
    )(starts, cosine, sine, projected, projected, projected, mixed_grad)


MESH = pl.DeviceIdType.MESH


def load_kernel(
    dims,
    tokens_ref,
    up_ref,
    one_ref,
    two_ref,
    qkv_ref,
    out_ref,
    vec_ref,
    normed_ref,
    all_up_ref,
    my_one_ref,
    two_right_ref,
    two_left_ref,
    attn_ref,
    full_ref,
    gathered,
    vec_seq,
    vec_sum,
    vec_all,
    local_sem,
    vec_send,
    vec_recv,
    a2a_send,
    a2a_recv,
    line_send,
    line_recv,
    row_send,
    row_recv,
):
    size, depth, micro, length, width, units, cols = dims
    me, at = lax.axis_index("seq"), lax.axis_index("fsdp")
    count = size.bit_length() - 1
    half = width // 2

    def seq(step):
        return {"seq": me ^ step}

    def line(step):
        return {"fsdp": lax.rem(at + step, depth)}

    barrier = pltpu.get_barrier_semaphore()
    for step in range(1, size):
        pl.semaphore_signal(barrier, inc=1, device_id=seq(step), device_id_type=MESH)
    for step in range(1, depth):
        pl.semaphore_signal(barrier, inc=1, device_id=line(step), device_id_type=MESH)
    pl.semaphore_wait(barrier, size + depth - 2)

    def remote(src, dst, send, recv, device):
        return pltpu.make_async_remote_copy(
            src_ref=src,
            dst_ref=dst,
            send_sem=send,
            recv_sem=recv,
            device_id=device,
            device_id_type=MESH,
        )

    def vec_seq_copy(step):
        return remote(
            vec_ref, vec_seq.at[step], vec_send.at[step], vec_recv.at[step], seq(step)
        )

    def vec_line_copy(step):
        number = size + step
        return remote(
            vec_sum, vec_all.at[step], vec_send.at[number], vec_recv.at[number], line(step)
        )

    def one_copy(step):
        peer = me ^ step
        return remote(
            one_ref.at[:, pl.ds(pl.multiple_of(peer * units, 128), units)],
            my_one_ref.at[me, at],
            a2a_send.at[step],
            a2a_recv.at[step],
            seq(step),
        )

    def qkv_copy(step, part):
        peer = me ^ step
        number = size * (1 + part) + step
        return remote(
            qkv_ref.at[:, pl.ds(pl.multiple_of(part * width + peer * cols, 128), cols)],
            attn_ref.at[me, :, pl.ds(part * cols, cols)],
            a2a_send.at[number],
            a2a_recv.at[number],
            seq(step),
        )

    local = [
        pltpu.make_async_copy(
            one_ref.at[:, pl.ds(pl.multiple_of(me * units, 128), units)],
            my_one_ref.at[me, at],
            local_sem.at[0],
        ),
        pltpu.make_async_copy(
            tokens_ref,
            gathered.at[:, me],
            local_sem.at[1],
        ),
        pltpu.make_async_copy(
            up_ref,
            all_up_ref.at[:, me],
            local_sem.at[2],
        ),
    ]
    for part in range(3):
        local.append(
            pltpu.make_async_copy(
                qkv_ref.at[:, pl.ds(pl.multiple_of(part * width + me * cols, 128), cols)],
                attn_ref.at[me, :, pl.ds(part * cols, cols)],
                local_sem.at[3 + part],
            )
        )
    for peer in range(size):
        local.append(
            pltpu.make_async_copy(
                out_ref.at[:, pl.ds(peer * cols, cols)],
                attn_ref.at[peer, :, pl.ds(3 * cols, cols)],
                local_sem.at[6 + peer],
            )
        )

    def one_line(step, way):
        origin = jnp.clip(at - way * (step - 1), 0, depth - 1)
        number = 2 * step + (way > 0)
        piece = my_one_ref.at[:, origin]
        ok = (at + way >= 0) & (at + way < depth)
        ok = ok & (at - way * (step - 1) >= 0) & (at - way * (step - 1) < depth)
        return ok, remote(
            piece,
            piece,
            line_send.at[number],
            line_recv.at[number],
            {"fsdp": jnp.clip(at + way, 0, depth - 1)},
        )

    def one_arrives(step, way):
        ok = (at - way * step >= 0) & (at - way * step < depth)
        return ok, one_line(step, way)[1]

    def two_line(way):
        ok = (at + way >= 0) & (at + way < depth)
        number = way > 0
        return ok, remote(
            two_ref,
            two_right_ref if way > 0 else two_left_ref,
            line_send.at[int(number)],
            line_recv.at[int(number)],
            {"fsdp": jnp.clip(at + way, 0, depth - 1)},
        )

    def two_arrives(way):
        return (at - way >= 0) & (at - way < depth), two_line(way)[1]

    def start(pair):
        ok, copy = pair

        @pl.when(ok)
        def _():
            copy.start()

    def wait_recv(pair):
        ok, copy = pair

        @pl.when(ok)
        def _():
            copy.wait_recv()

    def wait_send(pair):
        ok, copy = pair

        @pl.when(ok)
        def _():
            copy.wait_send()

    sources = (tokens_ref, up_ref)
    targets = (gathered, all_up_ref)
    orders = (list(range(1, count)), list(range(1, count))[::-1])

    def row_copy(which, part, mask, bit):
        columns = slice(part * half, (part + 1) * half)
        block = me ^ mask
        if mask == 0:
            src = sources[which].at[:, :, columns]
        else:
            src = targets[which].at[:, block, :, columns]
        number = (which * 2 + part) * size + (mask | (1 << bit))
        return remote(
            src,
            targets[which].at[:, block, :, columns],
            row_send.at[number],
            row_recv.at[number],
            seq(1 << bit),
        )

    def row_stage(which, part, stage):
        order = orders[part]
        masks = [0]
        for bit in order[:stage]:
            masks = masks + [mask | (1 << bit) for mask in masks]
        return [row_copy(which, part, mask, order[stage]) for mask in masks]

    def row_cores(which, part, stage):
        order = orders[part]
        masks = [0]
        new = [0]
        for bit in order[: stage + 1]:
            new = [mask | (1 << bit) for mask in masks]
            masks = masks + new
        return [row_copy(which, part, mask, 0) for mask in new]

    def both_parts(function, which, stage):
        return function(which, 0, stage) + function(which, 1, stage)

    def issue(copies):
        for copy in copies:
            copy.start()

    def arrive(copies):
        for copy in copies:
            copy.wait_recv()

    issue(vec_seq_copy(step) for step in range(1, size))
    issue(one_copy(step) for step in range(1, size))
    for way in (1, -1):
        start(two_line(way))
    issue(local)
    vec_seq[0] = vec_ref[...]
    arrive(vec_seq_copy(step) for step in range(1, size))
    summed = vec_seq[0].astype(F32)
    for step in range(1, size):
        summed = summed + vec_seq[step].astype(F32)
    vec_sum[...] = summed.astype(BF)
    issue(vec_line_copy(step) for step in range(1, depth))
    for which in range(2):
        issue(both_parts(row_cores, which, -1))
    arrive(one_copy(step) for step in range(1, size))
    local[0].wait()
    for way in (1, -1):
        start(one_line(1, way))
    for which in range(2):
        issue(both_parts(row_stage, which, 0))
    arrive(vec_line_copy(step) for step in range(1, depth))
    for step in range(1, depth):
        summed = summed + vec_all[step].astype(F32)
    full_ref[...] = summed

    line_step = 1
    for stage in range(count - 1):
        for which in range(2):
            arrive(both_parts(row_stage, which, stage))
            issue(both_parts(row_cores, which, stage))
            if stage + 1 < count - 1:
                issue(both_parts(row_stage, which, stage + 1))
        if line_step < depth - 1:
            for way in (1, -1):
                wait_recv(one_arrives(line_step, way))
                start(one_line(line_step + 1, way))
            line_step += 1
    for part in range(3):
        issue(qkv_copy(step, part) for step in range(1, size))
    while line_step < depth - 1:
        for way in (1, -1):
            wait_recv(one_arrives(line_step, way))
            start(one_line(line_step + 1, way))
        line_step += 1

    local[1].wait()
    for stage in range(-1, count - 1):
        arrive(both_parts(row_cores, 0, stage))
    gain = full_ref[0:1, :]
    shift = full_ref[1:2, :]

    @pl.loop(0, micro * size)
    def _(index):
        m, block = index // size, lax.rem(index, size)
        x = gathered[m, block].astype(F32)
        center = x - jnp.mean(x, axis=-1, keepdims=True)
        spread = jnp.mean(center * center, axis=-1, keepdims=True)
        y = center * lax.rsqrt(spread + EPSILON) * gain + shift
        normed_ref[m, block] = y.astype(BF)

    for copy in local[2:]:
        copy.wait()
    for stage in range(-1, count - 1):
        arrive(both_parts(row_cores, 1, stage))
    for part in range(3):
        arrive(qkv_copy(step, part) for step in range(1, size))
    for way in (1, -1):
        wait_recv(two_arrives(way))
        wait_recv(one_arrives(depth - 1, way))

    for step in range(1, size):
        vec_seq_copy(step).wait_send()
        one_copy(step).wait_send()
        for part in range(3):
            qkv_copy(step, part).wait_send()
    for step in range(1, depth):
        vec_line_copy(step).wait_send()
        for way in (1, -1):
            wait_send(one_line(step, way))
    for way in (1, -1):
        wait_send(two_line(way))
    for which in range(2):
        for stage in range(-1, count - 1):
            for copy in both_parts(row_cores, which, stage):
                copy.wait_send()
            if stage >= 0:
                for copy in both_parts(row_stage, which, stage):
                    copy.wait_send()


def load_all(tokens, upstream, w_fc1, w_fc2, w_qkv, w_out, vectors):
    size, depth = lax.axis_size("seq"), lax.axis_size("fsdp")
    micro, length, width = tokens.shape
    rows, units, cols = w_fc1.shape[0], w_fc1.shape[1] // size, width // size
    dims = (size, depth, micro, length, width, units, cols)
    hbm = pl.BlockSpec(memory_space=pl.ANY)
    vmem = pl.BlockSpec(memory_space=pltpu.VMEM)
    gathered = (micro, size, length, width)
    dma = pltpu.SemaphoreType.DMA
    return pl.pallas_call(
        functools.partial(load_kernel, dims),
        in_specs=[hbm] * 6 + [vmem],
        out_specs=[vmem] + [hbm] * 5 + [vmem],
        out_shape=[
            jax.ShapeDtypeStruct(gathered, BF),
            jax.ShapeDtypeStruct(gathered, BF),
            jax.ShapeDtypeStruct((size, depth, rows, units), BF),
            jax.ShapeDtypeStruct(w_fc2.shape, BF),
            jax.ShapeDtypeStruct(w_fc2.shape, BF),
            jax.ShapeDtypeStruct((size, rows, 4 * cols), BF),
            jax.ShapeDtypeStruct(vectors.shape, F32),
        ],
        scratch_shapes=[
            pltpu.VMEM(gathered, BF),
            pltpu.VMEM((size,) + vectors.shape, BF),
            pltpu.VMEM(vectors.shape, BF),
            pltpu.VMEM((depth,) + vectors.shape, BF),
            dma((6 + size,)),
            dma((size + depth,)),
            dma((size + depth,)),
            dma((4 * size,)),
            dma((4 * size,)),
            dma((2 * depth + 2,)),
            dma((2 * depth + 2,)),
            dma((4 * size,)),
            dma((4 * size,)),
        ],
        compiler_params=pltpu.CompilerParams(
            collective_id=1, has_side_effects=True, vmem_limit_bytes=40 * 1024 * 1024
        ),
        cost_estimate=pl.CostEstimate(
            flops=1000, bytes_accessed=300 * 1000 * 1000, transcendentals=0
        ),
    )(tokens, upstream, w_fc1, w_fc2, w_qkv, w_out, vectors)


def gelu_tanh(values):
    return jax.nn.gelu(values, approximate=True)


def layer_norm(values, gain, shift):
    center = values - jnp.mean(values, axis=-1, keepdims=True)
    spread = jnp.mean(center * center, axis=-1, keepdims=True)
    return center * lax.rsqrt(spread + EPSILON) * gain + shift


def fence(*values):
    return lax.optimization_barrier(values)


def line_right(value, senders):
    return lax.ppermute(value, "fsdp", [(i, i + 1) for i in senders])


def line_left(value, senders):
    last = lax.axis_size("fsdp") - 1
    return lax.ppermute(value, "fsdp", [(last - i, last - i - 1) for i in senders])


class Gather:
    def __init__(self, mine):
        self.right, self.left = [mine], [mine]

    def step(self):
        size = lax.axis_size("fsdp")
        number = len(self.right)
        if number < size:
            self.right.append(line_right(self.right[-1], range(number - 1, size - 1)))
            self.left.append(line_left(self.left[-1], range(number - 1, size - 1)))

    def fence(self, *others):
        (self.right[-1], self.left[-1]), *others = fence((self.right[-1], self.left[-1]), *others)
        return others

    def rest(self):
        while len(self.right) < lax.axis_size("fsdp"):
            self.step()

    def pieces(self):
        size = lax.axis_size("fsdp")
        at = lax.axis_index("fsdp")
        found = [(self.right[0], at)]
        for step in range(1, size):
            piece = jnp.where(at >= step, self.right[step], self.left[size - step])
            found.append((piece, lax.rem(at - step + size, size)))
        return found


class Scatter:
    def __init__(self, chunk):
        self.chunk = chunk
        self.number = 0
        self.right = self.left = None

    def step(self):
        size = lax.axis_size("fsdp")
        at = lax.axis_index("fsdp")
        if self.number == size - 1:
            return
        self.number += 1
        going = self.chunk(jnp.minimum(size - self.number + at, size - 1))
        coming = self.chunk(jnp.maximum(self.number - size + at, 0))
        if self.number > 1:
            going = (going.astype(F32) + self.right.astype(F32)).astype(BF)
            coming = (coming.astype(F32) + self.left.astype(F32)).astype(BF)
        self.right = line_right(going, range(self.number))
        self.left = line_left(coming, range(self.number))

    def rest(self):
        while self.number < lax.axis_size("fsdp") - 1:
            self.step()

    def fence(self, *others):
        (self.right, self.left), *others = fence((self.right, self.left), *others)
        return others

    def total(self):
        mine = self.chunk(lax.axis_index("fsdp")).astype(F32)
        return mine + self.right.astype(F32) + self.left.astype(F32)


def per_device(
    tokens,
    ln_gain,
    ln_bias,
    w_qkv,
    b_qkv,
    w_out,
    b_out,
    w_fc1,
    b_fc1,
    w_fc2,
    b_fc2,
    piece_starts,
    cotangent,
):
    size, depth = lax.axis_size("seq"), lax.axis_size("fsdp")
    me = lax.axis_index("seq")
    micro, _, length, width = tokens.shape
    rows = width // (size * depth)
    hidden_rows = w_fc2.shape[0]
    cols = width // size
    units = hidden_rows * depth
    count = micro * size * length
    tokens = tokens[:, 0]
    upstream = cotangent[:, 0]

    def contract_last(left, right):
        return lax.dot_general(left, right, (((1,), (1,)), ((), ())), preferred_element_type=F32)

    def contract_first(left, right):
        return lax.dot_general(left, right, (((0,), (0,)), ((), ())), preferred_element_type=F32)

    def place_columns(pieces):
        out = jnp.zeros((size, depth) + pieces[0][0].shape[1:], BF)
        for piece, origin in pieces:
            out = lax.dynamic_update_slice_in_dim(out, piece[:, None], origin, 1)
        return out

    def place_rows(pieces):
        out = jnp.zeros((depth,) + pieces[0][0].shape, BF)
        for piece, origin in pieces:
            out = lax.dynamic_update_slice_in_dim(out, piece[None], origin, 0)
        return out

    index = me * depth + lax.axis_index("fsdp")
    packed = []
    for vector in (ln_gain, ln_bias, b_qkv, b_out, b_fc1, b_fc2):
        extent = vector.shape[0]
        flat = jnp.zeros((extent * size * depth,), BF)
        flat = lax.dynamic_update_slice(flat, vector, (index * extent,))
        packed.append(flat.reshape(-1, width))
    packed = jnp.concatenate(packed, axis=0)
    packed = jnp.pad(packed, ((0, -packed.shape[0] % 16), (0, 0)))
    normed, up, my_one, two_right, two_left, attn_cols, full = load_all(
        tokens, upstream, w_fc1, w_fc2, w_qkv, w_out, packed
    )
    normed = normed.reshape(count, width)
    up = up.reshape(count, width)
    my_one = my_one.reshape(width, units)
    two = Gather(w_fc2)
    two.right.append(two_right)
    two.left.append(two_left)
    gain, shift, bias_out = full[0], full[1], full[5]
    bias_qkv = lax.dynamic_slice_in_dim(full[2:5], me * cols, cols, 1).reshape(-1)
    ratio = size * units // width
    bias_one = lax.dynamic_slice_in_dim(full[6 : 6 + ratio].reshape(-1), me * units, units, 0)
    bias_two = full[6 + ratio]
    two.step()
    pre = jnp.dot(normed, my_one, preferred_element_type=F32) + bias_one
    hidden, back = jax.vjp(gelu_tanh, pre)
    hidden = hidden.astype(BF)
    grad_two = contract_first(hidden, up).astype(BF).reshape(depth, hidden_rows, width)
    hidden, grad_two = two.fence(hidden, grad_two)
    two.step()
    sum_two = Scatter(lambda o: lax.dynamic_index_in_dim(grad_two, o, 0, keepdims=False))
    sum_two.step()
    (two.right, two.left), (sum_two.right, sum_two.left), attn_cols = fence(
        (two.right, two.left), (sum_two.right, sum_two.left), attn_cols
    )
    attn = Gather(attn_cols)
    attn.step()
    two.rest()
    my_two = place_rows(two.pieces()).reshape(units, width)
    pre_grad = back(contract_last(up, my_two))[0].astype(BF)
    grad_one = contract_first(normed, pre_grad).astype(BF).reshape(size, depth, rows, units)
    pre_grad, grad_one = attn.fence(pre_grad, grad_one)
    attn.step()
    sum_one = Scatter(lambda o: lax.dynamic_index_in_dim(grad_one, o, 1, keepdims=False))
    sum_one.step()
    (sum_one.right, sum_one.left), (sum_two.right, sum_two.left) = attn.fence(
        (sum_one.right, sum_one.left), (sum_two.right, sum_two.left)
    )
    attn.step()
    sum_two.step()
    (sum_two.right, sum_two.left), normed, up = attn.fence(
        (sum_two.right, sum_two.left), normed, up
    )
    sum_two.step()
    attn.rest()
    pieces = attn.pieces()
    my_qkv = place_columns([(p[..., : 3 * cols], o) for p, o in pieces]).reshape(width, 3 * cols)
    my_out = place_rows([(p[..., 3 * cols :].transpose(1, 0, 2), o) for p, o in pieces])
    my_out = my_out.reshape(cols, width)
    projected = jnp.dot(normed, my_qkv, preferred_element_type=F32) + bias_qkv
    projected = projected.reshape(micro, size, length, 3 * cols)
    mixed_grad = contract_last(up, my_out).astype(BF).reshape(micro, size, length, cols)
    starts = piece_starts[:, 0]
    parts = [attention(starts[:1], projected[:1], mixed_grad[:1])]
    (sum_one.right, sum_one.left), (projected, mixed_grad), parts = sum_two.fence(
        (sum_one.right, sum_one.left), (projected, mixed_grad), parts
    )
    sum_one.step()
    for m in range(1, micro):
        parts.append(attention(starts[m:][:1], projected[m:][:1], mixed_grad[m:][:1]))
    mixed = jnp.concatenate([part[0] for part in parts]).reshape(count, cols)
    projected_grad = jnp.concatenate(
        [jnp.concatenate(part[1:], axis=-1) for part in parts]
    ).reshape(count, 3 * cols)
    projected_grad, mixed = sum_one.fence(projected_grad, mixed)
    sum_one.step()
    grad_qkv = contract_first(normed, projected_grad).astype(BF).reshape(size, depth, rows, 3 * cols)
    grad_out = contract_first(mixed, up).astype(BF).reshape(depth, rows, size, cols)
    grad_qkv, grad_out, (sum_two.right, sum_two.left) = sum_one.fence(
        grad_qkv, grad_out, (sum_two.right, sum_two.left)
    )

    def attn_chunk(o):
        return jnp.concatenate(
            [
                lax.dynamic_index_in_dim(grad_qkv, o, 1, keepdims=False),
                lax.dynamic_index_in_dim(grad_out, o, 0, keepdims=False).transpose(1, 0, 2),
            ],
            axis=-1,
        )

    sum_attn = Scatter(attn_chunk)
    sum_attn.step()
    sum_one.rest()
    sum_two.rest()

    def to_rows(mine, parts):
        mine = lax.all_to_all(mine.astype(BF), "seq", 0, 0, tiled=True).astype(F32)
        return mine.reshape(size, rows, parts, -1).transpose(1, 2, 0, 3).reshape(rows, -1)

    out_two = sum_two.total()
    out_one = to_rows(sum_one.total(), 1)
    grad_terms = contract_last(projected_grad, my_qkv) + contract_last(pre_grad, my_one)
    grad_terms = grad_terms.astype(BF).reshape(micro, size, length, width)
    (grad_terms,) = sum_attn.fence(grad_terms)
    sum_attn.step()
    normed_grad = scatter_seq(grad_terms)
    terms = jnp.dot(mixed, my_out, preferred_element_type=F32)
    terms = terms + jnp.dot(hidden, my_two, preferred_element_type=F32)
    terms = terms.astype(BF).reshape(micro, size, length, width)
    sums = scatter_seq(terms)
    sum_attn.rest()
    attn_total = sum_attn.total()
    out_qkv = to_rows(attn_total[..., : 3 * cols], 3)
    out_out = attn_total[..., 3 * cols :].transpose(1, 0, 2).reshape(rows, width)
    activations = (tokens.astype(F32) + sums + (bias_out + bias_two)).astype(BF)
    _, norm_back = jax.vjp(layer_norm, tokens.astype(F32), gain, shift)
    input_grad, gain_grad, shift_grad = norm_back(normed_grad)
    input_grad = input_grad + upstream.astype(F32)

    def put(values, extent, at):
        return lax.dynamic_update_slice_in_dim(jnp.zeros(extent, F32), values, at, -1)

    bqkv = jnp.sum(projected_grad.astype(F32), axis=0).reshape(3, cols)
    bqkv = put(bqkv, (3, width), me * cols)
    bone = put(jnp.sum(pre_grad.astype(F32), axis=0), (size * units,), me * units)
    btwo = jnp.sum(upstream.astype(F32), axis=(0, 1))
    packed = [gain_grad, shift_grad, bqkv[:2], bqkv[2], bone, btwo]
    packed = [v.reshape(size, depth, -1) for v in packed]
    summed = scatter_small(jnp.concatenate(packed, axis=-1))
    vectors = []
    start = 0
    for v in packed:
        vectors.append(summed[start : start + v.shape[-1]])
        start += v.shape[-1]
    return (
        activations[:, None],
        input_grad[:, None],
        vectors[0],
        vectors[1],
        out_qkv,
        vectors[2],
        vectors[3],
        out_out,
        vectors[5],
        out_one,
        vectors[4],
        out_two,
        vectors[5],
    )


def solution(mesh):
    both = ("seq", "fsdp")
    row = P(both)
    matrix = P(both, None)
    tokens = P(None, "fsdp", "seq", None)
    weights = (row, row, matrix, row, matrix, row, matrix, row, matrix, row)
    grads = (row, row, matrix, row, row, matrix, row, matrix, row, matrix, row)
    return jax.shard_map(
        per_device,
        mesh=mesh,
        in_specs=(tokens,) + weights + (P(None, "fsdp", None), tokens),
        out_specs=(tokens, tokens) + grads,
        check_vma=False,
    )
```

```python
import functools
import math

import jax
import jax.numpy as jnp
import numpy as np
from jax import lax
from jax.experimental import pallas as pl
from jax.experimental.pallas import tpu as pltpu
from jax.sharding import PartitionSpec as P

HEADS = 32
HEAD_DIM = 64
ROT = 32
IMG = 256
PIECES = 2
EPSILON = 1e-05
BF = jnp.bfloat16
F32 = jnp.float32
SCALE = 1.0 / math.sqrt(HEAD_DIM)
LANES = 2 * HEAD_DIM


def swap(value, bit):
    size = lax.axis_size("seq")
    return lax.ppermute(value, "seq", [(i, i ^ bit) for i in range(size)])


def store_index(block):
    half = lax.axis_size("seq") // 2
    if isinstance(block, int):
        return block % 2 * half + block // 2
    return (block & 1) * half + (block >> 1)


def scatter_seq(terms):
    size = lax.axis_size("seq")
    me = lax.axis_index("seq")
    count = size.bit_length() - 1
    micro, _, length, width = terms.shape
    half = width // 2
    bits = list(range(1, count))

    def exchange(held, bit, axis):
        held = held.astype(BF)
        mine = (me >> bit) & 1
        away = lax.dynamic_index_in_dim(held, 1 - mine, axis, keepdims=False)
        kept = lax.dynamic_index_in_dim(held, mine, axis, keepdims=False)
        return kept.astype(F32) + swap(away, 1 << bit).astype(F32)

    sums = []
    for cols, order in ((slice(0, half), bits), (slice(half, width), bits[::-1])):
        held = terms[..., cols].reshape((micro,) + (2,) * count + (length, half))
        left = [0] + bits[::-1]
        for bit in [0] + order:
            held = exchange(held, bit, 1 + left.index(bit))
            left.remove(bit)
        sums.append(held)
    return jnp.concatenate(sums, axis=-1)


def attention_kernel(
    blocks,
    length,
    starts_ref,
    cos_ref,
    sin_ref,
    q_ref,
    k_ref,
    v_ref,
    do_ref,
    mixed_ref,
    dq_ref,
    dk_ref,
    dv_ref,
    q_s,
    k_s,
    v_s,
    do_s,
    dk_s,
    dv_s,
    bias_s,
):
    micro = pl.program_id(0)
    total = blocks * length
    tile = 256
    lane = lax.broadcasted_iota(jnp.int32, (1, LANES), 1)
    low_lane = (lane % HEAD_DIM) < (ROT // 2)

    def turn(value, cosine, sine):
        other = jnp.where(
            low_lane,
            pltpu.roll(value, LANES - ROT // 2, 1),
            pltpu.roll(value, ROT // 2, 1),
        )
        return value * cosine + other * sine

    for block in range(blocks):
        source = store_index(block)
        at = slice(block * length, (block + 1) * length)
        cosine, sine = cos_ref[at, :], sin_ref[at, :]
        q_s[at, :] = (turn(q_ref[0, source], cosine, sine)).astype(BF) * jnp.asarray(SCALE, BF)
        k_s[at, :] = turn(k_ref[0, source], cosine, sine).astype(BF)
        v_s[at, :] = v_ref[0, source].astype(BF)
        do_s[at, :] = do_ref[0, source]
    dk_s[...] = jnp.zeros_like(dk_s)
    dv_s[...] = jnp.zeros_like(dv_s)

    def label(positions):
        found = jnp.full(positions.shape, -1, jnp.int32)
        for piece in range(PIECES):
            start = starts_ref[micro, piece]
            found = jnp.where((positions >= start) & (positions < start + IMG), piece, found)
        return found

    for first in range(0, total, tile):
        last = min(total, first + tile + IMG)
        qpos = first + lax.broadcasted_iota(jnp.int32, (tile, 1), 0)
        kpos = first + lax.broadcasted_iota(jnp.int32, (1, last - first), 1)
        qlab, klab = label(qpos), label(kpos)
        allowed = (kpos <= qpos) | ((qlab == klab) & (qlab >= 0))
        bias_s[:, : last - first] = jnp.where(allowed, 0.0, -1e30)
        rows = slice(first, first + tile)
        keys = k_s[:last, :]
        values = v_s[:last, :]
        mixed = jnp.zeros((tile, LANES), F32)
        dq = jnp.zeros((tile, LANES), F32)
        for head in range(LANES // HEAD_DIM):
            mine = (lane // HEAD_DIM) == head
            q = jnp.where(mine, q_s[rows, :], 0)
            do = jnp.where(mine, do_s[rows, :], 0)
            dims = (((1,), (1,)), ((), ()))
            s = lax.dot_general(q, keys, dims, preferred_element_type=F32)
            if first:
                s = jnp.concatenate(
                    [s[:, :first], s[:, first:] + bias_s[:, : last - first]], axis=1
                )
            else:
                s = s + bias_s[:, : last - first]
            p = jnp.exp(s - jnp.max(s, axis=1, keepdims=True))
            p = p * (1.0 / jnp.sum(p, axis=1, keepdims=True))
            probs = p.astype(BF)
            att = jnp.dot(probs, values, preferred_element_type=F32)
            mixed = jnp.where(mine, att, mixed)
            dp = lax.dot_general(do, values, dims, preferred_element_type=F32)
            delta = jnp.sum(p * dp, axis=1, keepdims=True)
            ds = (p * (dp - delta)).astype(BF)
            dq = jnp.where(mine, jnp.dot(ds, keys, preferred_element_type=F32), dq)
            over = (((0,), (0,)), ((), ()))
            dk_s[:last, :] += lax.dot_general(ds, q, over, preferred_element_type=F32)
            dv_s[:last, :] += lax.dot_general(probs, do, over, preferred_element_type=F32)
        dq = dq * SCALE
        for part in range(tile // length):
            block = first // length + part
            here = slice(part * length, (part + 1) * length)
            at = slice(block * length, (block + 1) * length)
            mixed_ref[0, store_index(block)] = mixed[here].astype(BF)
            dq_ref[0, store_index(block)] = turn(dq[here], cos_ref[at, :], -sin_ref[at, :]).astype(BF)
    for block in range(blocks):
        at = slice(block * length, (block + 1) * length)
        dk_ref[0, store_index(block)] = turn(dk_s[at, :], cos_ref[at, :], -sin_ref[at, :]).astype(BF)
        dv_ref[0, store_index(block)] = dv_s[at, :].astype(BF)


def tables(total):
    half = ROT // 2
    frequency = (10000.0 ** (-2.0 * np.arange(half) / ROT)).astype(np.float32)
    angles = np.arange(total, dtype=np.float32)[:, None] * frequency[None, :]
    cosine, sine = np.cos(angles), np.sin(angles)
    ones = np.ones((total, HEAD_DIM - ROT), np.float32)
    cosine = np.concatenate([cosine, cosine, ones] * 2, axis=1)
    sine = np.concatenate([-sine, sine, 0 * ones] * 2, axis=1)
    return jnp.asarray(cosine), jnp.asarray(sine)


def attention(starts, projected, mixed_grad):
    micro, blocks, length, cols = mixed_grad.shape
    total = blocks * length
    groups = cols // LANES
    cosine, sine = tables(total)

    def spec(offset):
        return pl.BlockSpec(
            (1, blocks, length, LANES), lambda m, g, offset=offset: (m, 0, 0, offset * groups + g)
        )

    table = pl.BlockSpec((total, LANES), lambda m, g: (0, 0))
    shape = jax.ShapeDtypeStruct(mixed_grad.shape, BF)
    return pl.pallas_call(
        functools.partial(attention_kernel, blocks, length),
        grid=(micro, groups),
        in_specs=[
            pl.BlockSpec(memory_space=pltpu.SMEM),
            table,
            table,
            spec(0),
            spec(1),
            spec(2),
            spec(0),
        ],
        out_specs=[spec(0)] * 4,
        out_shape=[shape] * 4,
        scratch_shapes=[pltpu.VMEM((total, LANES), BF)] * 4
        + [pltpu.VMEM((total, LANES), F32)] * 2
        + [pltpu.VMEM((256, 512), F32)],
        compiler_params=pltpu.CompilerParams(vmem_limit_bytes=48 * 1024 * 1024),
        cost_estimate=pl.CostEstimate(
            flops=micro * groups * 40 * total * total * HEAD_DIM,
            bytes_accessed=micro * groups * total * LANES * 22,
            transcendentals=micro * groups * 2 * total * total,
        ),
    )(starts, cosine, sine, projected, projected, projected, mixed_grad)


MESH = pl.DeviceIdType.MESH


def remote(src, dst, send, recv, device):
    return pltpu.make_async_remote_copy(
        src_ref=src,
        dst_ref=dst,
        send_sem=send,
        recv_sem=recv,
        device_id=device,
        device_id_type=MESH,
    )


def greet(size, depth):
    me, at = lax.axis_index("seq"), lax.axis_index("fsdp")
    barrier = pltpu.get_barrier_semaphore()
    for step in range(1, size):
        pl.semaphore_signal(barrier, inc=1, device_id={"seq": me ^ step}, device_id_type=MESH)
    for step in range(1, depth):
        pl.semaphore_signal(
            barrier, inc=1, device_id={"fsdp": lax.rem(at + step, depth)}, device_id_type=MESH
        )
    pl.semaphore_wait(barrier, size + depth - 2)


class LineGather:
    def __init__(self, depth, source, target, send, recv):
        self.depth, self.source, self.target = depth, source, target
        self.send, self.recv = send, recv

    def copy(self, step, way):
        at = lax.axis_index("fsdp")
        origin = jnp.clip(at - way * (step - 1), 0, self.depth - 1)
        number = step * 2 + (way > 0)
        return remote(
            self.source(origin, step),
            self.target(origin),
            self.send.at[number],
            self.recv.at[number],
            {"fsdp": jnp.clip(at + way, 0, self.depth - 1)},
        )

    def sends(self, step, way):
        at = lax.axis_index("fsdp")
        origin = at - way * (step - 1)
        return (at + way >= 0) & (at + way < self.depth) & (origin >= 0) & (origin < self.depth)

    def start(self, step):
        for way in (1, -1):

            @pl.when(self.sends(step, way))
            def _():
                self.copy(step, way).start()

    def arrive(self, step):
        at = lax.axis_index("fsdp")
        for way in (1, -1):
            origin = at - way * step

            @pl.when((origin >= 0) & (origin < self.depth))
            def _():
                self.copy(step, way).wait_recv()

    def sent(self, step):
        for way in (1, -1):

            @pl.when(self.sends(step, way))
            def _():
                self.copy(step, way).wait_send()


class LineSum:
    def __init__(self, depth, chunk, landing, own, held, out, load, send, recv):
        self.depth, self.chunk, self.landing = depth, chunk, landing
        self.own, self.held, self.out = own, held, out
        self.load, self.send, self.recv = load, send, recv

    def place(self, way):
        at = lax.axis_index("fsdp")
        return at if way > 0 else self.depth - 1 - at

    def copy(self, step, way, src):
        number = step * 2 + (way > 0)
        at = lax.axis_index("fsdp")
        return remote(
            src,
            self.landing(step, way),
            self.send.at[number],
            self.recv.at[number],
            {"fsdp": jnp.clip(at + way, 0, self.depth - 1)},
        )

    def start(self, step, here=True):
        for way in (1, -1):
            place = self.place(way)
            away = jnp.clip(self.depth - step + place, 0, self.depth - 1)
            origin = away if way > 0 else self.depth - 1 - away

            @pl.when(place == 0)
            def _():
                self.copy(step, way, self.chunk(origin)).start()

            if step > 1:

                @pl.when((place >= 1) & (place <= step - 1) & (place < self.depth - 1))
                def _():
                    mine = pltpu.make_async_copy(self.chunk(origin), self.own, self.load.at[0])
                    mine.start()
                    if here:
                        self.copy(step - 1, way, self.out(step, way)).wait_recv()
                    came = pltpu.make_async_copy(
                        self.landing(step - 1, way), self.held, self.load.at[1]
                    )
                    came.start()
                    mine.wait()
                    came.wait()
                    target = self.out(step, way)
                    target[...] = (self.own[...].astype(F32) + self.held[...].astype(F32)).astype(
                        BF
                    )
                    self.copy(step, way, target).start()

    def arrive(self, step, consumed):
        for way in (1, -1):
            place = self.place(way)
            ok = (place >= 1) & (place <= step)
            if consumed:
                ok = ok & (place == self.depth - 1)

            @pl.when(ok)
            def _():
                self.copy(step, way, self.out(step, way)).wait_recv()

    def total(self, last, right, left):
        mine = pltpu.make_async_copy(self.chunk(lax.axis_index("fsdp")), self.own, self.load.at[0])
        mine.start()
        for way, target in ((1, right), (-1, left)):
            place = self.place(way)

            @pl.when(place >= 1)
            def _():
                self.copy(last, way, self.out(last, way)).wait_recv()
                came = pltpu.make_async_copy(self.landing(last, way), target, self.load.at[1])
                came.start()
                came.wait()

            @pl.when(place == 0)
            def _():
                target[...] = jnp.zeros_like(target)

        mine.wait()
        return self.own[...].astype(F32) + right[...].astype(F32) + left[...].astype(F32)

    def sent(self, step):
        for way in (1, -1):
            place = self.place(way)

            @pl.when((place == 0) | ((place <= step - 1) & (place < self.depth - 1)))
            def _():
                self.copy(step, way, self.out(step, way)).wait_send()


def load_kernel(
    dims,
    tokens_ref,
    up_ref,
    one_ref,
    two_ref,
    qkv_ref,
    out_ref,
    vec_ref,
    normed_ref,
    all_up_ref,
    my_one_ref,
    my_two_ref,
    attn_ref,
    full_ref,
    gathered,
    vec_seq,
    vec_sum,
    vec_all,
    local_sem,
    vec_send,
    vec_recv,
    a2a_send,
    a2a_recv,
    line_send,
    line_recv,
    row_send,
    row_recv,
):
    size, depth, micro, length, width, units, cols = dims
    me, at = lax.axis_index("seq"), lax.axis_index("fsdp")
    count = size.bit_length() - 1
    half = width // 2

    def seq(step):
        return {"seq": me ^ step}

    def line(step):
        return {"fsdp": lax.rem(at + step, depth)}

    greet(size, depth)

    def vec_seq_copy(step):
        return remote(
            vec_ref, vec_seq.at[step], vec_send.at[step], vec_recv.at[step], seq(step)
        )

    def vec_line_copy(step):
        number = size + step
        return remote(
            vec_sum, vec_all.at[step], vec_send.at[number], vec_recv.at[number], line(step)
        )

    def one_copy(step):
        peer = me ^ step
        return remote(
            one_ref.at[:, pl.ds(pl.multiple_of(peer * units, 128), units)],
            my_one_ref.at[me, at],
            a2a_send.at[step],
            a2a_recv.at[step],
            seq(step),
        )

    def qkv_copy(step, part):
        peer = me ^ step
        number = size * (1 + part) + step
        return remote(
            qkv_ref.at[:, pl.ds(pl.multiple_of(part * width + peer * cols, 128), cols)],
            attn_ref.at[me, :, pl.ds(part * cols, cols)],
            a2a_send.at[number],
            a2a_recv.at[number],
            seq(step),
        )

    local = [
        pltpu.make_async_copy(
            one_ref.at[:, pl.ds(pl.multiple_of(me * units, 128), units)],
            my_one_ref.at[me, at],
            local_sem.at[0],
        ),
        pltpu.make_async_copy(
            tokens_ref,
            gathered.at[:, store_index(me)],
            local_sem.at[1],
        ),
        pltpu.make_async_copy(
            up_ref,
            all_up_ref.at[:, store_index(me)],
            local_sem.at[2],
        ),
    ]
    for part in range(3):
        local.append(
            pltpu.make_async_copy(
                qkv_ref.at[:, pl.ds(pl.multiple_of(part * width + me * cols, 128), cols)],
                attn_ref.at[me, :, pl.ds(part * cols, cols)],
                local_sem.at[3 + part],
            )
        )
    local.append(pltpu.make_async_copy(two_ref, my_two_ref.at[at], local_sem.at[6]))
    for peer in range(size):
        local.append(
            pltpu.make_async_copy(
                out_ref.at[:, pl.ds(peer * cols, cols)],
                attn_ref.at[peer, :, pl.ds(3 * cols, cols)],
                local_sem.at[7 + peer],
            )
        )

    def one_line(step, way):
        origin = jnp.clip(at - way * (step - 1), 0, depth - 1)
        number = 2 * step + (way > 0)
        piece = my_one_ref.at[:, origin]
        ok = (at + way >= 0) & (at + way < depth)
        ok = ok & (at - way * (step - 1) >= 0) & (at - way * (step - 1) < depth)
        return ok, remote(
            piece,
            piece,
            line_send.at[number],
            line_recv.at[number],
            {"fsdp": jnp.clip(at + way, 0, depth - 1)},
        )

    def one_arrives(step, way):
        ok = (at - way * step >= 0) & (at - way * step < depth)
        return ok, one_line(step, way)[1]

    def two_line(way):
        ok = (at + way >= 0) & (at + way < depth)
        number = way > 0
        return ok, remote(
            two_ref,
            my_two_ref.at[at],
            line_send.at[int(number)],
            line_recv.at[int(number)],
            {"fsdp": jnp.clip(at + way, 0, depth - 1)},
        )

    def two_arrives(way):
        return (at - way >= 0) & (at - way < depth), two_line(way)[1]

    def start(pair):
        ok, copy = pair

        @pl.when(ok)
        def _():
            copy.start()

    def wait_recv(pair):
        ok, copy = pair

        @pl.when(ok)
        def _():
            copy.wait_recv()

    def wait_send(pair):
        ok, copy = pair

        @pl.when(ok)
        def _():
            copy.wait_send()

    sources = (tokens_ref, up_ref)
    targets = (gathered, all_up_ref)
    orders = (list(range(1, count)), list(range(1, count))[::-1])

    def row_copy(which, part, mask, bit):
        columns = slice(part * half, (part + 1) * half)
        block = store_index(me ^ mask)
        if mask == 0:
            src = sources[which].at[:, :, columns]
        else:
            src = targets[which].at[:, block, :, columns]
        number = (which * 2 + part) * size + (mask | (1 << bit))
        return remote(
            src,
            targets[which].at[:, block, :, columns],
            row_send.at[number],
            row_recv.at[number],
            seq(1 << bit),
        )

    def row_stage(which, part, stage):
        order = orders[part]
        masks = [0]
        for bit in order[:stage]:
            masks = masks + [mask | (1 << bit) for mask in masks]
        return [row_copy(which, part, mask, order[stage]) for mask in masks]

    def row_cores(which, part, stage):
        order = orders[part]
        masks = [0]
        new = [0]
        for bit in order[: stage + 1]:
            new = [mask | (1 << bit) for mask in masks]
            masks = masks + new
        return [row_copy(which, part, mask, 0) for mask in new]

    def both_parts(function, which, stage):
        return function(which, 0, stage) + function(which, 1, stage)

    def issue(copies):
        for copy in copies:
            copy.start()

    def arrive(copies):
        for copy in copies:
            copy.wait_recv()

    issue(vec_seq_copy(step) for step in range(1, size))
    issue(one_copy(step) for step in range(1, size))
    for way in (1, -1):
        start(two_line(way))
    issue(local)
    vec_seq[0] = vec_ref[...]
    arrive(vec_seq_copy(step) for step in range(1, size))
    summed = vec_seq[0].astype(F32)
    for step in range(1, size):
        summed = summed + vec_seq[step].astype(F32)
    vec_sum[...] = summed.astype(BF)
    issue(vec_line_copy(step) for step in range(1, depth))
    for which in range(2):
        issue(both_parts(row_cores, which, -1))
    arrive(one_copy(step) for step in range(1, size))
    local[0].wait()
    for way in (1, -1):
        start(one_line(1, way))
    for which in range(2):
        issue(both_parts(row_stage, which, 0))
    arrive(vec_line_copy(step) for step in range(1, depth))
    for step in range(1, depth):
        summed = summed + vec_all[step].astype(F32)
    full_ref[...] = summed

    line_step = 1
    for stage in range(count - 1):
        for which in range(2):
            arrive(both_parts(row_stage, which, stage))
            issue(both_parts(row_cores, which, stage))
            if stage + 1 < count - 1:
                issue(both_parts(row_stage, which, stage + 1))
        if line_step < depth - 1:
            for way in (1, -1):
                wait_recv(one_arrives(line_step, way))
                start(one_line(line_step + 1, way))
            line_step += 1
    for part in range(3):
        issue(qkv_copy(step, part) for step in range(1, size))
    while line_step < depth - 1:
        for way in (1, -1):
            wait_recv(one_arrives(line_step, way))
            start(one_line(line_step + 1, way))
        line_step += 1

    local[1].wait()
    for stage in range(-1, count - 1):
        arrive(both_parts(row_cores, 0, stage))
    gain = full_ref[0:1, :]
    shift = full_ref[1:2, :]

    @pl.loop(0, micro * size)
    def _(index):
        m, block = index // size, lax.rem(index, size)
        x = gathered[m, block].astype(F32)
        center = x - jnp.mean(x, axis=-1, keepdims=True)
        spread = jnp.mean(center * center, axis=-1, keepdims=True)
        y = center * lax.rsqrt(spread + EPSILON) * gain + shift
        normed_ref[m, block] = y.astype(BF)

    for copy in local[2:]:
        copy.wait()
    for stage in range(-1, count - 1):
        arrive(both_parts(row_cores, 1, stage))
    for part in range(3):
        arrive(qkv_copy(step, part) for step in range(1, size))
    for way in (1, -1):
        wait_recv(two_arrives(way))
        wait_recv(one_arrives(depth - 1, way))

    for step in range(1, size):
        vec_seq_copy(step).wait_send()
        one_copy(step).wait_send()
        for part in range(3):
            qkv_copy(step, part).wait_send()
    for step in range(1, depth):
        vec_line_copy(step).wait_send()
        for way in (1, -1):
            wait_send(one_line(step, way))
    for way in (1, -1):
        wait_send(two_line(way))
    for which in range(2):
        for stage in range(-1, count - 1):
            for copy in both_parts(row_cores, which, stage):
                copy.wait_send()
            if stage >= 0:
                for copy in both_parts(row_stage, which, stage):
                    copy.wait_send()


def load_all(tokens, upstream, w_fc1, w_fc2, w_qkv, w_out, vectors):
    size, depth = lax.axis_size("seq"), lax.axis_size("fsdp")
    micro, length, width = tokens.shape
    rows, units, cols = w_fc1.shape[0], w_fc1.shape[1] // size, width // size
    dims = (size, depth, micro, length, width, units, cols)
    hbm = pl.BlockSpec(memory_space=pl.ANY)
    vmem = pl.BlockSpec(memory_space=pltpu.VMEM)
    gathered = (micro, size, length, width)
    dma = pltpu.SemaphoreType.DMA
    return pl.pallas_call(
        functools.partial(load_kernel, dims),
        in_specs=[hbm] * 6 + [vmem],
        out_specs=[vmem] + [hbm] * 4 + [vmem],
        out_shape=[
            jax.ShapeDtypeStruct(gathered, BF),
            jax.ShapeDtypeStruct(gathered, BF),
            jax.ShapeDtypeStruct((size, depth, rows, units), BF),
            jax.ShapeDtypeStruct((depth,) + w_fc2.shape, BF),
            jax.ShapeDtypeStruct((size, rows, 4 * cols), BF),
            jax.ShapeDtypeStruct(vectors.shape, F32),
        ],
        scratch_shapes=[
            pltpu.VMEM(gathered, BF),
            pltpu.VMEM((size,) + vectors.shape, BF),
            pltpu.VMEM(vectors.shape, BF),
            pltpu.VMEM((depth,) + vectors.shape, BF),
            dma((7 + size,)),
            dma((size + depth,)),
            dma((size + depth,)),
            dma((4 * size,)),
            dma((4 * size,)),
            dma((2 * depth + 2,)),
            dma((2 * depth + 2,)),
            dma((4 * size,)),
            dma((4 * size,)),
        ],
        compiler_params=pltpu.CompilerParams(
            collective_id=1, has_side_effects=True, vmem_limit_bytes=40 * 1024 * 1024
        ),
        cost_estimate=pl.CostEstimate(
            flops=1000, bytes_accessed=300 * 1000 * 1000, transcendentals=0
        ),
    )(tokens, upstream, w_fc1, w_fc2, w_qkv, w_out, vectors)


def ffn_kernel(
    dims,
    normed_hbm,
    up_hbm,
    one_hbm,
    two_hbm,
    cols_hbm,
    full_ref,
    hidden_hbm,
    pre_hbm,
    all_two_hbm,
    attn_hbm,
    grad_two_hbm,
    grad_one_hbm,
    land_two,
    land_one,
    bone_ref,
    normed_v,
    up_v,
    one_v,
    two_v,
    hidden_v,
    pre_v,
    grad_two_v,
    grad_one_v,
    own_two,
    held_two,
    out_two,
    load_sem,
    line_load,
    store_sem,
    two_send,
    two_recv,
    attn_send,
    attn_recv,
    sum_two_send,
    sum_two_recv,
    sum_one_send,
    sum_one_recv,
):
    size, depth, micro, length, width, units, cols = dims
    me, at = lax.axis_index("seq"), lax.axis_index("fsdp")
    count = micro * size * length
    tile = 512
    group = units // depth

    loads = [
        pltpu.make_async_copy(src, dst, load_sem.at[n])
        for n, (src, dst) in enumerate(
            ((normed_hbm, normed_v), (one_hbm, one_v), (up_hbm, up_v))
        )
    ]
    for load in loads:
        load.start()

    def two_load(way):
        origin = jnp.clip(at + way, 0, depth - 1)
        return (at + way >= 0) & (at + way < depth), pltpu.make_async_copy(
            two_hbm.at[origin], two_v.at[origin], load_sem.at[4 + way]
        )

    for way in (0, 1, -1):
        ok, copy = two_load(way)

        @pl.when(ok)
        def _():
            copy.start()

    own_attn = pltpu.make_async_copy(cols_hbm, attn_hbm.at[:, at], store_sem.at[0])
    own_attn.start()
    greet(size, depth)

    two = LineGather(
        depth,
        lambda o, step: two_hbm.at[o] if step == 2 else two_v.at[o],
        lambda o: two_v.at[o],
        two_send,
        two_recv,
    )
    attn = LineGather(
        depth,
        lambda o, step: cols_hbm if step == 1 else attn_hbm.at[:, o],
        lambda o: attn_hbm.at[:, o],
        attn_send,
        attn_recv,
    )
    sum_two = LineSum(
        depth,
        lambda o: grad_two_v.at[o],
        lambda step, way: land_two.at[(step - 1) * 2 + (way > 0)],
        own_two,
        held_two,
        lambda step, way: out_two.at[int(way > 0)],
        line_load,
        sum_two_send,
        sum_two_recv,
    )
    sum_one = LineSum(
        depth,
        lambda o: grad_one_v.at[:, o],
        lambda step, way: land_one.at[(step - 1) * 2 + (way > 0)],
        own_two,
        held_two,
        lambda step, way: grad_one_v.at[:, 0],
        line_load,
        sum_one_send,
        sum_one_recv,
    )
    two.start(2)

    for load in loads[:2]:
        load.wait()
    root = math.sqrt(2.0 / math.pi)
    flat = me * units
    bias_row = 6 + flat // width
    bias_at = pl.multiple_of(lax.rem(flat, width), units)
    bias = full_ref[pl.ds(bias_row, 1), pl.ds(bias_at, units)]
    bone_ref[...] = bias

    @pl.loop(0, count // tile)
    def _(r):
        rows = pl.ds(pl.multiple_of(r * tile, tile), tile)
        a = normed_v[rows, :]
        for o in range(depth):
            columns = slice(o * group, (o + 1) * group)
            w = one_v[:, :, :, columns].reshape(width, group)
            v = jnp.dot(a, w, preferred_element_type=F32) + bone_ref[:, columns]
            square = v * v
            t = jnp.tanh(root * v * (1.0 + 0.044715 * square))
            hidden_v[rows, columns] = (0.5 * v * (1.0 + t)).astype(BF)
            slope = 0.5 * (1.0 + t) + 0.5 * root * v * (1.0 - t * t) * (
                1.0 + 3 * 0.044715 * square
            )
            pre_v[rows, columns] = slope.astype(BF)

    loads[2].wait()
    hidden_out = pltpu.make_async_copy(hidden_v, hidden_hbm, store_sem.at[1])
    hidden_out.start()
    over_first = (((0,), (0,)), ((), ()))
    over_last = (((1,), (1,)), ((), ()))

    @pl.loop(0, depth)
    def _(o):
        columns = pl.ds(pl.multiple_of(o * group, group), group)
        y = lax.dot_general(hidden_v[:, columns], up_v[...], over_first, preferred_element_type=F32)
        grad_two_v[o] = y.astype(BF)

    two.arrive(2)
    two.start(3)
    sum_two.start(1)
    grad_two_out = pltpu.make_async_copy(grad_two_v, grad_two_hbm, store_sem.at[2])
    grad_two_out.start()
    bone_ref[...] = jnp.zeros_like(bone_ref)

    def piece(o):
        columns = pl.ds(pl.multiple_of(o * group, group), group)

        @pl.loop(0, count // tile)
        def _(r):
            rows = pl.ds(pl.multiple_of(r * tile, tile), tile)
            y = lax.dot_general(up_v[rows, :], two_v[o], over_last, preferred_element_type=F32)
            y = (y * pre_v[rows, columns].astype(F32)).astype(BF)
            pre_v[rows, columns] = y
            bone_ref[:, columns] += jnp.sum(y.astype(F32), axis=0, keepdims=True)

        wide = 1024
        per = width // size

        @pl.loop(0, width // wide)
        def _(d):
            rows = pl.ds(pl.multiple_of(d * wide, wide), wide)
            y = lax.dot_general(
                normed_v[:, rows], pre_v[:, columns], over_first, preferred_element_type=F32
            )
            n = wide // per
            y = y.astype(BF).reshape(n, depth, per // depth, group)
            grad_one_v[pl.ds(d * n, n), :, :, columns] = y

    for way in (0, 1, -1):
        ok, copy = two_load(way)

        @pl.when(ok)
        def _():
            copy.wait()

    @pl.loop(0, 2 * depth - 3)
    def _(number):
        distance = (number + 1) // 2
        origin = jnp.where(lax.rem(number, 2) == 1, at - distance, at + distance)

        @pl.when((origin >= 0) & (origin < depth))
        def _():
            piece(jnp.clip(origin, 0, depth - 1))

    two.arrive(3)
    attn.start(1)

    @pl.loop(2 * depth - 3, 2 * depth - 1)
    def _(number):
        distance = (number + 1) // 2
        origin = jnp.where(lax.rem(number, 2) == 1, at - distance, at + distance)

        @pl.when((origin >= 0) & (origin < depth))
        def _():
            piece(jnp.clip(origin, 0, depth - 1))

    stores = [
        pltpu.make_async_copy(pre_v, pre_hbm, store_sem.at[3]),
        pltpu.make_async_copy(two_v, all_two_hbm, store_sem.at[4]),
        pltpu.make_async_copy(grad_one_v, grad_one_hbm, store_sem.at[5]),
    ]
    for store in stores:
        store.start()
    attn.arrive(1)
    attn.start(2)
    sum_one.start(1)
    attn.arrive(2)
    attn.start(3)
    sum_two.start(2)
    own_attn.wait()
    hidden_out.wait()
    grad_two_out.wait()
    for store in stores:
        store.wait()
    attn.arrive(3)
    sum_two.arrive(1, True)
    sum_two.arrive(2, False)
    sum_one.arrive(1, False)
    for step in (2, 3):
        two.sent(step)
    for step in (1, 2, 3):
        attn.sent(step)
    sum_two.sent(1)
    sum_two.sent(2)
    sum_one.sent(1)


def feed_forward(normed, up, one, two, columns, full):
    size, depth = lax.axis_size("seq"), lax.axis_size("fsdp")
    micro, _, length, width = normed.shape
    units, cols = one.shape[-1], width // size
    rows = width // (size * depth)
    count = micro * size * length
    dims = (size, depth, micro, length, width, units, cols)
    hbm = pl.BlockSpec(memory_space=pl.ANY)
    vmem = pl.BlockSpec(memory_space=pltpu.VMEM)
    dma = pltpu.SemaphoreType.DMA
    sums = dma((2 * depth,))
    shape = jax.ShapeDtypeStruct
    tall, deep = (depth, units // depth, width), (size, depth, rows, units)
    return pl.pallas_call(
        functools.partial(ffn_kernel, dims),
        in_specs=[hbm] * 5 + [vmem],
        out_specs=[hbm] * 8 + [vmem],
        out_shape=[
            shape((count, units), BF),
            shape((count, units), BF),
            shape(tall, BF),
            shape((size, depth, rows, 4 * cols), BF),
            shape(tall, BF),
            shape(deep, BF),
            shape((4,) + tall[1:], BF),
            shape((2, size, rows, units), BF),
            shape((1, units), F32),
        ],
        scratch_shapes=[
            pltpu.VMEM((count, width), BF),
            pltpu.VMEM((count, width), BF),
            pltpu.VMEM(deep, BF),
            pltpu.VMEM(tall, BF),
            pltpu.VMEM((count, units), BF),
            pltpu.VMEM((count, units), BF),
            pltpu.VMEM(tall, BF),
            pltpu.VMEM(deep, BF),
            pltpu.VMEM(tall[1:], BF),
            pltpu.VMEM(tall[1:], BF),
            pltpu.VMEM((2,) + tall[1:], BF),
            dma((6,)),
            dma((2,)),
            dma((6,)),
        ]
        + [sums] * 8,
        compiler_params=pltpu.CompilerParams(
            collective_id=2, has_side_effects=True, vmem_limit_bytes=60 * 1024 * 1024
        ),
        cost_estimate=pl.CostEstimate(
            flops=34 * 1000**3, bytes_accessed=300 * 1000 * 1000, transcendentals=0
        ),
    )(normed.reshape(count, width), up.reshape(count, width), one, two, columns, full)


def attn_layer_kernel(
    dims,
    starts_ref,
    cos_ref,
    sin_ref,
    normed_hbm,
    up_hbm,
    attn_hbm,
    grad_two_hbm,
    grad_one_hbm,
    old_two,
    old_one,
    full_ref,
    turned_hbm,
    mixed_hbm,
    grads_hbm,
    one_hbm,
    land_two,
    land_one,
    bqkv_ref,
    two_ref,
    normed_v,
    up_v,
    attn_v,
    natural_v,
    turned_v,
    mixed_v,
    grads_v,
    dk_s,
    dv_s,
    bias_s,
    own_two,
    held_two,
    out_two,
    own_one,
    held_one,
    out_one,
    load_sem,
    line_load,
    store_sem,
    sum_two_send,
    sum_two_recv,
    sum_one_send,
    sum_one_recv,
):
    size, depth, micro, length, width, units, cols = dims
    me = lax.axis_index("seq")
    chips = size // 2
    groups = cols // LANES
    total = size * length
    count = micro * total
    per = width // size
    loads = [
        pltpu.make_async_copy(src, dst, load_sem.at[n])
        for n, (src, dst) in enumerate(
            ((normed_hbm, normed_v), (attn_hbm, attn_v), (up_hbm, up_v))
        )
    ]
    for load in loads:
        load.start()
    greet(size, depth)
    sum_two = LineSum(
        depth,
        lambda o: grad_two_hbm.at[o],
        lambda step, way: (
            old_two.at[(step - 1) * 2 + (way > 0)] if step < 3 else land_two.at[int(way > 0)]
        ),
        own_two,
        held_two,
        lambda step, way: out_two.at[int(way > 0)],
        line_load,
        sum_two_send,
        sum_two_recv,
    )
    sum_one = LineSum(
        depth,
        lambda o: grad_one_hbm.at[:, o],
        lambda step, way: (
            old_one.at[int(way > 0)] if step < 2 else land_one.at[(step - 2) * 2 + (way > 0)]
        ),
        own_one,
        held_one,
        lambda step, way: out_one.at[(step - 2) * 2 + (way > 0)],
        line_load,
        sum_one_send,
        sum_one_recv,
    )
    sum_two.start(3, here=False)
    sum_one.start(2, here=False)
    for load in loads:
        load.wait()

    lane = lax.broadcasted_iota(jnp.int32, (1, LANES), 1)
    low_lane = (lane % HEAD_DIM) < (ROT // 2)
    over_first = (((0,), (0,)), ((), ()))
    over_last = (((1,), (1,)), ((), ()))

    def turn(value, cosine, sine):
        other = jnp.where(
            low_lane,
            pltpu.roll(value, LANES - ROT // 2, 1),
            pltpu.roll(value, ROT // 2, 1),
        )
        return value * cosine + other * sine

    high = chips * length

    @pl.loop(0, micro * 2)
    def _(r):
        m, parity = r // 2, lax.rem(r, 2)
        rows = pl.ds(pl.multiple_of(r * high, high), high)
        a = normed_v[rows, :]
        u = up_v[rows, :]
        for part in range(3):
            w = attn_v[:, :, :, part * cols : (part + 1) * cols].reshape(width, cols)
            y = jnp.dot(a, w, preferred_element_type=F32)
            y = y + full_ref[2 + part : 3 + part, pl.ds(pl.multiple_of(me * cols, cols), cols)]
            for block in range(chips):
                at = pl.ds(pl.multiple_of((block * 2 + parity) * length, length), length)
                cosine, sine = cos_ref[at, :], sin_ref[at, :]
                for g in range(groups):
                    v = y[block * length : (block + 1) * length, g * LANES : (g + 1) * LANES]
                    if part < 2:
                        v = turn(v, cosine, sine)
                    v = v.astype(BF)
                    if part == 0:
                        v = v * jnp.asarray(SCALE, BF)
                    natural_v[part, m, g, at, :] = v
        y = jnp.zeros((high, cols), F32)
        for s in range(size):
            w = attn_v[s, :, :, 3 * cols :].reshape(cols, cols)
            y = y + lax.dot_general(
                u[:, s * per : (s + 1) * per], w, over_last, preferred_element_type=F32
            )
        for block in range(chips):
            at = pl.ds(pl.multiple_of((block * 2 + parity) * length, length), length)
            for g in range(groups):
                v = y[block * length : (block + 1) * length, g * LANES : (g + 1) * LANES]
                natural_v[3, m, g, at, :] = v.astype(BF)

    tile = 256

    @pl.loop(0, micro * groups)
    def _(index):
        m, g = index // groups, lax.rem(index, groups)

        @pl.when(index == micro * groups - 1)
        def _():
            sum_one.start(3)

        def label(positions):
            found = jnp.full(positions.shape, -1, jnp.int32)
            for piece in range(PIECES):
                start = starts_ref[m, piece]
                found = jnp.where((positions >= start) & (positions < start + IMG), piece, found)
            return found

        def put(target, at, columns, value):
            for part in range(value.shape[0] // length):
                block = at // length + part
                rows = m * total + store_index(block) * length
                target[pl.ds(pl.multiple_of(rows, length), length), columns] = value[
                    part * length : (part + 1) * length
                ].astype(BF)

        def columns_of(part):
            return pl.ds(pl.multiple_of(part * cols + g * LANES, LANES), LANES)

        dk_s[...] = jnp.zeros_like(dk_s)
        dv_s[...] = jnp.zeros_like(dv_s)
        for first in range(0, total, tile):
            last = min(total, first + tile + IMG)
            qpos = first + lax.broadcasted_iota(jnp.int32, (tile, 1), 0)
            kpos = first + lax.broadcasted_iota(jnp.int32, (1, last - first), 1)
            qlab, klab = label(qpos), label(kpos)
            allowed = (kpos <= qpos) | ((qlab == klab) & (qlab >= 0))
            bias_s[:, : last - first] = jnp.where(allowed, 0.0, -1e30)
            rows = slice(first, first + tile)
            keys = natural_v[1, m, g, :last, :]
            values = natural_v[2, m, g, :last, :]
            mixed = jnp.zeros((tile, LANES), F32)
            dq = jnp.zeros((tile, LANES), F32)
            for head in range(LANES // HEAD_DIM):
                mine = (lane // HEAD_DIM) == head
                q = jnp.where(mine, natural_v[0, m, g, rows, :], 0)
                do = jnp.where(mine, natural_v[3, m, g, rows, :], 0)
                s = lax.dot_general(q, keys, over_last, preferred_element_type=F32)
                if first:
                    s = jnp.concatenate(
                        [s[:, :first], s[:, first:] + bias_s[:, : last - first]], axis=1
                    )
                else:
                    s = s + bias_s[:, : last - first]
                p = jnp.exp(s - jnp.max(s, axis=1, keepdims=True))
                p = p * (1.0 / jnp.sum(p, axis=1, keepdims=True))
                probs = p.astype(BF)
                att = jnp.dot(probs, values, preferred_element_type=F32)
                mixed = jnp.where(mine, att, mixed)
                dp = lax.dot_general(do, values, over_last, preferred_element_type=F32)
                delta = jnp.sum(p * dp, axis=1, keepdims=True)
                ds = (p * (dp - delta)).astype(BF)
                dq = jnp.where(mine, jnp.dot(ds, keys, preferred_element_type=F32), dq)
                dk_s[:last, :] += lax.dot_general(ds, q, over_first, preferred_element_type=F32)
                dv_s[:last, :] += lax.dot_general(
                    probs, do, over_first, preferred_element_type=F32
                )
            put(mixed_v, first, pl.ds(pl.multiple_of(g * LANES, LANES), LANES), mixed)
            dq = turn(dq * SCALE, cos_ref[rows, :], -sin_ref[rows, :])
            put(turned_v, first, columns_of(0), dq)
        put(turned_v, 0, columns_of(1), turn(dk_s[...], cos_ref[...], -sin_ref[...]))
        put(turned_v, 0, columns_of(2), dv_s[...])

    stores = [
        pltpu.make_async_copy(turned_v, turned_hbm, store_sem.at[0]),
        pltpu.make_async_copy(mixed_v, mixed_hbm, store_sem.at[1]),
    ]
    for store in stores:
        store.start()

    wide = 512

    @pl.loop(0, width // wide)
    def _(d):
        rows = pl.ds(pl.multiple_of(d * wide, wide), wide)
        y = lax.dot_general(normed_v[:, rows], turned_v[...], over_first, preferred_element_type=F32)
        n = wide // per
        grads_v[pl.ds(d * n, n), :, :, : 3 * cols] = y.astype(BF).reshape(
            n, depth, per // depth, 3 * cols
        )
        y = lax.dot_general(mixed_v[...], up_v[:, rows], over_first, preferred_element_type=F32)
        y = y.astype(BF)
        for k in range(n):
            grads_v[d * n + k, :, :, 3 * cols :] = y[:, k * per : (k + 1) * per].reshape(
                depth, cols // depth, per
            )

    grads_out = pltpu.make_async_copy(grads_v, grads_hbm, store_sem.at[2])
    grads_out.start()
    bqkv_ref[...] = jnp.sum(turned_v[...].astype(F32), axis=0, keepdims=True)
    sum_two.sent(3)
    two_ref[...] = sum_two.total(3, held_two, out_two.at[0])
    sum_one.sent(2)
    one_sum = sum_one.total(3, held_one, out_one.at[0])
    out_one[1] = one_sum.astype(BF)
    one_out = pltpu.make_async_copy(out_one.at[1], one_hbm, store_sem.at[3])
    one_out.start()
    for store in stores:
        store.wait()
    grads_out.wait()
    one_out.wait()
    sum_one.sent(3)


def attention_layer(starts, normed, up, attn, grad_two, grad_one, old_two, old_one, full):
    size, depth, rows, units = grad_one.shape
    micro, _, length, width = normed.shape
    cols = width // size
    count, total = micro * size * length, size * length
    dims = (size, depth, micro, length, width, units, cols)
    cosine, sine = tables(total)
    hbm = pl.BlockSpec(memory_space=pl.ANY)
    vmem = pl.BlockSpec(memory_space=pltpu.VMEM)
    dma = pltpu.SemaphoreType.DMA
    sums = dma((2 * depth,))
    shape = jax.ShapeDtypeStruct
    tall, deep = (units // depth, width), (size, rows, units)
    return pl.pallas_call(
        functools.partial(attn_layer_kernel, dims),
        in_specs=[pl.BlockSpec(memory_space=pltpu.SMEM)] + [vmem] * 2 + [hbm] * 7 + [vmem],
        out_specs=[hbm] * 6 + [vmem] * 2,
        out_shape=[
            shape((count, 3 * cols), BF),
            shape((count, cols), BF),
            shape(attn.shape, BF),
            shape(deep, BF),
            shape((2,) + tall, BF),
            shape((4,) + deep, BF),
            shape((1, 3 * cols), F32),
            shape(tall, F32),
        ],
        scratch_shapes=[
            pltpu.VMEM((count, width), BF),
            pltpu.VMEM((count, width), BF),
            pltpu.VMEM(attn.shape, BF),
            pltpu.VMEM((4, micro, cols // LANES, total, LANES), BF),
            pltpu.VMEM((count, 3 * cols), BF),
            pltpu.VMEM((count, cols), BF),
            pltpu.VMEM(attn.shape, BF),
            pltpu.VMEM((total, LANES), F32),
            pltpu.VMEM((total, LANES), F32),
            pltpu.VMEM((256, 512), F32),
            pltpu.VMEM(tall, BF),
            pltpu.VMEM(tall, BF),
            pltpu.VMEM((2,) + tall, BF),
            pltpu.VMEM(deep, BF),
            pltpu.VMEM(deep, BF),
            pltpu.VMEM((4,) + deep, BF),
            dma((3,)),
            dma((2,)),
            dma((4,)),
        ]
        + [sums] * 4,
        compiler_params=pltpu.CompilerParams(
            collective_id=3, has_side_effects=True, vmem_limit_bytes=60 * 1024 * 1024
        ),
        cost_estimate=pl.CostEstimate(
            flops=40 * 1000**3, bytes_accessed=300 * 1000 * 1000, transcendentals=0
        ),
    )(
        starts,
        cosine,
        sine,
        normed.reshape(count, width),
        up.reshape(count, width),
        attn,
        grad_two,
        grad_one,
        old_two,
        old_one,
        full,
    )


def close_kernel(
    dims,
    tokens_hbm,
    up_hbm,
    grads_hbm,
    attn_hbm,
    one_hbm,
    two_hbm,
    turned_hbm,
    pre_hbm,
    mixed_hbm,
    hidden_hbm,
    one_sum_hbm,
    full_ref,
    bqkv_ref,
    bone_ref,
    act_ref,
    ingrad_ref,
    qkv_ref,
    out_ref,
    vec_ref,
    one_out_hbm,
    landing,
    tokens_v,
    up_v,
    attn_v,
    one_v,
    two_v,
    turned_v,
    pre_v,
    mixed_v,
    hidden_v,
    to_core,
    sums,
    coming,
    line_a,
    line_b,
    line_out,
    total_v,
    spread_v,
    one_land,
    one_wide,
    vec_in,
    load_sem,
    core_send,
    core_recv,
    axis_send,
    axis_recv,
    line_load,
    line_send,
    line_recv,
    a2a_send,
    a2a_recv,
    vec_send,
    vec_recv,
    one_send,
    one_recv,
    wide_sem,
):
    size, depth, micro, length, width, units, cols = dims
    me, at = lax.axis_index("seq"), lax.axis_index("fsdp")
    count = size.bit_length() - 1
    chips = size // 2
    chip, core = me >> 1, me & 1
    half = width // 2
    per = width // size

    loads = [
        pltpu.make_async_copy(src, dst, load_sem.at[n])
        for n, (src, dst) in enumerate(
            (
                (turned_hbm, turned_v),
                (attn_hbm, attn_v),
                (pre_hbm, pre_v),
                (one_hbm, one_v),
                (hidden_hbm, hidden_v),
                (two_hbm, two_v),
                (mixed_hbm, mixed_v),
                (tokens_hbm, tokens_v),
                (up_hbm, up_v),
            )
        )
    ]
    for load in loads:
        load.start()
    greet(size, depth)

    def line_copy(step, way, part, src):
        number = (step * 2 + (way > 0)) * 2 + part
        return remote(
            src,
            landing.at[number],
            line_send.at[number],
            line_recv.at[number],
            {"fsdp": jnp.clip(at + way, 0, depth - 1)},
        )

    def place_of(way):
        return at if way > 0 else depth - 1 - at

    def chunk(origin, part):
        return grads_hbm.at[pl.ds(part * chips, chips), origin]

    def line_step(step):
        for part in range(2):
            for way in (1, -1):
                place = place_of(way)
                away = jnp.clip(depth - step + place, 0, depth - 1)
                origin = away if way > 0 else depth - 1 - away
                slot = (way > 0) * 2 + part

                @pl.when(place == 0)
                def _():
                    line_copy(step, way, part, chunk(origin, part)).start()

                if step > 1:

                    @pl.when((place >= 1) & (place <= step - 1) & (place < depth - 1))
                    def _():
                        mine = pltpu.make_async_copy(
                            chunk(origin, part), line_a.at[0], line_load.at[0]
                        )
                        mine.start()
                        arrived = line_copy(step - 1, way, part, line_out.at[slot])
                        arrived.wait_recv()
                        came = pltpu.make_async_copy(
                            landing.at[((step - 1) * 2 + (way > 0)) * 2 + part],
                            line_b.at[0],
                            line_load.at[1],
                        )
                        came.start()

                        @pl.when(place <= step - 2)
                        def _():
                            arrived.wait_send()

                        mine.wait()
                        came.wait()
                        line_out[slot] = (
                            line_a[0].astype(F32) + line_b[0].astype(F32)
                        ).astype(BF)
                        line_copy(step, way, part, line_out.at[slot]).start()

    def line_finish(part):
        mine = pltpu.make_async_copy(chunk(at, part), line_a.at[0], line_load.at[0])
        mine.start()
        for way in (1, -1):
            place = place_of(way)
            slot = int(way > 0)

            @pl.when(place >= 1)
            def _():
                line_copy(depth - 1, way, part, line_out.at[0]).wait_recv()
                came = pltpu.make_async_copy(
                    landing.at[((depth - 1) * 2 + (way > 0)) * 2 + part],
                    line_b.at[slot],
                    line_load.at[1],
                )
                came.start()
                came.wait()

            @pl.when(place == 0)
            def _():
                line_b[slot] = jnp.zeros_like(line_b[slot])

        mine.wait()
        summed = line_a[0].astype(F32) + line_b[0].astype(F32) + line_b[1].astype(F32)
        total_v[pl.ds(part * chips, chips)] = summed.astype(BF)
        for block in range(chips):
            out_ref[:, (part * chips + block) * cols : (part * chips + block + 1) * cols] = summed[
                block, :, 3 * cols :
            ]

    def line_sent():
        for part in range(2):
            for way in (1, -1):
                place = place_of(way)

                @pl.when(place == 0)
                def _():
                    for step in range(1, depth):
                        line_copy(step, way, part, line_out.at[0]).wait_send()

                @pl.when((place >= 1) & (place < depth - 1))
                def _():
                    line_copy(depth - 1, way, part, line_out.at[0]).wait_send()

    def back_copy(step):
        peer = me ^ step
        return remote(
            total_v.at[peer, :, pl.ds(0, 3 * cols)],
            spread_v.at[me],
            a2a_send.at[step],
            a2a_recv.at[step],
            {"seq": peer},
        )

    def one_copy(step):
        peer = me ^ step
        return remote(
            one_sum_hbm.at[peer],
            one_land.at[me],
            one_send.at[step],
            one_recv.at[step],
            {"seq": peer},
        )

    one_mine = pltpu.make_async_copy(one_sum_hbm.at[me], one_land.at[me], one_recv.at[0])

    def one_widen():
        one_mine.wait()
        for step in range(1, size):
            one_copy(step).wait_recv()

        def copy(block, slot):
            at = pl.ds(pl.multiple_of(block * units, units), units)
            return pltpu.make_async_copy(
                one_wide.at[slot], one_out_hbm.at[:, at], wide_sem.at[slot]
            )

        for block in range(size):
            slot = block % 2
            if block >= 2:
                copy(block - 2, slot).wait()
            one_wide[slot] = one_land[block].astype(F32)
            copy(block, slot).start()
        for block in range(size - 2, size):
            copy(block, block % 2).wait()

    def core_copy(array, m):
        number = array * micro + m
        return remote(
            to_core.at[m],
            sums.at[number],
            core_send.at[number],
            core_recv.at[number],
            {"seq": me ^ 1},
        )

    orders = (list(range(count - 1)), list(range(count - 1))[::-1])

    def stage_copies(array, m, part, stage):
        bit = orders[part][stage]
        done = sum(1 << b for b in orders[part][:stage])
        first = chips - (chips >> stage)
        columns = slice(part * half, (part + 1) * half)
        found = []
        for mask in range(chips):
            if mask & (done | (1 << bit)):
                continue
            slot = first + len(found)
            number = ((array * micro + m) * 2 + part) * (chips - 1) + slot
            copy = remote(
                sums.at[array * micro + m, chip ^ (mask | (1 << bit)), :, columns],
                coming.at[array * micro + m, slot, :, columns],
                axis_send.at[number],
                axis_recv.at[number],
                {"seq": me ^ (2 << bit)},
            )
            found.append((mask, slot, copy))
        return found

    def stage_start(array, m, stage):
        for part in range(2):
            for _, _, copy in stage_copies(array, m, part, stage):
                copy.start()

    def stage_add(array, m, stage):
        number = array * micro + m
        for part in range(2):
            columns = slice(part * half, (part + 1) * half)
            for mask, slot, copy in stage_copies(array, m, part, stage):
                copy.wait_recv()
                if stage < count - 2:
                    block = chip ^ mask
                    sums[number, block, :, columns] = (
                        sums[number, block, :, columns].astype(F32)
                        + coming[number, slot, :, columns].astype(F32)
                    ).astype(BF)

    def stage_last(array, m):
        number = array * micro + m
        return sums[number, chip].astype(F32) + coming[number, chips - 2].astype(F32)

    over_last = (((1,), (1,)), ((), ()))

    def grad_terms(m, parity, write):
        first = parity * chips
        turned = turned_v[m, pl.ds(first, chips)].reshape(chips * length, 3 * cols)
        pre = pre_v[m, pl.ds(first, chips)].reshape(chips * length, units)

        @pl.loop(0, size)
        def _(s):
            w = attn_v[s, :, :, : 3 * cols].reshape(per, 3 * cols)
            y = lax.dot_general(turned, w, over_last, preferred_element_type=F32)
            w = one_v[s].reshape(per, units)
            y = y + lax.dot_general(pre, w, over_last, preferred_element_type=F32)
            write(pl.ds(pl.multiple_of(s * per, per), per), y.reshape(chips, length, per))

    def act_terms(m, parity, write):
        first = parity * chips
        mixed = mixed_v[m, pl.ds(first, chips)].reshape(chips * length, cols)
        hidden = hidden_v[m, pl.ds(first, chips)].reshape(chips * length, units)

        @pl.loop(0, size)
        def _(s):
            columns = pl.ds(pl.multiple_of(s * per, per), per)
            w = attn_v[s, :, :, 3 * cols :].reshape(per, cols)
            y = jnp.dot(mixed, w, preferred_element_type=F32)
            w = two_v[:, :, columns].reshape(units, per)
            y = y + jnp.dot(hidden, w, preferred_element_type=F32)
            write(columns, y.reshape(chips, length, per))

    def terms_away(array, m, function):
        if array:
            core_copy(0, m).wait_send()

        def write(columns, y):
            to_core[m, :, :, columns] = y.astype(BF)

        function(m, 1 - core, write)
        core_copy(array, m).start()

    def terms_here(array, m, function):
        core_copy(array, m).wait_recv()
        number = array * micro + m

        def write(columns, y):
            sums[number, :, :, columns] = (y + sums[number, :, :, columns].astype(F32)).astype(BF)

        function(m, core, write)
        stage_start(array, m, 0)

    gain = full_ref[0:1, :]
    vec_ref[...] = jnp.zeros_like(vec_ref)
    for part in range(3):
        columns = pl.ds(pl.multiple_of(me * cols, cols), cols)
        vec_ref[2 + part : 3 + part, columns] = bqkv_ref[:, part * cols : (part + 1) * cols]
    bone_at = pl.multiple_of(lax.rem(me * units, width), units)
    vec_ref[pl.ds(6 + me * units // width, 1), pl.ds(bone_at, units)] = bone_ref[...]

    def norm_back(m):
        x = tokens_v[m].astype(F32)
        dy = stage_last(0, m)
        center = x - jnp.mean(x, axis=-1, keepdims=True)
        spread = jnp.mean(center * center, axis=-1, keepdims=True)
        r = lax.rsqrt(spread + EPSILON)
        xhat = center * r
        g = dy * gain
        inner = g - jnp.mean(g, axis=-1, keepdims=True)
        inner = inner - xhat * jnp.mean(g * xhat, axis=-1, keepdims=True)
        upstream = up_v[m].astype(F32)
        ingrad_ref[m] = upstream + r * inner
        vec_ref[5:6, :] += jnp.sum(upstream, axis=0, keepdims=True)
        vec_ref[0:1, :] += jnp.sum(dy * xhat, axis=0, keepdims=True)
        vec_ref[1:2, :] += jnp.sum(dy, axis=0, keepdims=True)

    def act_out(m):
        bias = full_ref[5:6, :] + full_ref[6 + size * units // width : 7 + size * units // width, :]
        total = tokens_v[m].astype(F32) + stage_last(1, m) + bias
        act_ref[m] = total.astype(BF)

    levels = [("seq", 1 << bit) for bit in range(count)]
    levels = levels + [("fsdp", 1 << bit) for bit in range(depth.bit_length() - 1)]

    def vec_copy(level):
        axis, step = levels[level]
        mine = me if axis == "seq" else at
        return remote(
            vec_ref,
            vec_in.at[level],
            vec_send.at[level],
            vec_recv.at[level],
            {axis: mine ^ step},
        )

    def vec_level(level):
        copy = vec_copy(level)
        copy.wait()
        vec_ref[...] += vec_in[level]
        if level + 1 < len(levels):
            vec_copy(level + 1).start()

    one_mine.start()
    for step in range(1, size):
        one_copy(step).start()
    line_step(1)
    for load in loads[:4]:
        load.wait()
    for m in range(micro):
        terms_away(0, m, grad_terms)
    for m in range(micro):
        terms_here(0, m, grad_terms)
    line_step(2)
    for load in loads[4:]:
        load.wait()
    stage_add(0, 0, 0)
    stage_start(0, 0, 1)
    for m in range(micro):
        terms_away(1, m, act_terms)
    stage_add(0, 1, 0)
    stage_start(0, 1, 1)
    for m in range(micro):
        terms_here(1, m, act_terms)
    one_widen()
    stage_add(0, 0, 1)
    norm_back(0)
    line_step(3)
    stage_add(0, 1, 1)
    norm_back(1)
    vec_copy(0).start()
    stage_add(1, 0, 0)
    stage_start(1, 0, 1)
    vec_level(0)
    vec_level(1)
    stage_add(1, 1, 0)
    stage_start(1, 1, 1)
    vec_level(2)
    vec_level(3)
    stage_add(1, 0, 1)
    act_out(0)
    vec_level(4)
    stage_add(1, 1, 1)
    act_out(1)
    for part in range(2):
        line_finish(part)
        for step in range(1, size):
            peer = me ^ step

            @pl.when((peer >= part * chips) & (peer < (part + 1) * chips))
            def _():
                back_copy(step).start()

    def put(block, values):
        for part in range(3):
            start = pl.multiple_of(part * width + block * cols, cols)
            qkv_ref[:, pl.ds(start, cols)] = values[:, part * cols : (part + 1) * cols]

    put(me, total_v[me, :, : 3 * cols].astype(F32))
    for step in range(1, size):
        back_copy(step).wait_recv()
        put(me ^ step, spread_v[me ^ step].astype(F32))

    line_sent()
    for step in range(1, size):
        back_copy(step).wait_send()
        one_copy(step).wait_send()
    for m in range(micro):
        core_copy(1, m).wait_send()
        for array in range(2):
            for part in range(2):
                for stage in range(count - 1):
                    for _, _, copy in stage_copies(array, m, part, stage):
                        copy.wait_send()


def close_layer(
    tokens, upstream, grads, attn, one, two, turned, pre, mixed, hidden, one_sum, full, bqkv, bone
):
    size, depth = lax.axis_size("seq"), lax.axis_size("fsdp")
    micro, length, width = tokens.shape
    units, cols = one.shape[-1], width // size
    rows = width // (size * depth)
    dims = (size, depth, micro, length, width, units, cols)
    chips, count = size // 2, size.bit_length() - 1
    hbm = pl.BlockSpec(memory_space=pl.ANY)
    vmem = pl.BlockSpec(memory_space=pltpu.VMEM)
    dma = pltpu.SemaphoreType.DMA
    levels = count + depth.bit_length() - 1
    piece = (chips, rows, 4 * cols)
    loaded = (tokens, upstream, attn, one, two, turned, pre, mixed, hidden)
    return pl.pallas_call(
        functools.partial(close_kernel, dims),
        in_specs=[hbm] * 11 + [vmem] * 3,
        out_specs=[vmem] * 5 + [hbm] * 2,
        out_shape=[
            jax.ShapeDtypeStruct(tokens.shape, BF),
            jax.ShapeDtypeStruct(tokens.shape, F32),
            jax.ShapeDtypeStruct((rows, 3 * width), F32),
            jax.ShapeDtypeStruct((rows, width), F32),
            jax.ShapeDtypeStruct(full.shape, F32),
            jax.ShapeDtypeStruct((rows, size * units), F32),
            jax.ShapeDtypeStruct((4 * depth,) + piece, BF),
        ],
        scratch_shapes=[pltpu.VMEM(v.shape, BF) for v in loaded]
        + [
            pltpu.VMEM((micro, chips, length, width), BF),
            pltpu.VMEM((2 * micro, chips, length, width), BF),
            pltpu.VMEM((2 * micro, chips - 1, length, width), BF),
            pltpu.VMEM((1,) + piece, BF),
            pltpu.VMEM((2,) + piece, BF),
            pltpu.VMEM((4,) + piece, BF),
            pltpu.VMEM((size, rows, 4 * cols), BF),
            pltpu.VMEM((size, rows, 3 * cols), BF),
            pltpu.VMEM(one_sum.shape, BF),
            pltpu.VMEM((2,) + one_sum.shape[1:], F32),
            pltpu.VMEM((levels,) + full.shape, F32),
            dma((9,)),
            dma((2 * micro,)),
            dma((2 * micro,)),
            dma((4 * micro * (chips - 1),)),
            dma((4 * micro * (chips - 1),)),
            dma((2,)),
            dma((4 * depth,)),
            dma((4 * depth,)),
            dma((size,)),
            dma((size,)),
            dma((levels,)),
            dma((levels,)),
            dma((size,)),
            dma((size,)),
            dma((2,)),
        ],
        compiler_params=pltpu.CompilerParams(
            collective_id=4, has_side_effects=True, vmem_limit_bytes=60 * 1024 * 1024
        ),
        cost_estimate=pl.CostEstimate(
            flops=30 * 1000**3, bytes_accessed=300 * 1000 * 1000, transcendentals=0
        ),
    )(
        tokens,
        upstream,
        grads,
        attn,
        one,
        two,
        turned,
        pre,
        mixed,
        hidden,
        one_sum,
        full,
        bqkv,
        bone,
    )[:6]


def gelu_tanh(values):
    return jax.nn.gelu(values, approximate=True)


def layer_norm(values, gain, shift):
    center = values - jnp.mean(values, axis=-1, keepdims=True)
    spread = jnp.mean(center * center, axis=-1, keepdims=True)
    return center * lax.rsqrt(spread + EPSILON) * gain + shift


def fence(*values):
    return lax.optimization_barrier(values)


def line_right(value, senders):
    return lax.ppermute(value, "fsdp", [(i, i + 1) for i in senders])


def line_left(value, senders):
    last = lax.axis_size("fsdp") - 1
    return lax.ppermute(value, "fsdp", [(last - i, last - i - 1) for i in senders])


class Gather:
    def __init__(self, mine):
        self.right, self.left = [mine], [mine]

    def step(self):
        size = lax.axis_size("fsdp")
        number = len(self.right)
        if number < size:
            self.right.append(line_right(self.right[-1], range(number - 1, size - 1)))
            self.left.append(line_left(self.left[-1], range(number - 1, size - 1)))

    def fence(self, *others):
        (self.right[-1], self.left[-1]), *others = fence((self.right[-1], self.left[-1]), *others)
        return others

    def rest(self):
        while len(self.right) < lax.axis_size("fsdp"):
            self.step()

    def pieces(self):
        size = lax.axis_size("fsdp")
        at = lax.axis_index("fsdp")
        found = [(self.right[0], at)]
        for step in range(1, size):
            piece = jnp.where(at >= step, self.right[step], self.left[size - step])
            found.append((piece, lax.rem(at - step + size, size)))
        return found


class Scatter:
    def __init__(self, chunk):
        self.chunk = chunk
        self.number = 0
        self.right = self.left = None

    def step(self):
        size = lax.axis_size("fsdp")
        at = lax.axis_index("fsdp")
        if self.number == size - 1:
            return
        self.number += 1
        going = self.chunk(jnp.minimum(size - self.number + at, size - 1))
        coming = self.chunk(jnp.maximum(self.number - size + at, 0))
        if self.number > 1:
            going = (going.astype(F32) + self.right.astype(F32)).astype(BF)
            coming = (coming.astype(F32) + self.left.astype(F32)).astype(BF)
        self.right = line_right(going, range(self.number))
        self.left = line_left(coming, range(self.number))

    def rest(self):
        while self.number < lax.axis_size("fsdp") - 1:
            self.step()

    def fence(self, *others):
        (self.right, self.left), *others = fence((self.right, self.left), *others)
        return others

    def total(self):
        mine = self.chunk(lax.axis_index("fsdp")).astype(F32)
        return mine + self.right.astype(F32) + self.left.astype(F32)


def staged_layer(
    tokens, upstream, w_fc2, starts, normed, up, my_one, two_near, attn_cols, full, index
):
    size, depth = lax.axis_size("seq"), lax.axis_size("fsdp")
    me = lax.axis_index("seq")
    micro, length, width = tokens.shape
    rows = width // (size * depth)
    hidden_rows = w_fc2.shape[0]
    cols = width // size
    units = hidden_rows * depth
    count = micro * size * length

    def contract_last(left, right):
        return lax.dot_general(left, right, (((1,), (1,)), ((), ())), preferred_element_type=F32)

    def contract_first(left, right):
        return lax.dot_general(left, right, (((0,), (0,)), ((), ())), preferred_element_type=F32)

    def place_columns(pieces):
        out = jnp.zeros((size, depth) + pieces[0][0].shape[1:], BF)
        for piece, origin in pieces:
            out = lax.dynamic_update_slice_in_dim(out, piece[:, None], origin, 1)
        return out

    def place_rows(pieces):
        out = jnp.zeros((depth,) + pieces[0][0].shape, BF)
        for piece, origin in pieces:
            out = lax.dynamic_update_slice_in_dim(out, piece[None], origin, 0)
        return out

    normed = normed.reshape(count, width)
    up = up.reshape(count, width)
    my_one = my_one.reshape(width, units)
    two = Gather(w_fc2)
    at = lax.axis_index("fsdp")
    for way, found in ((-1, two.right), (1, two.left)):
        origin = jnp.clip(at + way, 0, depth - 1)
        found.append(lax.dynamic_index_in_dim(two_near, origin, 0, keepdims=False))
    gain, shift, bias_out = full[0], full[1], full[5]
    bias_qkv = lax.dynamic_slice_in_dim(full[2:5], me * cols, cols, 1).reshape(-1)
    ratio = size * units // width
    bias_one = lax.dynamic_slice_in_dim(full[6 : 6 + ratio].reshape(-1), me * units, units, 0)
    bias_two = full[6 + ratio]
    two.step()
    pre = jnp.dot(normed, my_one, preferred_element_type=F32) + bias_one
    hidden, back = jax.vjp(gelu_tanh, pre)
    hidden = hidden.astype(BF)
    grad_two = contract_first(hidden, up).astype(BF).reshape(depth, hidden_rows, width)
    hidden, grad_two = two.fence(hidden, grad_two)
    two.step()
    sum_two = Scatter(lambda o: lax.dynamic_index_in_dim(grad_two, o, 0, keepdims=False))
    sum_two.step()
    (two.right, two.left), (sum_two.right, sum_two.left), attn_cols = fence(
        (two.right, two.left), (sum_two.right, sum_two.left), attn_cols
    )
    attn = Gather(attn_cols)
    attn.step()
    two.rest()
    my_two = place_rows(two.pieces()).reshape(units, width)
    pre_grad = back(contract_last(up, my_two))[0].astype(BF)
    grad_one = contract_first(normed, pre_grad).astype(BF).reshape(size, depth, rows, units)
    pre_grad, grad_one = attn.fence(pre_grad, grad_one)
    attn.step()
    sum_one = Scatter(lambda o: lax.dynamic_index_in_dim(grad_one, o, 1, keepdims=False))
    sum_one.step()
    (sum_one.right, sum_one.left), (sum_two.right, sum_two.left) = attn.fence(
        (sum_one.right, sum_one.left), (sum_two.right, sum_two.left)
    )
    attn.step()
    sum_two.step()
    (sum_two.right, sum_two.left), normed, up = attn.fence(
        (sum_two.right, sum_two.left), normed, up
    )
    sum_two.step()
    attn.rest()
    attn_weights = place_columns(attn.pieces())
    my_qkv = attn_weights[..., : 3 * cols].reshape(width, 3 * cols)
    my_out = attn_weights[..., 3 * cols :].transpose(1, 2, 0, 3).reshape(cols, width)
    projected = jnp.dot(normed, my_qkv, preferred_element_type=F32) + bias_qkv
    projected = projected.reshape(micro, size, length, 3 * cols)
    mixed_grad = contract_last(up, my_out).astype(BF).reshape(micro, size, length, cols)
    parts = [attention(starts[:1], projected[:1], mixed_grad[:1])]
    (sum_one.right, sum_one.left), (projected, mixed_grad), parts = sum_two.fence(
        (sum_one.right, sum_one.left), (projected, mixed_grad), parts
    )
    sum_one.step()
    for m in range(1, micro):
        parts.append(attention(starts[m:][:1], projected[m:][:1], mixed_grad[m:][:1]))
    mixed = jnp.concatenate([part[0] for part in parts]).reshape(count, cols)
    projected_grad = jnp.concatenate(
        [jnp.concatenate(part[1:], axis=-1) for part in parts]
    ).reshape(count, 3 * cols)
    projected_grad, mixed = sum_one.fence(projected_grad, mixed)
    sum_one.step()
    grad_qkv = contract_first(normed, projected_grad).astype(BF).reshape(size, depth, rows, 3 * cols)
    grad_out = contract_first(mixed, up).astype(BF).reshape(depth, rows, size, cols)
    grad_qkv, grad_out, (sum_two.right, sum_two.left) = sum_one.fence(
        grad_qkv, grad_out, (sum_two.right, sum_two.left)
    )
    grad_attn = jnp.concatenate([grad_qkv, grad_out.transpose(2, 0, 1, 3)], axis=-1)

    def to_rows(mine, parts):
        mine = lax.all_to_all(mine.astype(BF), "seq", 0, 0, tiled=True).astype(F32)
        return mine.reshape(size, rows, parts, -1).transpose(1, 2, 0, 3).reshape(rows, -1)

    sum_one.rest()
    sum_two.rest()
    out_two = sum_two.total()
    out_one = to_rows(sum_one.total(), 1)

    def put(values, extent, at):
        return lax.dynamic_update_slice_in_dim(jnp.zeros(extent, F32), values, at, -1)

    bqkv = jnp.sum(projected_grad.astype(F32), axis=0).reshape(3, cols)
    bqkv = put(bqkv, (3, width), me * cols)
    bone = put(jnp.sum(pre_grad.astype(F32), axis=0), (size * units,), me * units)
    btwo = jnp.sum(upstream.astype(F32), axis=(0, 1))[None]
    early = [jnp.zeros((2, width), F32), bqkv, btwo, bone.reshape(ratio, width)]
    early = jnp.pad(jnp.concatenate(early), ((0, full.shape[0] - 6 - ratio), (0, 0)))

    sum_attn = Scatter(lambda o: lax.dynamic_index_in_dim(grad_attn, o, 1, keepdims=False))
    sum_attn.step()
    grad_terms = contract_last(projected_grad, my_qkv) + contract_last(pre_grad, my_one)
    grad_terms = grad_terms.astype(BF).reshape(micro, size, length, width)
    (grad_terms,) = sum_attn.fence(grad_terms)
    sum_attn.step()
    normed_grad = scatter_seq(grad_terms)
    terms = jnp.dot(mixed, my_out, preferred_element_type=F32)
    terms = terms + jnp.dot(hidden, my_two, preferred_element_type=F32)
    terms = terms.astype(BF).reshape(micro, size, length, width)
    sums = scatter_seq(terms)
    sum_attn.rest()
    attn_total = sum_attn.total()
    out_qkv = to_rows(attn_total[..., : 3 * cols], 3)
    out_out = attn_total[..., 3 * cols :].transpose(1, 0, 2).reshape(rows, width)
    activations = (tokens.astype(F32) + sums + (bias_out + bias_two)).astype(BF)
    _, norm_back = jax.vjp(layer_norm, tokens.astype(F32), gain, shift)
    input_grad, gain_grad, shift_grad = norm_back(normed_grad)
    input_grad = input_grad + upstream.astype(F32)
    vectors = early.at[:2].add(jnp.stack([gain_grad, shift_grad]))
    vectors = lax.psum(vectors, ("seq", "fsdp"))

    return activations, input_grad, out_qkv, out_out, vectors, out_one, out_two


def per_device(
    tokens,
    ln_gain,
    ln_bias,
    w_qkv,
    b_qkv,
    w_out,
    b_out,
    w_fc1,
    b_fc1,
    w_fc2,
    b_fc2,
    piece_starts,
    cotangent,
):
    size, depth = lax.axis_size("seq"), lax.axis_size("fsdp")
    me = lax.axis_index("seq")
    micro, _, length, width = tokens.shape
    rows = width // (size * depth)
    hidden_rows = w_fc2.shape[0]
    cols = width // size
    units = hidden_rows * depth
    count = micro * size * length
    tokens = tokens[:, 0]
    upstream = cotangent[:, 0]

    index = me * depth + lax.axis_index("fsdp")
    packed = []
    for vector in (ln_gain, ln_bias, b_qkv, b_out, b_fc1, b_fc2):
        extent = vector.shape[0]
        flat = jnp.zeros((extent * size * depth,), BF)
        flat = lax.dynamic_update_slice(flat, vector, (index * extent,))
        packed.append(flat.reshape(-1, width))
    packed = jnp.concatenate(packed, axis=0)
    packed = jnp.pad(packed, ((0, -packed.shape[0] % 16), (0, 0)))
    starts = piece_starts[:, 0]
    loaded = load_all(tokens, upstream, w_fc1, w_fc2, w_qkv, w_out, packed)
    if (size, depth, micro) == (8, 4, 2):
        normed, up, one, two_near, attn_cols, full = loaded
        hidden, pre, two, attn, grad_two, grad_one, land_two, land_one, bone = feed_forward(
            normed, up, one, two_near, attn_cols, full
        )
        turned, mixed, grads, one_sum, _, _, bqkv, out_two = attention_layer(
            starts, normed, up, attn, grad_two, grad_one, land_two, land_one, full
        )
        wide = (micro, size, length, -1)
        activations, input_grad, out_qkv, out_out, vectors, out_one = close_layer(
            tokens,
            upstream,
            grads,
            attn,
            one,
            two,
            turned.reshape(wide),
            pre.reshape(wide),
            mixed.reshape(wide),
            hidden.reshape(wide),
            one_sum,
            full,
            bqkv,
            bone,
        )
    else:
        activations, input_grad, out_qkv, out_out, vectors, out_one, out_two = staged_layer(
            tokens, upstream, w_fc2, starts, *loaded, index
        )
    ratio = w_fc1.shape[1] // width

    def own(values):
        values = values.reshape(-1)
        extent = values.shape[0] // (size * depth)
        return lax.dynamic_slice_in_dim(values, index * extent, extent, 0)

    grad_b_two = own(vectors[5])
    return (
        activations[:, None],
        input_grad[:, None],
        own(vectors[0]),
        own(vectors[1]),
        out_qkv,
        own(vectors[2:4]),
        own(vectors[4]),
        out_out,
        grad_b_two,
        out_one,
        own(vectors[6 : 6 + ratio]),
        out_two,
        grad_b_two,
    )


def solution(mesh):
    both = ("seq", "fsdp")
    row = P(both)
    matrix = P(both, None)
    tokens = P(None, "fsdp", "seq", None)
    weights = (row, row, matrix, row, matrix, row, matrix, row, matrix, row)
    grads = (row, row, matrix, row, row, matrix, row, matrix, row, matrix, row)
    return jax.shard_map(
        per_device,
        mesh=mesh,
        in_specs=(tokens,) + weights + (P(None, "fsdp", None), tokens),
        out_specs=(tokens, tokens) + grads,
        check_vma=False,
    )
```

```python
import functools
import math

import jax
import jax.numpy as jnp
import numpy as np
from jax import lax
from jax.experimental import pallas as pl
from jax.experimental.pallas import tpu as pltpu
from jax.sharding import PartitionSpec as P

HEADS = 32
HEAD_DIM = 64
ROT = 32
IMG = 256
PIECES = 2
EPSILON = 1e-05
BF = jnp.bfloat16
F32 = jnp.float32
SCALE = 1.0 / math.sqrt(HEAD_DIM)
LANES = 2 * HEAD_DIM


def swap(value, bit):
    size = lax.axis_size("seq")
    return lax.ppermute(value, "seq", [(i, i ^ bit) for i in range(size)])


def store_index(block):
    half = lax.axis_size("seq") // 2
    if isinstance(block, int):
        return block % 2 * half + block // 2
    return (block & 1) * half + (block >> 1)


def scatter_seq(terms):
    size = lax.axis_size("seq")
    me = lax.axis_index("seq")
    count = size.bit_length() - 1
    micro, _, length, width = terms.shape
    half = width // 2
    bits = list(range(1, count))

    def exchange(held, bit, axis):
        held = held.astype(BF)
        mine = (me >> bit) & 1
        away = lax.dynamic_index_in_dim(held, 1 - mine, axis, keepdims=False)
        kept = lax.dynamic_index_in_dim(held, mine, axis, keepdims=False)
        return kept.astype(F32) + swap(away, 1 << bit).astype(F32)

    sums = []
    for cols, order in ((slice(0, half), bits), (slice(half, width), bits[::-1])):
        held = terms[..., cols].reshape((micro,) + (2,) * count + (length, half))
        left = [0] + bits[::-1]
        for bit in [0] + order:
            held = exchange(held, bit, 1 + left.index(bit))
            left.remove(bit)
        sums.append(held)
    return jnp.concatenate(sums, axis=-1)


def attention_kernel(
    blocks,
    length,
    starts_ref,
    cos_ref,
    sin_ref,
    q_ref,
    k_ref,
    v_ref,
    do_ref,
    mixed_ref,
    dq_ref,
    dk_ref,
    dv_ref,
    q_s,
    k_s,
    v_s,
    do_s,
    dk_s,
    dv_s,
    bias_s,
):
    micro = pl.program_id(0)
    total = blocks * length
    tile = 256
    lane = lax.broadcasted_iota(jnp.int32, (1, LANES), 1)
    low_lane = (lane % HEAD_DIM) < (ROT // 2)

    def turn(value, cosine, sine):
        other = jnp.where(
            low_lane,
            pltpu.roll(value, LANES - ROT // 2, 1),
            pltpu.roll(value, ROT // 2, 1),
        )
        return value * cosine + other * sine

    for block in range(blocks):
        source = store_index(block)
        at = slice(block * length, (block + 1) * length)
        cosine, sine = cos_ref[at, :], sin_ref[at, :]
        q_s[at, :] = (turn(q_ref[0, source], cosine, sine)).astype(BF) * jnp.asarray(SCALE, BF)
        k_s[at, :] = turn(k_ref[0, source], cosine, sine).astype(BF)
        v_s[at, :] = v_ref[0, source].astype(BF)
        do_s[at, :] = do_ref[0, source]
    dk_s[...] = jnp.zeros_like(dk_s)
    dv_s[...] = jnp.zeros_like(dv_s)

    def label(positions):
        found = jnp.full(positions.shape, -1, jnp.int32)
        for piece in range(PIECES):
            start = starts_ref[micro, piece]
            found = jnp.where((positions >= start) & (positions < start + IMG), piece, found)
        return found

    for first in range(0, total, tile):
        last = min(total, first + tile + IMG)
        qpos = first + lax.broadcasted_iota(jnp.int32, (tile, 1), 0)
        kpos = first + lax.broadcasted_iota(jnp.int32, (1, last - first), 1)
        qlab, klab = label(qpos), label(kpos)
        allowed = (kpos <= qpos) | ((qlab == klab) & (qlab >= 0))
        bias_s[:, : last - first] = jnp.where(allowed, 0.0, -1e30)
        rows = slice(first, first + tile)
        keys = k_s[:last, :]
        values = v_s[:last, :]
        mixed = jnp.zeros((tile, LANES), F32)
        dq = jnp.zeros((tile, LANES), F32)
        for head in range(LANES // HEAD_DIM):
            mine = (lane // HEAD_DIM) == head
            q = jnp.where(mine, q_s[rows, :], 0)
            do = jnp.where(mine, do_s[rows, :], 0)
            dims = (((1,), (1,)), ((), ()))
            s = lax.dot_general(q, keys, dims, preferred_element_type=F32)
            if first:
                s = jnp.concatenate(
                    [s[:, :first], s[:, first:] + bias_s[:, : last - first]], axis=1
                )
            else:
                s = s + bias_s[:, : last - first]
            p = jnp.exp(s - jnp.max(s, axis=1, keepdims=True))
            p = p * (1.0 / jnp.sum(p, axis=1, keepdims=True))
            probs = p.astype(BF)
            att = jnp.dot(probs, values, preferred_element_type=F32)
            mixed = jnp.where(mine, att, mixed)
            dp = lax.dot_general(do, values, dims, preferred_element_type=F32)
            delta = jnp.sum(p * dp, axis=1, keepdims=True)
            ds = (p * (dp - delta)).astype(BF)
            dq = jnp.where(mine, jnp.dot(ds, keys, preferred_element_type=F32), dq)
            over = (((0,), (0,)), ((), ()))
            dk_s[:last, :] += lax.dot_general(ds, q, over, preferred_element_type=F32)
            dv_s[:last, :] += lax.dot_general(probs, do, over, preferred_element_type=F32)
        dq = dq * SCALE
        for part in range(tile // length):
            block = first // length + part
            here = slice(part * length, (part + 1) * length)
            at = slice(block * length, (block + 1) * length)
            mixed_ref[0, store_index(block)] = mixed[here].astype(BF)
            dq_ref[0, store_index(block)] = turn(dq[here], cos_ref[at, :], -sin_ref[at, :]).astype(BF)
    for block in range(blocks):
        at = slice(block * length, (block + 1) * length)
        dk_ref[0, store_index(block)] = turn(dk_s[at, :], cos_ref[at, :], -sin_ref[at, :]).astype(BF)
        dv_ref[0, store_index(block)] = dv_s[at, :].astype(BF)


def tables(total):
    half = ROT // 2
    frequency = (10000.0 ** (-2.0 * np.arange(half) / ROT)).astype(np.float32)
    angles = np.arange(total, dtype=np.float32)[:, None] * frequency[None, :]
    cosine, sine = np.cos(angles), np.sin(angles)
    ones = np.ones((total, HEAD_DIM - ROT), np.float32)
    cosine = np.concatenate([cosine, cosine, ones] * 2, axis=1)
    sine = np.concatenate([-sine, sine, 0 * ones] * 2, axis=1)
    return jnp.asarray(cosine), jnp.asarray(sine)


def attention(starts, projected, mixed_grad):
    micro, blocks, length, cols = mixed_grad.shape
    total = blocks * length
    groups = cols // LANES
    cosine, sine = tables(total)

    def spec(offset):
        return pl.BlockSpec(
            (1, blocks, length, LANES), lambda m, g, offset=offset: (m, 0, 0, offset * groups + g)
        )

    table = pl.BlockSpec((total, LANES), lambda m, g: (0, 0))
    shape = jax.ShapeDtypeStruct(mixed_grad.shape, BF)
    return pl.pallas_call(
        functools.partial(attention_kernel, blocks, length),
        grid=(micro, groups),
        in_specs=[
            pl.BlockSpec(memory_space=pltpu.SMEM),
            table,
            table,
            spec(0),
            spec(1),
            spec(2),
            spec(0),
        ],
        out_specs=[spec(0)] * 4,
        out_shape=[shape] * 4,
        scratch_shapes=[pltpu.VMEM((total, LANES), BF)] * 4
        + [pltpu.VMEM((total, LANES), F32)] * 2
        + [pltpu.VMEM((256, 512), F32)],
        compiler_params=pltpu.CompilerParams(vmem_limit_bytes=48 * 1024 * 1024),
        cost_estimate=pl.CostEstimate(
            flops=micro * groups * 40 * total * total * HEAD_DIM,
            bytes_accessed=micro * groups * total * LANES * 22,
            transcendentals=micro * groups * 2 * total * total,
        ),
    )(starts, cosine, sine, projected, projected, projected, mixed_grad)


MESH = pl.DeviceIdType.MESH


def remote(src, dst, send, recv, device):
    return pltpu.make_async_remote_copy(
        src_ref=src,
        dst_ref=dst,
        send_sem=send,
        recv_sem=recv,
        device_id=device,
        device_id_type=MESH,
    )


def greet(size, depth):
    me, at = lax.axis_index("seq"), lax.axis_index("fsdp")
    barrier = pltpu.get_barrier_semaphore()
    for step in range(1, size):
        pl.semaphore_signal(barrier, inc=1, device_id={"seq": me ^ step}, device_id_type=MESH)
    for step in range(1, depth):
        pl.semaphore_signal(
            barrier, inc=1, device_id={"fsdp": lax.rem(at + step, depth)}, device_id_type=MESH
        )
    pl.semaphore_wait(barrier, size + depth - 2)


class LineGather:
    def __init__(self, depth, source, target, send, recv):
        self.depth, self.source, self.target = depth, source, target
        self.send, self.recv = send, recv

    def copy(self, step, way):
        at = lax.axis_index("fsdp")
        origin = jnp.clip(at - way * (step - 1), 0, self.depth - 1)
        number = step * 2 + (way > 0)
        return remote(
            self.source(origin, step),
            self.target(origin),
            self.send.at[number],
            self.recv.at[number],
            {"fsdp": jnp.clip(at + way, 0, self.depth - 1)},
        )

    def sends(self, step, way):
        at = lax.axis_index("fsdp")
        origin = at - way * (step - 1)
        return (at + way >= 0) & (at + way < self.depth) & (origin >= 0) & (origin < self.depth)

    def start(self, step):
        for way in (1, -1):

            @pl.when(self.sends(step, way))
            def _():
                self.copy(step, way).start()

    def arrive(self, step):
        at = lax.axis_index("fsdp")
        for way in (1, -1):
            origin = at - way * step

            @pl.when((origin >= 0) & (origin < self.depth))
            def _():
                self.copy(step, way).wait_recv()

    def sent(self, step):
        for way in (1, -1):

            @pl.when(self.sends(step, way))
            def _():
                self.copy(step, way).wait_send()


class LineSum:
    def __init__(self, depth, chunk, landing, own, held, out, load, send, recv):
        self.depth, self.chunk, self.landing = depth, chunk, landing
        self.own, self.held, self.out = own, held, out
        self.load, self.send, self.recv = load, send, recv

    def place(self, way):
        at = lax.axis_index("fsdp")
        return at if way > 0 else self.depth - 1 - at

    def copy(self, step, way, src):
        number = step * 2 + (way > 0)
        at = lax.axis_index("fsdp")
        return remote(
            src,
            self.landing(step, way),
            self.send.at[number],
            self.recv.at[number],
            {"fsdp": jnp.clip(at + way, 0, self.depth - 1)},
        )

    def origin(self, step, way):
        away = jnp.clip(self.depth - step + self.place(way), 0, self.depth - 1)
        return away if way > 0 else self.depth - 1 - away

    def source(self, step):
        for way in (1, -1):

            @pl.when(self.place(way) == 0)
            def _():
                self.copy(step, way, self.chunk(self.origin(step, way))).start()

    def forward(self, step, here=True):
        for way in (1, -1):
            place = self.place(way)

            @pl.when((place >= 1) & (place <= step - 1) & (place < self.depth - 1))
            def _():
                mine = pltpu.make_async_copy(
                    self.chunk(self.origin(step, way)), self.own, self.load.at[0]
                )
                mine.start()
                if here:
                    self.copy(step - 1, way, self.out(step, way)).wait_recv()
                came = pltpu.make_async_copy(
                    self.landing(step - 1, way), self.held, self.load.at[1]
                )
                came.start()
                mine.wait()
                came.wait()
                target = self.out(step, way)
                target[...] = (self.own[...].astype(F32) + self.held[...].astype(F32)).astype(BF)
                self.copy(step, way, target).start()

    def arrive(self, step, consumed):
        for way in (1, -1):
            place = self.place(way)
            ok = (place >= 1) & (place <= step)
            if consumed:
                ok = ok & (place == self.depth - 1)

            @pl.when(ok)
            def _():
                self.copy(step, way, self.out(step, way)).wait_recv()

    def total(self, last, right, left):
        mine = pltpu.make_async_copy(self.chunk(lax.axis_index("fsdp")), self.own, self.load.at[0])
        mine.start()
        for way, target in ((1, right), (-1, left)):
            place = self.place(way)

            @pl.when(place >= 1)
            def _():
                self.copy(last, way, self.out(last, way)).wait_recv()
                came = pltpu.make_async_copy(self.landing(last, way), target, self.load.at[1])
                came.start()
                came.wait()

            @pl.when(place == 0)
            def _():
                target[...] = jnp.zeros_like(target)

        mine.wait()
        return self.own[...].astype(F32) + right[...].astype(F32) + left[...].astype(F32)

    def sent_first(self, step):
        for way in (1, -1):

            @pl.when(self.place(way) == 0)
            def _():
                self.copy(step, way, self.out(step, way)).wait_send()

    def sent_on(self, step):
        for way in (1, -1):
            place = self.place(way)

            @pl.when((place >= 1) & (place <= step - 1) & (place < self.depth - 1))
            def _():
                self.copy(step, way, self.out(step, way)).wait_send()

    def sent(self, step):
        self.sent_first(step)
        self.sent_on(step)


class SeqSum:
    def __init__(self, size, width, to_core, sums, coming, core_sems, axis_sems, base):
        self.size, self.width = size, width
        self.to_core, self.sums, self.coming = to_core, sums, coming
        self.core_sems, self.axis_sems, self.base = core_sems, axis_sems, base
        self.chips = size // 2
        self.bits = size.bit_length() - 2
        bits = list(range(self.bits))
        self.orders = (bits, bits[::-1])

    def core_copy(self):
        me = lax.axis_index("seq")
        send, recv = self.core_sems
        return remote(self.to_core, self.sums, send, recv, {"seq": me ^ 1})

    def away(self, terms):
        def write(columns, y):
            self.to_core[:, :, columns] = y.astype(BF)

        terms(1 - (lax.axis_index("seq") & 1), write)
        self.core_copy().start()

    def here(self, terms):
        self.core_copy().wait_recv()

        def write(columns, y):
            self.sums[:, :, columns] = (y + self.sums[:, :, columns].astype(F32)).astype(BF)

        terms(lax.axis_index("seq") & 1, write)
        self.start(0)

    def copies(self, part, stage):
        me = lax.axis_index("seq")
        half = self.width // 2
        bit = self.orders[part][stage]
        done = sum(1 << b for b in self.orders[part][:stage])
        first = self.chips - (self.chips >> stage)
        columns = slice(part * half, (part + 1) * half)
        send, recv = self.axis_sems
        found = []
        for mask in range(self.chips):
            if mask & (done | (1 << bit)):
                continue
            slot = first + len(found)
            number = self.base + part * (self.chips - 1) + slot
            copy = remote(
                self.sums.at[(me >> 1) ^ (mask | (1 << bit)), :, columns],
                self.coming.at[slot, :, columns],
                send.at[number],
                recv.at[number],
                {"seq": me ^ (2 << bit)},
            )
            found.append((mask, slot, copy))
        return found

    def start(self, stage):
        for part in range(2):
            for _, _, copy in self.copies(part, stage):
                copy.start()

    def add(self, stage):
        half = self.width // 2
        for part in range(2):
            columns = slice(part * half, (part + 1) * half)
            for mask, slot, copy in self.copies(part, stage):
                copy.wait_recv()
                if stage < self.bits - 1:
                    block = (lax.axis_index("seq") >> 1) ^ mask
                    self.sums[block, :, columns] = (
                        self.sums[block, :, columns].astype(F32)
                        + self.coming[slot, :, columns].astype(F32)
                    ).astype(BF)

    def step(self, stage):
        self.add(stage)
        if stage + 1 < self.bits:
            self.start(stage + 1)

    def last(self):
        chip = lax.axis_index("seq") >> 1
        return self.sums[chip].astype(F32) + self.coming[self.chips - 2].astype(F32)

    def core_sent(self):
        self.core_copy().wait_send()

    def sent(self):
        for part in range(2):
            for stage in range(self.bits):
                for _, _, copy in self.copies(part, stage):
                    copy.wait_send()


def load_kernel(
    dims,
    tokens_ref,
    up_ref,
    one_ref,
    two_ref,
    vec_ref,
    normed_ref,
    all_up_ref,
    my_one_ref,
    my_two_ref,
    full_ref,
    gathered,
    normed_v,
    vec_seq,
    vec_sum,
    vec_all,
    local_sem,
    vec_send,
    vec_recv,
    a2a_send,
    a2a_recv,
    line_send,
    line_recv,
    row_send,
    row_recv,
):
    size, depth, micro, length, width, units, cols = dims
    me, at = lax.axis_index("seq"), lax.axis_index("fsdp")
    count = size.bit_length() - 1
    half = width // 2

    def seq(step):
        return {"seq": me ^ step}

    def line(step):
        return {"fsdp": lax.rem(at + step, depth)}

    greet(size, depth)

    def vec_seq_copy(step):
        return remote(
            vec_sum.at[step],
            vec_seq.at[step],
            vec_send.at[step],
            vec_recv.at[step],
            seq(1 << step),
        )

    def vec_line_copy(step):
        number = size + step
        return remote(
            vec_sum.at[count], vec_all.at[step], vec_send.at[number], vec_recv.at[number], line(step)
        )

    def one_copy(step):
        peer = me ^ step
        return remote(
            one_ref.at[:, pl.ds(pl.multiple_of(peer * units, 128), units)],
            my_one_ref.at[me, at],
            a2a_send.at[step],
            a2a_recv.at[step],
            seq(step),
        )

    local = [
        pltpu.make_async_copy(
            one_ref.at[:, pl.ds(pl.multiple_of(me * units, 128), units)],
            my_one_ref.at[me, at],
            local_sem.at[0],
        ),
        pltpu.make_async_copy(
            tokens_ref,
            gathered.at[:, store_index(me)],
            local_sem.at[1],
        ),
        pltpu.make_async_copy(
            up_ref,
            all_up_ref.at[:, store_index(me)],
            local_sem.at[2],
        ),
    ]
    local.append(pltpu.make_async_copy(two_ref, my_two_ref.at[at], local_sem.at[3]))

    def one_line(step, way):
        origin = jnp.clip(at - way * (step - 1), 0, depth - 1)
        number = 2 * step + (way > 0)
        piece = my_one_ref.at[:, origin]
        ok = (at + way >= 0) & (at + way < depth)
        ok = ok & (at - way * (step - 1) >= 0) & (at - way * (step - 1) < depth)
        return ok, remote(
            piece,
            piece,
            line_send.at[number],
            line_recv.at[number],
            {"fsdp": jnp.clip(at + way, 0, depth - 1)},
        )

    def one_arrives(step, way):
        ok = (at - way * step >= 0) & (at - way * step < depth)
        return ok, one_line(step, way)[1]

    def two_line(way):
        ok = (at + way >= 0) & (at + way < depth)
        number = way > 0
        return ok, remote(
            two_ref,
            my_two_ref.at[at],
            line_send.at[int(number)],
            line_recv.at[int(number)],
            {"fsdp": jnp.clip(at + way, 0, depth - 1)},
        )

    def two_arrives(way):
        return (at - way >= 0) & (at - way < depth), two_line(way)[1]

    def start(pair):
        ok, copy = pair

        @pl.when(ok)
        def _():
            copy.start()

    def wait_recv(pair):
        ok, copy = pair

        @pl.when(ok)
        def _():
            copy.wait_recv()

    def wait_send(pair):
        ok, copy = pair

        @pl.when(ok)
        def _():
            copy.wait_send()

    sources = (tokens_ref, up_ref)
    targets = (gathered, all_up_ref)
    orders = (list(range(1, count)), list(range(1, count))[::-1])

    def row_copy(which, part, mask, bit):
        columns = slice(part * half, (part + 1) * half)
        block = store_index(me ^ mask)
        if mask == 0:
            src = sources[which].at[:, :, columns]
        else:
            src = targets[which].at[:, block, :, columns]
        number = (which * 2 + part) * size + (mask | (1 << bit))
        return remote(
            src,
            targets[which].at[:, block, :, columns],
            row_send.at[number],
            row_recv.at[number],
            seq(1 << bit),
        )

    def row_stage(which, part, stage):
        order = orders[part]
        masks = [0]
        for bit in order[:stage]:
            masks = masks + [mask | (1 << bit) for mask in masks]
        return [row_copy(which, part, mask, order[stage]) for mask in masks]

    def row_cores(which, part, stage):
        order = orders[part]
        masks = [0]
        new = [0]
        for bit in order[: stage + 1]:
            new = [mask | (1 << bit) for mask in masks]
            masks = masks + new
        return [row_copy(which, part, mask, 0) for mask in new]

    def both_parts(function, which, stage):
        return function(which, 0, stage) + function(which, 1, stage)

    def issue(copies):
        for copy in copies:
            copy.start()

    def arrive(copies):
        for copy in copies:
            copy.wait_recv()

    def vec_stage(step):
        vec_seq_copy(step).wait_recv()
        total = vec_sum[step].astype(F32) + vec_seq[step].astype(F32)
        vec_sum[step + 1] = total.astype(BF)

    issue(one_copy(step) for step in range(1, size))
    for way in (1, -1):
        start(two_line(way))
    issue(local)
    vec_sum[0] = vec_ref[...]
    vec_seq_copy(0).start()
    issue(both_parts(row_cores, 0, -1))
    vec_stage(0)
    vec_seq_copy(1).start()
    arrive(one_copy(step) for step in range(1, size))
    local[0].wait()
    for way in (1, -1):
        start(one_line(1, way))
    for step in range(1, count):
        vec_stage(step)
        if step + 1 < count:
            vec_seq_copy(step + 1).start()
    issue(both_parts(row_stage, 0, 0))
    issue(vec_line_copy(step) for step in range(1, depth))

    def line_on(step):
        for way in (1, -1):
            wait_recv(one_arrives(step, way))
            start(one_line(step + 1, way))

    events = [(which, stage) for which in range(2) for stage in range(count - 1)]
    line_step = 1
    for number, (which, stage) in enumerate(events):
        arrive(both_parts(row_stage, which, stage))
        if number + 1 < len(events):
            issue(both_parts(row_stage, *events[number + 1]))
        issue(both_parts(row_cores, which, stage))
        if number == 0:
            issue(both_parts(row_cores, 1, -1))
            arrive(vec_line_copy(step) for step in range(1, depth))
            summed = vec_sum[count].astype(F32)
            for step in range(1, depth):
                summed = summed + vec_all[step].astype(F32)
            full_ref[...] = summed
        if line_step < depth - 1:
            line_on(line_step)
            line_step += 1
        if number == len(events) - 2:
            while line_step < depth - 1:
                line_on(line_step)
                line_step += 1
            local[1].wait()
            for step in range(-1, count - 1):
                arrive(both_parts(row_cores, 0, step))
            gain = full_ref[0:1, :]
            shift = full_ref[1:2, :]

            @pl.loop(0, micro * size)
            def _(index):
                m, block = index // size, lax.rem(index, size)
                x = gathered[m, block].astype(F32)
                center = x - jnp.mean(x, axis=-1, keepdims=True)
                spread = jnp.mean(center * center, axis=-1, keepdims=True)
                y = center * lax.rsqrt(spread + EPSILON) * gain + shift
                normed_v[m, block] = y.astype(BF)

            normed_out = pltpu.make_async_copy(normed_v, normed_ref, local_sem.at[4])
            normed_out.start()

    for copy in local[2:]:
        copy.wait()
    normed_out.wait()
    for stage in range(-1, count - 1):
        arrive(both_parts(row_cores, 1, stage))
    for way in (1, -1):
        wait_recv(two_arrives(way))
        wait_recv(one_arrives(depth - 1, way))

    for step in range(count):
        vec_seq_copy(step).wait_send()
    for step in range(1, size):
        one_copy(step).wait_send()
    for step in range(1, depth):
        vec_line_copy(step).wait_send()
        for way in (1, -1):
            wait_send(one_line(step, way))
    for way in (1, -1):
        wait_send(two_line(way))
    for which in range(2):
        for stage in range(-1, count - 1):
            for copy in both_parts(row_cores, which, stage):
                copy.wait_send()
            if stage >= 0:
                for copy in both_parts(row_stage, which, stage):
                    copy.wait_send()


def load_all(tokens, upstream, w_fc1, w_fc2, vectors):
    size, depth = lax.axis_size("seq"), lax.axis_size("fsdp")
    micro, length, width = tokens.shape
    rows, units, cols = w_fc1.shape[0], w_fc1.shape[1] // size, width // size
    dims = (size, depth, micro, length, width, units, cols)
    hbm = pl.BlockSpec(memory_space=pl.ANY)
    vmem = pl.BlockSpec(memory_space=pltpu.VMEM)
    gathered = (micro, size, length, width)
    dma = pltpu.SemaphoreType.DMA
    return pl.pallas_call(
        functools.partial(load_kernel, dims),
        in_specs=[hbm] * 4 + [vmem],
        out_specs=[hbm] * 4 + [vmem],
        out_shape=[
            jax.ShapeDtypeStruct(gathered, BF),
            jax.ShapeDtypeStruct(gathered, BF),
            jax.ShapeDtypeStruct((size, depth, rows, units), BF),
            jax.ShapeDtypeStruct((depth,) + w_fc2.shape, BF),
            jax.ShapeDtypeStruct(vectors.shape, F32),
        ],
        scratch_shapes=[
            pltpu.VMEM(gathered, BF),
            pltpu.VMEM(gathered, BF),
            pltpu.VMEM((size,) + vectors.shape, BF),
            pltpu.VMEM((size,) + vectors.shape, BF),
            pltpu.VMEM((depth,) + vectors.shape, BF),
            dma((5,)),
            dma((size + depth,)),
            dma((size + depth,)),
            dma((size,)),
            dma((size,)),
            dma((2 * depth + 2,)),
            dma((2 * depth + 2,)),
            dma((4 * size,)),
            dma((4 * size,)),
        ],
        compiler_params=pltpu.CompilerParams(
            collective_id=1, has_side_effects=True, vmem_limit_bytes=60 * 1024 * 1024
        ),
        cost_estimate=pl.CostEstimate(
            flops=1000, bytes_accessed=300 * 1000 * 1000, transcendentals=0
        ),
    )(tokens, upstream, w_fc1, w_fc2, vectors)


def ffn_kernel(
    dims,
    normed_hbm,
    up_hbm,
    one_hbm,
    two_hbm,
    qkv_hbm,
    out_hbm,
    full_ref,
    part_grad_hbm,
    part_act_hbm,
    attn_hbm,
    grad_two_hbm,
    grad_one_hbm,
    land_two,
    land_one,
    bone_ref,
    normed_v,
    up_v,
    one_v,
    two_v,
    hidden_v,
    pre_v,
    grad_two_v,
    grad_one_v,
    own_one,
    held_one,
    out_one,
    load_sem,
    line_load,
    store_sem,
    two_send,
    two_recv,
    attn_send,
    attn_recv,
    sum_two_send,
    sum_two_recv,
    sum_one_send,
    sum_one_recv,
    a2a_send,
    a2a_recv,
    local_sem,
):
    size, depth, micro, length, width, units, cols = dims
    me, at = lax.axis_index("seq"), lax.axis_index("fsdp")
    count = micro * size * length
    per = width // size
    tile = 512
    group = units // depth

    loads = [
        pltpu.make_async_copy(src, dst, load_sem.at[n])
        for n, (src, dst) in enumerate(
            ((normed_hbm, normed_v), (one_hbm, one_v), (up_hbm, up_v))
        )
    ]
    for load in loads:
        load.start()

    def two_load(way):
        origin = jnp.clip(at + way, 0, depth - 1)
        return (at + way >= 0) & (at + way < depth), pltpu.make_async_copy(
            two_hbm.at[origin], two_v.at[origin], load_sem.at[4 + way]
        )

    for way in (0, 1, -1):
        ok, copy = two_load(way)

        @pl.when(ok)
        def _():
            copy.start()

    def qkv_part(peer, part):
        return qkv_hbm.at[:, pl.ds(pl.multiple_of(part * width + peer * cols, 128), cols)]

    def qkv_copy(step, part):
        number = part * size + step
        return remote(
            qkv_part(me ^ step, part),
            attn_hbm.at[me, at, :, pl.ds(part * cols, cols)],
            a2a_send.at[number],
            a2a_recv.at[number],
            {"seq": me ^ step},
        )

    local = [
        pltpu.make_async_copy(
            qkv_part(me, part), attn_hbm.at[me, at, :, pl.ds(part * cols, cols)], local_sem.at[part]
        )
        for part in range(3)
    ] + [
        pltpu.make_async_copy(
            out_hbm.at[:, pl.ds(peer * cols, cols)],
            attn_hbm.at[peer, at, :, pl.ds(3 * cols, cols)],
            local_sem.at[3 + peer],
        )
        for peer in range(size)
    ]
    for copy in local:
        copy.start()
    greet(size, depth)

    two = LineGather(
        depth,
        lambda o, step: two_hbm.at[o] if step == 2 else two_v.at[o],
        lambda o: two_v.at[o],
        two_send,
        two_recv,
    )
    attn = LineGather(
        depth,
        lambda o, step: attn_hbm.at[:, o],
        lambda o: attn_hbm.at[:, o],
        attn_send,
        attn_recv,
    )
    sum_two = LineSum(
        depth,
        lambda o: grad_two_v.at[o],
        lambda step, way: land_two.at[int(way > 0)],
        own_one,
        held_one,
        lambda step, way: grad_two_v.at[0],
        line_load,
        sum_two_send,
        sum_two_recv,
    )
    sum_one = LineSum(
        depth,
        lambda o: grad_one_v.at[:, o],
        lambda step, way: land_one.at[(step - 1) * 2 + (way > 0)],
        own_one,
        held_one,
        lambda step, way: out_one.at[int(way > 0)],
        line_load,
        sum_one_send,
        sum_one_recv,
    )
    two.start(2)
    for part in range(3):
        for step in range(1, size):
            qkv_copy(step, part).start()

    for load in loads[:2]:
        load.wait()
    root = math.sqrt(2.0 / math.pi)
    flat = me * units
    bias_row = 6 + flat // width
    bias_at = pl.multiple_of(lax.rem(flat, width), units)
    bias = full_ref[pl.ds(bias_row, 1), pl.ds(bias_at, units)]
    bone_ref[...] = bias

    @pl.loop(0, count // tile)
    def _(r):
        rows = pl.ds(pl.multiple_of(r * tile, tile), tile)
        a = normed_v[rows, :]
        for o in range(depth):
            columns = slice(o * group, (o + 1) * group)
            w = one_v[:, :, :, columns].reshape(width, group)
            v = jnp.dot(a, w, preferred_element_type=F32) + bone_ref[:, columns]
            square = v * v
            t = jnp.tanh(root * v * (1.0 + 0.044715 * square))
            hidden_v[rows, columns] = (0.5 * v * (1.0 + t)).astype(BF)
            slope = 0.5 * (1.0 + t) + 0.5 * root * v * (1.0 - t * t) * (
                1.0 + 3 * 0.044715 * square
            )
            pre_v[rows, columns] = slope.astype(BF)

    loads[2].wait()
    over_first = (((0,), (0,)), ((), ()))
    over_last = (((1,), (1,)), ((), ()))

    @pl.loop(0, depth)
    def _(o):
        columns = pl.ds(pl.multiple_of(o * group, group), group)
        y = lax.dot_general(hidden_v[:, columns], up_v[...], over_first, preferred_element_type=F32)
        grad_two_v[o] = y.astype(BF)

    two.arrive(2)
    two.start(3)
    sum_two.source(1)
    grad_two_out = pltpu.make_async_copy(grad_two_v, grad_two_hbm, store_sem.at[2])
    grad_two_out.start()
    bone_ref[...] = jnp.zeros_like(bone_ref)

    def piece(o):
        columns = pl.ds(pl.multiple_of(o * group, group), group)

        @pl.loop(0, count // tile)
        def _(r):
            rows = pl.ds(pl.multiple_of(r * tile, tile), tile)
            y = lax.dot_general(up_v[rows, :], two_v[o], over_last, preferred_element_type=F32)
            y = (y * pre_v[rows, columns].astype(F32)).astype(BF)
            pre_v[rows, columns] = y
            bone_ref[:, columns] += jnp.sum(y.astype(F32), axis=0, keepdims=True)

        wide = 1024

        @pl.loop(0, width // wide)
        def _(d):
            rows = pl.ds(pl.multiple_of(d * wide, wide), wide)
            y = lax.dot_general(
                normed_v[:, rows], pre_v[:, columns], over_first, preferred_element_type=F32
            )
            n = wide // per
            y = y.astype(BF).reshape(n, depth, per // depth, group)
            grad_one_v[pl.ds(d * n, n), :, :, columns] = y

    for way in (0, 1, -1):
        ok, copy = two_load(way)

        @pl.when(ok)
        def _():
            copy.wait()

    @pl.loop(0, 2 * depth - 3)
    def _(number):
        distance = (number + 1) // 2
        origin = jnp.where(lax.rem(number, 2) == 1, at - distance, at + distance)

        @pl.when((origin >= 0) & (origin < depth))
        def _():
            piece(jnp.clip(origin, 0, depth - 1))

    for copy in local:
        copy.wait()
    for part in range(3):
        for step in range(1, size):
            qkv_copy(step, part).wait_recv()
    two.arrive(3)
    attn.start(1)

    @pl.loop(2 * depth - 3, 2 * depth - 1)
    def _(number):
        distance = (number + 1) // 2
        origin = jnp.where(lax.rem(number, 2) == 1, at - distance, at + distance)

        @pl.when((origin >= 0) & (origin < depth))
        def _():
            piece(jnp.clip(origin, 0, depth - 1))

    sum_one.source(1)
    sum_one.source(2)
    grad_one_out = pltpu.make_async_copy(grad_one_v, grad_one_hbm, store_sem.at[5])
    grad_one_out.start()

    @pl.loop(0, count // tile)
    def _(r):
        rows = pl.ds(pl.multiple_of(r * tile, tile), tile)
        a = pre_v[rows, :]
        for s in range(size):
            w = one_v[s].reshape(per, units)
            y = lax.dot_general(a, w, over_last, preferred_element_type=F32)
            normed_v[rows, s * per : (s + 1) * per] = y.astype(BF)

    part_grad = pltpu.make_async_copy(normed_v, part_grad_hbm, store_sem.at[3])
    part_grad.start()
    attn.arrive(1)
    attn.start(2)

    @pl.loop(0, count // tile)
    def _(r):
        rows = pl.ds(pl.multiple_of(r * tile, tile), tile)
        a = hidden_v[rows, :]
        for s in range(size):
            columns = slice(s * per, (s + 1) * per)
            w = two_v[:, :, columns].reshape(units, per)
            up_v[rows, columns] = jnp.dot(a, w, preferred_element_type=F32).astype(BF)

    part_act = pltpu.make_async_copy(up_v, part_act_hbm, store_sem.at[4])
    part_act.start()
    attn.arrive(2)
    attn.start(3)
    sum_one.forward(2)
    grad_two_out.wait()
    for store in (grad_one_out, part_grad, part_act):
        store.wait()
    attn.arrive(3)
    sum_two.arrive(1, False)
    sum_one.arrive(1, True)
    sum_one.arrive(2, False)
    for step in (2, 3):
        two.sent(step)
    for step in (1, 2, 3):
        attn.sent(step)
    sum_two.sent(1)
    sum_one.sent(1)
    sum_one.sent(2)
    for part in range(3):
        for step in range(1, size):
            qkv_copy(step, part).wait_send()


def feed_forward(normed, up, one, two, w_qkv, w_out, full):
    size, depth = lax.axis_size("seq"), lax.axis_size("fsdp")
    micro, _, length, width = normed.shape
    units, cols = one.shape[-1], width // size
    rows = width // (size * depth)
    count = micro * size * length
    dims = (size, depth, micro, length, width, units, cols)
    hbm = pl.BlockSpec(memory_space=pl.ANY)
    vmem = pl.BlockSpec(memory_space=pltpu.VMEM)
    dma = pltpu.SemaphoreType.DMA
    sums = dma((2 * depth,))
    shape = jax.ShapeDtypeStruct
    tall, deep = (depth, units // depth, width), (size, depth, rows, units)
    return pl.pallas_call(
        functools.partial(ffn_kernel, dims),
        in_specs=[hbm] * 6 + [vmem],
        out_specs=[hbm] * 7 + [vmem],
        out_shape=[
            shape((count, width), BF),
            shape((count, width), BF),
            shape((size, depth, rows, 4 * cols), BF),
            shape(tall, BF),
            shape(deep, BF),
            shape((2,) + tall[1:], BF),
            shape((4, size, rows, units), BF),
            shape((1, units), F32),
        ],
        scratch_shapes=[
            pltpu.VMEM((count, width), BF),
            pltpu.VMEM((count, width), BF),
            pltpu.VMEM(deep, BF),
            pltpu.VMEM(tall, BF),
            pltpu.VMEM((count, units), BF),
            pltpu.VMEM((count, units), BF),
            pltpu.VMEM(tall, BF),
            pltpu.VMEM(deep, BF),
            pltpu.VMEM((size, rows, units), BF),
            pltpu.VMEM((size, rows, units), BF),
            pltpu.VMEM((2, size, rows, units), BF),
            dma((6,)),
            dma((2,)),
            dma((6,)),
        ]
        + [sums] * 8
        + [dma((3 * size,)), dma((3 * size,)), dma((3 + size,))],
        compiler_params=pltpu.CompilerParams(
            collective_id=2, has_side_effects=True, vmem_limit_bytes=60 * 1024 * 1024
        ),
        cost_estimate=pl.CostEstimate(
            flops=34 * 1000**3, bytes_accessed=300 * 1000 * 1000, transcendentals=0
        ),
    )(
        normed.reshape(count, width),
        up.reshape(count, width),
        one,
        two,
        w_qkv,
        w_out,
        full,
    )


def attn_layer_kernel(
    dims,
    starts_ref,
    cos_ref,
    sin_ref,
    normed_hbm,
    up_hbm,
    attn_hbm,
    grad_two_hbm,
    grad_one_hbm,
    old_two,
    old_one,
    part_act_hbm,
    tokens_hbm,
    full_ref,
    turned_hbm,
    mixed_hbm,
    grads_hbm,
    spread_hbm,
    land_two,
    land_one,
    bqkv_ref,
    two_ref,
    act_ref,
    normed_v,
    up_v,
    attn_v,
    natural_v,
    turned_v,
    mixed_v,
    grads_v,
    dk_s,
    dv_s,
    bias_s,
    own_two,
    held_two,
    out_two,
    one_total,
    held_one,
    part_act_v,
    tokens_v,
    to_core,
    act_sums,
    act_coming,
    load_sem,
    line_load,
    store_sem,
    sum_two_send,
    sum_two_recv,
    sum_one_send,
    sum_one_recv,
    a2a_send,
    a2a_recv,
    core_sem,
    axis_send,
    axis_recv,
):
    size, depth, micro, length, width, units, cols = dims
    me = lax.axis_index("seq")
    chips = size // 2
    groups = cols // LANES
    total = size * length
    count = micro * total
    per = width // size
    loads = [
        pltpu.make_async_copy(src, dst, load_sem.at[n])
        for n, (src, dst) in enumerate(
            ((normed_hbm, normed_v), (attn_hbm, attn_v), (up_hbm, up_v))
        )
    ]
    for load in loads:
        load.start()
    greet(size, depth)
    sum_two = LineSum(
        depth,
        lambda o: grad_two_hbm.at[o],
        lambda step, way: (
            old_two.at[int(way > 0)] if step < 2 else land_two.at[(step - 2) * 2 + (way > 0)]
        ),
        own_two,
        held_two,
        lambda step, way: out_two.at[int(way > 0)],
        line_load,
        sum_two_send,
        sum_two_recv,
    )
    sum_one = LineSum(
        depth,
        lambda o: grad_one_hbm.at[:, o],
        lambda step, way: (
            old_one.at[(step - 1) * 2 + (way > 0)] if step < 3 else land_one.at[int(way > 0)]
        ),
        one_total,
        held_one.at[0],
        lambda step, way: held_one.at[1 + (way > 0)],
        line_load,
        sum_one_send,
        sum_one_recv,
    )
    sum_one.source(3)
    sum_two.source(2)
    sum_two.source(3)
    sum_one.forward(3, here=False)
    sum_two.forward(2, here=False)
    tokens_load = pltpu.make_async_copy(tokens_hbm.at[0], tokens_v, load_sem.at[4])
    tokens_load.start()

    def part_act_half(parity):
        blocks = pl.ds(parity * chips, chips)
        return pltpu.make_async_copy(part_act_hbm.at[0, blocks], part_act_v, load_sem.at[3])

    part_act_half(1 - (me & 1)).start()

    def spread_copy(step):
        peer = me ^ step
        return remote(
            one_total.at[peer],
            spread_hbm.at[me],
            a2a_send.at[step],
            a2a_recv.at[step],
            {"seq": peer},
        )

    spread_mine = pltpu.make_async_copy(one_total.at[me], spread_hbm.at[me], store_sem.at[3])
    act = SeqSum(
        size,
        width,
        to_core,
        act_sums,
        act_coming,
        (core_sem.at[0], core_sem.at[1]),
        (axis_send, axis_recv),
        0,
    )

    def act_terms(parity, write):
        first = pl.multiple_of(parity * chips * length, chips * length)
        mine = mixed_v[pl.ds(first, chips * length), :]

        @pl.loop(0, size)
        def _(s):
            columns = pl.ds(pl.multiple_of(s * per, per), per)
            w = attn_v[s, :, :, 3 * cols :].reshape(cols, cols)
            y = jnp.dot(mine, w, preferred_element_type=F32).reshape(chips, length, per)
            write(columns, y + part_act_v[:, :, columns].astype(F32))

    for load in loads:
        load.wait()

    lane = lax.broadcasted_iota(jnp.int32, (1, LANES), 1)
    low_lane = (lane % HEAD_DIM) < (ROT // 2)
    over_first = (((0,), (0,)), ((), ()))
    over_last = (((1,), (1,)), ((), ()))

    def turn(value, cosine, sine):
        other = jnp.where(
            low_lane,
            pltpu.roll(value, LANES - ROT // 2, 1),
            pltpu.roll(value, ROT // 2, 1),
        )
        return value * cosine + other * sine

    high = chips * length

    @pl.loop(0, micro * 2)
    def _(r):
        m, parity = r // 2, lax.rem(r, 2)
        rows = pl.ds(pl.multiple_of(r * high, high), high)
        a = normed_v[rows, :]
        u = up_v[rows, :]
        for part in range(3):
            w = attn_v[:, :, :, part * cols : (part + 1) * cols].reshape(width, cols)
            y = jnp.dot(a, w, preferred_element_type=F32)
            y = y + full_ref[2 + part : 3 + part, pl.ds(pl.multiple_of(me * cols, cols), cols)]
            for block in range(chips):
                at = pl.ds(pl.multiple_of((block * 2 + parity) * length, length), length)
                cosine, sine = cos_ref[at, :], sin_ref[at, :]
                for g in range(groups):
                    v = y[block * length : (block + 1) * length, g * LANES : (g + 1) * LANES]
                    if part < 2:
                        v = turn(v, cosine, sine)
                    v = v.astype(BF)
                    if part == 0:
                        v = v * jnp.asarray(SCALE, BF)
                    natural_v[part, m, g, at, :] = v
        y = jnp.zeros((high, cols), F32)
        for s in range(size):
            w = attn_v[s, :, :, 3 * cols :].reshape(cols, cols)
            y = y + lax.dot_general(
                u[:, s * per : (s + 1) * per], w, over_last, preferred_element_type=F32
            )
        for block in range(chips):
            at = pl.ds(pl.multiple_of((block * 2 + parity) * length, length), length)
            for g in range(groups):
                v = y[block * length : (block + 1) * length, g * LANES : (g + 1) * LANES]
                natural_v[3, m, g, at, :] = v.astype(BF)

    tile = 256

    @pl.loop(0, micro * groups)
    def _(index):
        m, g = index // groups, lax.rem(index, groups)

        @pl.when(index == 2)
        def _():
            sum_one.sent(3)
            total = sum_one.total(3, held_one.at[0], held_one.at[1])
            one_total[...] = total.astype(BF)
            for step in range(1, size):
                spread_copy(step).start()
            spread_mine.start()
            tokens_load.wait()

        @pl.when(index == groups)
        def _():
            part_act_half(1 - (me & 1)).wait()
            act.away(act_terms)
            part_act_half(me & 1).start()

        @pl.when(index == micro * groups - 1)
        def _():
            part_act_half(me & 1).wait()
            act.here(act_terms)
            sum_two.sent_on(2)
            sum_two.forward(3)

        def label(positions):
            found = jnp.full(positions.shape, -1, jnp.int32)
            for piece in range(PIECES):
                start = starts_ref[m, piece]
                found = jnp.where((positions >= start) & (positions < start + IMG), piece, found)
            return found

        def put(target, at, columns, value):
            for part in range(value.shape[0] // length):
                block = at // length + part
                rows = m * total + store_index(block) * length
                target[pl.ds(pl.multiple_of(rows, length), length), columns] = value[
                    part * length : (part + 1) * length
                ].astype(BF)

        def columns_of(part):
            return pl.ds(pl.multiple_of(part * cols + g * LANES, LANES), LANES)

        dk_s[...] = jnp.zeros_like(dk_s)
        dv_s[...] = jnp.zeros_like(dv_s)
        for first in range(0, total, tile):
            last = min(total, first + tile + IMG)
            qpos = first + lax.broadcasted_iota(jnp.int32, (tile, 1), 0)
            kpos = first + lax.broadcasted_iota(jnp.int32, (1, last - first), 1)
            qlab, klab = label(qpos), label(kpos)
            allowed = (kpos <= qpos) | ((qlab == klab) & (qlab >= 0))
            bias_s[:, : last - first] = jnp.where(allowed, 0.0, -1e30)
            rows = slice(first, first + tile)
            keys = natural_v[1, m, g, :last, :]
            values = natural_v[2, m, g, :last, :]
            heads = [(lane // HEAD_DIM) == head for head in range(LANES // HEAD_DIM)]
            q = jnp.concatenate([jnp.where(h, natural_v[0, m, g, rows, :], 0) for h in heads])
            do = jnp.concatenate([jnp.where(h, natural_v[3, m, g, rows, :], 0) for h in heads])
            s = lax.dot_general(q, keys, over_last, preferred_element_type=F32)
            bias = jnp.concatenate([bias_s[:, : last - first]] * len(heads))
            if first:
                s = jnp.concatenate([s[:, :first], s[:, first:] + bias], axis=1)
            else:
                s = s + bias
            p = jnp.exp(s - jnp.max(s, axis=1, keepdims=True))
            p = p * (1.0 / jnp.sum(p, axis=1, keepdims=True))
            probs = p.astype(BF)
            dp = lax.dot_general(do, values, over_last, preferred_element_type=F32)
            att = jnp.dot(probs, values, preferred_element_type=F32)
            delta = jnp.sum(p * dp, axis=1, keepdims=True)
            ds = (p * (dp - delta)).astype(BF)
            mixed = jnp.where(heads[0], att[:tile], att[tile:])
            dq = jnp.dot(ds, keys, preferred_element_type=F32)
            dq = jnp.where(heads[0], dq[:tile], dq[tile:])
            dk_s[:last, :] += lax.dot_general(ds, q, over_first, preferred_element_type=F32)
            dv_s[:last, :] += lax.dot_general(probs, do, over_first, preferred_element_type=F32)
            put(mixed_v, first, pl.ds(pl.multiple_of(g * LANES, LANES), LANES), mixed)
            dq = turn(dq * SCALE, cos_ref[rows, :], -sin_ref[rows, :])
            put(turned_v, first, columns_of(0), dq)
        put(turned_v, 0, columns_of(1), turn(dk_s[...], cos_ref[...], -sin_ref[...]))
        put(turned_v, 0, columns_of(2), dv_s[...])

    stores = [
        pltpu.make_async_copy(turned_v, turned_hbm, store_sem.at[0]),
        pltpu.make_async_copy(mixed_v, mixed_hbm, store_sem.at[1]),
    ]
    for store in stores:
        store.start()
    bits = size.bit_length() - 2
    for stage in range(bits - 1):
        act.step(stage)

    wide = 512

    @pl.loop(0, width // wide)
    def _(d):
        rows = pl.ds(pl.multiple_of(d * wide, wide), wide)
        y = lax.dot_general(normed_v[:, rows], turned_v[...], over_first, preferred_element_type=F32)
        n = wide // per
        grads_v[pl.ds(d * n, n), :, :, : 3 * cols] = y.astype(BF).reshape(
            n, depth, per // depth, 3 * cols
        )
        y = lax.dot_general(mixed_v[...], up_v[:, rows], over_first, preferred_element_type=F32)
        y = y.astype(BF)
        for k in range(n):
            grads_v[d * n + k, :, :, 3 * cols :] = y[:, k * per : (k + 1) * per].reshape(
                depth, cols // depth, per
            )

    grads_out = pltpu.make_async_copy(grads_v, grads_hbm, store_sem.at[2])
    grads_out.start()
    bqkv_ref[...] = jnp.sum(turned_v[...].astype(F32), axis=0, keepdims=True)
    act.add(bits - 1)
    bias = full_ref[5:6, :] + full_ref[6 + size * units // width : 7 + size * units // width, :]
    act_ref[...] = (tokens_v[...].astype(F32) + act.last() + bias).astype(BF)
    sum_two.sent_first(2)
    sum_two.sent(3)
    two_ref[...] = sum_two.total(3, held_two, out_two.at[0])
    for store in stores:
        store.wait()
    grads_out.wait()
    spread_mine.wait()
    for step in range(1, size):
        spread_copy(step).wait_recv()
        spread_copy(step).wait_send()
    act.core_sent()
    act.sent()


def attention_layer(
    starts, normed, up, attn, grad_two, grad_one, old_two, old_one, part_act, tokens, full
):
    size, depth, rows, units = grad_one.shape
    micro, _, length, width = normed.shape
    cols = width // size
    count, total = micro * size * length, size * length
    dims = (size, depth, micro, length, width, units, cols)
    cosine, sine = tables(total)
    chips = size // 2
    hbm = pl.BlockSpec(memory_space=pl.ANY)
    vmem = pl.BlockSpec(memory_space=pltpu.VMEM)
    dma = pltpu.SemaphoreType.DMA
    sums = dma((2 * depth,))
    shape = jax.ShapeDtypeStruct
    tall, deep = (units // depth, width), (size, rows, units)
    return pl.pallas_call(
        functools.partial(attn_layer_kernel, dims),
        in_specs=[pl.BlockSpec(memory_space=pltpu.SMEM)] + [vmem] * 2 + [hbm] * 9 + [vmem],
        out_specs=[hbm] * 6 + [vmem] * 3,
        out_shape=[
            shape((count, 3 * cols), BF),
            shape((count, cols), BF),
            shape(attn.shape, BF),
            shape(deep, BF),
            shape((4,) + tall, BF),
            shape((2,) + deep, BF),
            shape((1, 3 * cols), F32),
            shape(tall, F32),
            shape((length, width), BF),
        ],
        scratch_shapes=[
            pltpu.VMEM((count, width), BF),
            pltpu.VMEM((count, width), BF),
            pltpu.VMEM(attn.shape, BF),
            pltpu.VMEM((4, micro, cols // LANES, total, LANES), BF),
            pltpu.VMEM((count, 3 * cols), BF),
            pltpu.VMEM((count, cols), BF),
            pltpu.VMEM(attn.shape, BF),
            pltpu.VMEM((total, LANES), F32),
            pltpu.VMEM((total, LANES), F32),
            pltpu.VMEM((256, 512), F32),
            pltpu.VMEM(tall, BF),
            pltpu.VMEM(tall, BF),
            pltpu.VMEM((2,) + tall, BF),
            pltpu.VMEM(deep, BF),
            pltpu.VMEM((3,) + deep, BF),
            pltpu.VMEM((chips, length, width), BF),
            pltpu.VMEM((length, width), BF),
            pltpu.VMEM((chips, length, width), BF),
            pltpu.VMEM((chips, length, width), BF),
            pltpu.VMEM((chips - 1, length, width), BF),
            dma((5,)),
            dma((2,)),
            dma((4,)),
        ]
        + [sums] * 4
        + [dma((size,)), dma((size,)), dma((2,))]
        + [dma((2 * (chips - 1),))] * 2,
        compiler_params=pltpu.CompilerParams(
            collective_id=3, has_side_effects=True, vmem_limit_bytes=62 * 1024 * 1024
        ),
        cost_estimate=pl.CostEstimate(
            flops=40 * 1000**3, bytes_accessed=300 * 1000 * 1000, transcendentals=0
        ),
    )(
        starts,
        cosine,
        sine,
        normed.reshape(count, width),
        up.reshape(count, width),
        attn,
        grad_two,
        grad_one,
        old_two,
        old_one,
        part_act,
        tokens,
        full,
    )


def close_kernel(
    dims,
    tokens_hbm,
    up_hbm,
    grads_hbm,
    attn_hbm,
    turned_hbm,
    mixed_hbm,
    part_grad_hbm,
    part_act_hbm,
    full_ref,
    bqkv_ref,
    bone_ref,
    first_act_ref,
    act_ref,
    ingrad_ref,
    out_ref,
    vec_ref,
    spread_hbm,
    tokens_v,
    up_v,
    attn_v,
    turned_v,
    mixed_v,
    part_grad_v,
    part_act_v,
    to_core,
    sums,
    coming,
    grads_v,
    landing,
    line_out,
    total_v,
    vec_in,
    load_sem,
    core_send,
    core_recv,
    axis_send,
    axis_recv,
    line_send,
    line_recv,
    a2a_send,
    a2a_recv,
    vec_send,
    vec_recv,
):
    size, depth, micro, length, width, units, cols = dims
    me, at = lax.axis_index("seq"), lax.axis_index("fsdp")
    count = size.bit_length() - 1
    chips = size // 2
    chip, core = me >> 1, me & 1
    half = width // 2
    per = width // size

    loads = [
        pltpu.make_async_copy(src, dst, load_sem.at[n])
        for n, (src, dst) in enumerate(
            (
                (turned_hbm, turned_v),
                (attn_hbm, attn_v),
                (part_grad_hbm, part_grad_v),
                (part_act_hbm.at[pl.ds(1, micro - 1)], part_act_v),
                (mixed_hbm, mixed_v),
                (tokens_hbm, tokens_v),
                (up_hbm, up_v),
                (grads_hbm, grads_v),
            )
        )
    ]
    for load in loads[7:] + loads[:7]:
        load.start()
    greet(size, depth)

    def line_copy(step, way, part, src):
        number = (step * 2 + (way > 0)) * 2 + part
        return remote(
            src,
            landing.at[number],
            line_send.at[number],
            line_recv.at[number],
            {"fsdp": jnp.clip(at + way, 0, depth - 1)},
        )

    def place_of(way):
        return at if way > 0 else depth - 1 - at

    def chunk(origin, part):
        return grads_v.at[pl.ds(part * chips, chips), origin]

    def origin_of(step, way):
        away = jnp.clip(depth - step + place_of(way), 0, depth - 1)
        return away if way > 0 else depth - 1 - away

    def line_source():
        for step in range(1, depth):
            for part in range(2):
                for way in (1, -1):

                    @pl.when(place_of(way) == 0)
                    def _():
                        line_copy(step, way, part, chunk(origin_of(step, way), part)).start()

    def line_forward(step, part):
        for way in (1, -1):
            place = place_of(way)
            slot = (way > 0) * 2 + part

            @pl.when((place >= 1) & (place <= step - 1) & (place < depth - 1))
            def _():
                arrived = line_copy(step - 1, way, part, line_out.at[slot])
                arrived.wait_recv()

                @pl.when(place <= step - 2)
                def _():
                    arrived.wait_send()

                came = landing[((step - 1) * 2 + (way > 0)) * 2 + part]
                mine = chunk(origin_of(step, way), part)[...]
                line_out[slot] = (mine.astype(F32) + came.astype(F32)).astype(BF)
                line_copy(step, way, part, line_out.at[slot]).start()

    def line_finish(part):
        for way in (1, -1):
            place = place_of(way)
            number = ((depth - 1) * 2 + (way > 0)) * 2 + part

            @pl.when(place >= 1)
            def _():
                line_copy(depth - 1, way, part, line_out.at[0]).wait_recv()

            @pl.when(place == 0)
            def _():
                landing[number] = jnp.zeros_like(landing[number])

        first = (depth - 1) * 4 + part
        summed = chunk(at, part)[...].astype(F32)
        summed = summed + landing[first].astype(F32) + landing[first + 2].astype(F32)
        total_v[pl.ds(part * chips, chips)] = summed.astype(BF)
        for block in range(chips):
            out_ref[:, (part * chips + block) * cols : (part * chips + block + 1) * cols] = summed[
                block, :, 3 * cols :
            ]

    def line_sent():
        for part in range(2):
            for way in (1, -1):
                place = place_of(way)

                @pl.when(place == 0)
                def _():
                    for step in range(1, depth):
                        line_copy(step, way, part, line_out.at[0]).wait_send()

                @pl.when((place >= 1) & (place < depth - 1))
                def _():
                    line_copy(depth - 1, way, part, line_out.at[0]).wait_send()

    def back_copy(step):
        peer = me ^ step
        return remote(
            total_v.at[peer, :, pl.ds(0, 3 * cols)],
            spread_hbm.at[me],
            a2a_send.at[step],
            a2a_recv.at[step],
            {"seq": peer},
        )

    orders = [(0, m) for m in range(micro)] + [(1, m) for m in range(1, micro)]
    found = {}
    for number, (array, m) in enumerate(orders):
        found[array, m] = SeqSum(
            size,
            width,
            to_core.at[number],
            sums.at[number],
            coming.at[number],
            (core_send.at[number], core_recv.at[number]),
            (axis_send, axis_recv),
            number * 2 * (chips - 1),
        )

    over_last = (((1,), (1,)), ((), ()))

    def grad_terms(m):
        def terms(parity, write):
            blocks = pl.ds(parity * chips, chips)
            turned = turned_v[m, blocks].reshape(chips * length, 3 * cols)

            @pl.loop(0, size)
            def _(s):
                columns = pl.ds(pl.multiple_of(s * per, per), per)
                w = attn_v[s, :, :, : 3 * cols].reshape(per, 3 * cols)
                y = lax.dot_general(turned, w, over_last, preferred_element_type=F32)
                y = y.reshape(chips, length, per)
                write(columns, y + part_grad_v[m, blocks, :, columns].astype(F32))

        return terms

    def act_terms(m):
        def terms(parity, write):
            blocks = pl.ds(parity * chips, chips)
            mixed = mixed_v[m, blocks].reshape(chips * length, cols)

            @pl.loop(0, size)
            def _(s):
                columns = pl.ds(pl.multiple_of(s * per, per), per)
                w = attn_v[s, :, :, 3 * cols :].reshape(per, cols)
                y = jnp.dot(mixed, w, preferred_element_type=F32).reshape(chips, length, per)
                write(columns, y + part_act_v[m - 1, blocks, :, columns].astype(F32))

        return terms

    gain = full_ref[0:1, :]
    vec_ref[...] = jnp.zeros_like(vec_ref)
    for part in range(3):
        columns = pl.ds(pl.multiple_of(me * cols, cols), cols)
        vec_ref[2 + part : 3 + part, columns] = bqkv_ref[:, part * cols : (part + 1) * cols]
    bone_at = pl.multiple_of(lax.rem(me * units, width), units)
    vec_ref[pl.ds(6 + me * units // width, 1), pl.ds(bone_at, units)] = bone_ref[...]

    def norm_back(m):
        x = tokens_v[m].astype(F32)
        dy = found[0, m].last()
        center = x - jnp.mean(x, axis=-1, keepdims=True)
        spread = jnp.mean(center * center, axis=-1, keepdims=True)
        r = lax.rsqrt(spread + EPSILON)
        xhat = center * r
        g = dy * gain
        inner = g - jnp.mean(g, axis=-1, keepdims=True)
        inner = inner - xhat * jnp.mean(g * xhat, axis=-1, keepdims=True)
        upstream = up_v[m].astype(F32)
        ingrad_ref[m] = upstream + r * inner
        vec_ref[5:6, :] += jnp.sum(upstream, axis=0, keepdims=True)
        vec_ref[0:1, :] += jnp.sum(dy * xhat, axis=0, keepdims=True)
        vec_ref[1:2, :] += jnp.sum(dy, axis=0, keepdims=True)

    def act_out(m):
        bias = full_ref[5:6, :] + full_ref[6 + size * units // width : 7 + size * units // width, :]
        total = tokens_v[m].astype(F32) + found[1, m].last() + bias
        act_ref[m] = total.astype(BF)

    levels = [("seq", 1 << bit) for bit in range(count)]
    levels = levels + [("fsdp", 1 << bit) for bit in range(depth.bit_length() - 1)]

    def vec_copy(level):
        axis, step = levels[level]
        mine = me if axis == "seq" else at
        return remote(
            vec_ref,
            vec_in.at[level],
            vec_send.at[level],
            vec_recv.at[level],
            {axis: mine ^ step},
        )

    def vec_level(level):
        copy = vec_copy(level)
        copy.wait()
        vec_ref[...] += vec_in[level]
        if level + 1 < len(levels):
            vec_copy(level + 1).start()

    loads[7].wait()
    line_source()
    for load in loads[:3]:
        load.wait()
    for m in range(micro):
        found[0, m].away(grad_terms(m))
    line_forward(2, 0)
    for m in range(micro):
        found[0, m].here(grad_terms(m))
    for load in loads[3:7]:
        load.wait()
    act_ref[0] = first_act_ref[...]
    found[1, 1].away(act_terms(1))
    line_forward(2, 1)
    found[1, 1].here(act_terms(1))
    found[0, 0].step(0)
    line_forward(3, 0)
    found[0, 1].step(0)
    found[0, 0].add(1)
    line_forward(3, 1)
    norm_back(0)
    found[1, 1].step(0)
    found[0, 1].add(1)
    norm_back(1)
    vec_copy(0).start()

    def finish(part):
        line_finish(part)
        for step in range(1, size):
            peer = me ^ step

            @pl.when((peer >= part * chips) & (peer < (part + 1) * chips))
            def _():
                back_copy(step).start()

    found[1, 1].add(1)
    act_out(1)
    vec_level(0)
    vec_level(1)
    finish(0)
    for level in range(2, len(levels)):
        vec_level(level)
    finish(1)

    back_mine = pltpu.make_async_copy(
        total_v.at[me, :, pl.ds(0, 3 * cols)], spread_hbm.at[me], a2a_recv.at[0]
    )
    back_mine.start()
    back_mine.wait()
    for step in range(1, size):
        back_copy(step).wait_recv()

    line_sent()
    for step in range(1, size):
        back_copy(step).wait_send()
    for terms in found.values():
        terms.core_sent()
        terms.sent()


def close_layer(
    tokens, upstream, grads, attn, turned, mixed, part_grad, part_act, full, bqkv, bone, first_act
):
    size, depth = lax.axis_size("seq"), lax.axis_size("fsdp")
    micro, length, width = tokens.shape
    units, cols = bone.shape[-1], width // size
    rows = width // (size * depth)
    dims = (size, depth, micro, length, width, units, cols)
    chips, count = size // 2, size.bit_length() - 1
    hbm = pl.BlockSpec(memory_space=pl.ANY)
    vmem = pl.BlockSpec(memory_space=pltpu.VMEM)
    dma = pltpu.SemaphoreType.DMA
    levels = count + depth.bit_length() - 1
    piece = (chips, rows, 4 * cols)
    arrays = 2 * micro - 1
    shape = jax.ShapeDtypeStruct
    loaded = [v.shape for v in (tokens, upstream, attn, turned, mixed, part_grad)]
    loaded = loaded + [(micro - 1,) + part_act.shape[1:]]
    return pl.pallas_call(
        functools.partial(close_kernel, dims),
        in_specs=[hbm] * 8 + [vmem] * 4,
        out_specs=[vmem] * 4 + [hbm],
        out_shape=[
            shape(tokens.shape, BF),
            shape(tokens.shape, F32),
            shape((rows, width), F32),
            shape(full.shape, F32),
            shape((size, rows, 3 * cols), BF),
        ],
        scratch_shapes=[pltpu.VMEM(s, BF) for s in loaded]
        + [
            pltpu.VMEM((arrays, chips, length, width), BF),
            pltpu.VMEM((arrays, chips, length, width), BF),
            pltpu.VMEM((arrays, chips - 1, length, width), BF),
            pltpu.VMEM(grads.shape, BF),
            pltpu.VMEM((4 * depth,) + piece, BF),
            pltpu.VMEM((4,) + piece, BF),
            pltpu.VMEM((size, rows, 4 * cols), BF),
            pltpu.VMEM((levels,) + full.shape, F32),
            dma((9,)),
            dma((arrays,)),
            dma((arrays,)),
            dma((2 * arrays * (chips - 1),)),
            dma((2 * arrays * (chips - 1),)),
            dma((4 * depth,)),
            dma((4 * depth,)),
            dma((size,)),
            dma((size,)),
            dma((levels,)),
            dma((levels,)),
        ],
        compiler_params=pltpu.CompilerParams(
            collective_id=4, has_side_effects=True, vmem_limit_bytes=62 * 1024 * 1024
        ),
        cost_estimate=pl.CostEstimate(
            flops=30 * 1000**3, bytes_accessed=300 * 1000 * 1000, transcendentals=0
        ),
    )(
        tokens,
        upstream,
        grads,
        attn,
        turned,
        mixed,
        part_grad,
        part_act,
        full,
        bqkv,
        bone,
        first_act,
    )


def result_kernel(
    dims,
    place_ref,
    act_ref,
    ingrad_ref,
    out_ref,
    two_ref,
    one_ref,
    qkv_ref,
    vec_ref,
    act_to,
    ingrad_to,
    gain_ref,
    shift_ref,
    wqkv_ref,
    bqk_ref,
    bv_ref,
    out_to,
    bout_ref,
    one_to,
    bone_ref,
    two_to,
    btwo_ref,
):
    size, depth, width, cols, units = dims
    for source, target in (
        (ingrad_ref, ingrad_to),
        (two_ref, two_to),
        (act_ref, act_to),
        (out_ref, out_to),
    ):
        target[...] = source[...]
    for s in range(size):
        one_to[:, s * units : (s + 1) * units] = one_ref[s].astype(F32)
        for part in range(3):
            start = part * width + s * cols
            wqkv_ref[:, start : start + cols] = qkv_ref[s, :, part * cols : (part + 1) * cols].astype(
                F32
            )
    index = place_ref[0]

    def own(row, total, target):
        extent = total // (size * depth)
        flat = index * extent
        at = lax.rem(flat, width)
        values = vec_ref[pl.ds(row + flat // width, 1), :]
        values = pltpu.roll(values, lax.rem(width - at, width), 1)
        target[...] = values[:, :extent]

    own(0, width, gain_ref)
    own(1, width, shift_ref)
    own(2, 2 * width, bqk_ref)
    own(4, width, bv_ref)
    own(5, width, bout_ref)
    own(5, width, btwo_ref)
    own(6, size * units, bone_ref)


def results(activations, input_grad, grad_out, grad_two, spread_one, spread_qkv, vectors, index):
    size, rows, units = spread_one.shape
    width = vectors.shape[-1]
    depth = width // (size * rows)
    cols = width // size
    dims = (size, depth, width, cols, units)
    vmem = pl.BlockSpec(memory_space=pltpu.VMEM)

    def row(extent):
        return jax.ShapeDtypeStruct((1, extent // (size * depth)), F32)

    def like(value):
        return jax.ShapeDtypeStruct(value.shape, value.dtype)

    wide = jax.ShapeDtypeStruct((rows, size * units), F32)
    shapes = [
        like(activations),
        like(input_grad),
        row(width),
        row(width),
        jax.ShapeDtypeStruct((rows, 3 * width), F32),
        row(2 * width),
        row(width),
        like(grad_out),
        row(width),
        wide,
        row(size * units),
        like(grad_two),
        row(width),
    ]
    return pl.pallas_call(
        functools.partial(result_kernel, dims),
        in_specs=[pl.BlockSpec(memory_space=pltpu.SMEM)] + [vmem] * 7,
        out_specs=[vmem] * len(shapes),
        out_shape=shapes,
        compiler_params=pltpu.CompilerParams(vmem_limit_bytes=60 * 1024 * 1024),
    )(index[None], activations, input_grad, grad_out, grad_two, spread_one, spread_qkv, vectors)


def gelu_tanh(values):
    return jax.nn.gelu(values, approximate=True)


def layer_norm(values, gain, shift):
    center = values - jnp.mean(values, axis=-1, keepdims=True)
    spread = jnp.mean(center * center, axis=-1, keepdims=True)
    return center * lax.rsqrt(spread + EPSILON) * gain + shift


def fence(*values):
    return lax.optimization_barrier(values)


def line_right(value, senders):
    return lax.ppermute(value, "fsdp", [(i, i + 1) for i in senders])


def line_left(value, senders):
    last = lax.axis_size("fsdp") - 1
    return lax.ppermute(value, "fsdp", [(last - i, last - i - 1) for i in senders])


class Gather:
    def __init__(self, mine):
        self.right, self.left = [mine], [mine]

    def step(self):
        size = lax.axis_size("fsdp")
        number = len(self.right)
        if number < size:
            self.right.append(line_right(self.right[-1], range(number - 1, size - 1)))
            self.left.append(line_left(self.left[-1], range(number - 1, size - 1)))

    def fence(self, *others):
        (self.right[-1], self.left[-1]), *others = fence((self.right[-1], self.left[-1]), *others)
        return others

    def rest(self):
        while len(self.right) < lax.axis_size("fsdp"):
            self.step()

    def pieces(self):
        size = lax.axis_size("fsdp")
        at = lax.axis_index("fsdp")
        found = [(self.right[0], at)]
        for step in range(1, size):
            piece = jnp.where(at >= step, self.right[step], self.left[size - step])
            found.append((piece, lax.rem(at - step + size, size)))
        return found


class Scatter:
    def __init__(self, chunk):
        self.chunk = chunk
        self.number = 0
        self.right = self.left = None

    def step(self):
        size = lax.axis_size("fsdp")
        at = lax.axis_index("fsdp")
        if self.number == size - 1:
            return
        self.number += 1
        going = self.chunk(jnp.minimum(size - self.number + at, size - 1))
        coming = self.chunk(jnp.maximum(self.number - size + at, 0))
        if self.number > 1:
            going = (going.astype(F32) + self.right.astype(F32)).astype(BF)
            coming = (coming.astype(F32) + self.left.astype(F32)).astype(BF)
        self.right = line_right(going, range(self.number))
        self.left = line_left(coming, range(self.number))

    def rest(self):
        while self.number < lax.axis_size("fsdp") - 1:
            self.step()

    def fence(self, *others):
        (self.right, self.left), *others = fence((self.right, self.left), *others)
        return others

    def total(self):
        mine = self.chunk(lax.axis_index("fsdp")).astype(F32)
        return mine + self.right.astype(F32) + self.left.astype(F32)


def staged_layer(
    tokens, upstream, w_fc2, w_qkv, w_out, starts, normed, up, my_one, two_near, full, index
):
    size, depth = lax.axis_size("seq"), lax.axis_size("fsdp")
    me = lax.axis_index("seq")
    micro, length, width = tokens.shape
    rows = width // (size * depth)
    hidden_rows = w_fc2.shape[0]
    cols = width // size
    units = hidden_rows * depth
    count = micro * size * length

    def contract_last(left, right):
        return lax.dot_general(left, right, (((1,), (1,)), ((), ())), preferred_element_type=F32)

    def contract_first(left, right):
        return lax.dot_general(left, right, (((0,), (0,)), ((), ())), preferred_element_type=F32)

    def place_columns(pieces):
        out = jnp.zeros((size, depth) + pieces[0][0].shape[1:], BF)
        for piece, origin in pieces:
            out = lax.dynamic_update_slice_in_dim(out, piece[:, None], origin, 1)
        return out

    def place_rows(pieces):
        out = jnp.zeros((depth,) + pieces[0][0].shape, BF)
        for piece, origin in pieces:
            out = lax.dynamic_update_slice_in_dim(out, piece[None], origin, 0)
        return out

    normed = normed.reshape(count, width)
    up = up.reshape(count, width)
    my_one = my_one.reshape(width, units)
    two = Gather(w_fc2)
    at = lax.axis_index("fsdp")
    for way, found in ((-1, two.right), (1, two.left)):
        origin = jnp.clip(at + way, 0, depth - 1)
        found.append(lax.dynamic_index_in_dim(two_near, origin, 0, keepdims=False))
    gain, shift, bias_out = full[0], full[1], full[5]
    bias_qkv = lax.dynamic_slice_in_dim(full[2:5], me * cols, cols, 1).reshape(-1)
    ratio = size * units // width
    bias_one = lax.dynamic_slice_in_dim(full[6 : 6 + ratio].reshape(-1), me * units, units, 0)
    bias_two = full[6 + ratio]
    two.step()
    split = w_qkv.reshape(rows, 3, size, cols).transpose(2, 0, 1, 3).reshape(size, rows, 3 * cols)
    attn_cols = lax.all_to_all(split, "seq", 0, 0, tiled=True)
    out_cols = w_out.reshape(rows, size, cols).transpose(1, 0, 2)
    attn_cols = jnp.concatenate([attn_cols, out_cols], axis=-1)
    pre = jnp.dot(normed, my_one, preferred_element_type=F32) + bias_one
    hidden, back = jax.vjp(gelu_tanh, pre)
    hidden = hidden.astype(BF)
    grad_two = contract_first(hidden, up).astype(BF).reshape(depth, hidden_rows, width)
    hidden, grad_two = two.fence(hidden, grad_two)
    two.step()
    sum_two = Scatter(lambda o: lax.dynamic_index_in_dim(grad_two, o, 0, keepdims=False))
    sum_two.step()
    (two.right, two.left), (sum_two.right, sum_two.left), attn_cols = fence(
        (two.right, two.left), (sum_two.right, sum_two.left), attn_cols
    )
    attn = Gather(attn_cols)
    attn.step()
    two.rest()
    my_two = place_rows(two.pieces()).reshape(units, width)
    pre_grad = back(contract_last(up, my_two))[0].astype(BF)
    grad_one = contract_first(normed, pre_grad).astype(BF).reshape(size, depth, rows, units)
    pre_grad, grad_one = attn.fence(pre_grad, grad_one)
    attn.step()
    sum_one = Scatter(lambda o: lax.dynamic_index_in_dim(grad_one, o, 1, keepdims=False))
    sum_one.step()
    (sum_one.right, sum_one.left), (sum_two.right, sum_two.left) = attn.fence(
        (sum_one.right, sum_one.left), (sum_two.right, sum_two.left)
    )
    attn.step()
    sum_two.step()
    (sum_two.right, sum_two.left), normed, up = attn.fence(
        (sum_two.right, sum_two.left), normed, up
    )
    sum_two.step()
    attn.rest()
    attn_weights = place_columns(attn.pieces())
    my_qkv = attn_weights[..., : 3 * cols].reshape(width, 3 * cols)
    my_out = attn_weights[..., 3 * cols :].transpose(1, 2, 0, 3).reshape(cols, width)
    projected = jnp.dot(normed, my_qkv, preferred_element_type=F32) + bias_qkv
    projected = projected.reshape(micro, size, length, 3 * cols)
    mixed_grad = contract_last(up, my_out).astype(BF).reshape(micro, size, length, cols)
    parts = [attention(starts[:1], projected[:1], mixed_grad[:1])]
    (sum_one.right, sum_one.left), (projected, mixed_grad), parts = sum_two.fence(
        (sum_one.right, sum_one.left), (projected, mixed_grad), parts
    )
    sum_one.step()
    for m in range(1, micro):
        parts.append(attention(starts[m:][:1], projected[m:][:1], mixed_grad[m:][:1]))
    mixed = jnp.concatenate([part[0] for part in parts]).reshape(count, cols)
    projected_grad = jnp.concatenate(
        [jnp.concatenate(part[1:], axis=-1) for part in parts]
    ).reshape(count, 3 * cols)
    projected_grad, mixed = sum_one.fence(projected_grad, mixed)
    sum_one.step()
    grad_qkv = contract_first(normed, projected_grad).astype(BF).reshape(size, depth, rows, 3 * cols)
    grad_out = contract_first(mixed, up).astype(BF).reshape(depth, rows, size, cols)
    grad_qkv, grad_out, (sum_two.right, sum_two.left) = sum_one.fence(
        grad_qkv, grad_out, (sum_two.right, sum_two.left)
    )
    grad_attn = jnp.concatenate([grad_qkv, grad_out.transpose(2, 0, 1, 3)], axis=-1)

    def to_rows(mine, parts):
        mine = lax.all_to_all(mine.astype(BF), "seq", 0, 0, tiled=True).astype(F32)
        return mine.reshape(size, rows, parts, -1).transpose(1, 2, 0, 3).reshape(rows, -1)

    sum_one.rest()
    sum_two.rest()
    out_two = sum_two.total()
    out_one = to_rows(sum_one.total(), 1)

    def put(values, extent, at):
        return lax.dynamic_update_slice_in_dim(jnp.zeros(extent, F32), values, at, -1)

    bqkv = jnp.sum(projected_grad.astype(F32), axis=0).reshape(3, cols)
    bqkv = put(bqkv, (3, width), me * cols)
    bone = put(jnp.sum(pre_grad.astype(F32), axis=0), (size * units,), me * units)
    btwo = jnp.sum(upstream.astype(F32), axis=(0, 1))[None]
    early = [jnp.zeros((2, width), F32), bqkv, btwo, bone.reshape(ratio, width)]
    early = jnp.pad(jnp.concatenate(early), ((0, full.shape[0] - 6 - ratio), (0, 0)))

    sum_attn = Scatter(lambda o: lax.dynamic_index_in_dim(grad_attn, o, 1, keepdims=False))
    sum_attn.step()
    grad_terms = contract_last(projected_grad, my_qkv) + contract_last(pre_grad, my_one)
    grad_terms = grad_terms.astype(BF).reshape(micro, size, length, width)
    (grad_terms,) = sum_attn.fence(grad_terms)
    sum_attn.step()
    normed_grad = scatter_seq(grad_terms)
    terms = jnp.dot(mixed, my_out, preferred_element_type=F32)
    terms = terms + jnp.dot(hidden, my_two, preferred_element_type=F32)
    terms = terms.astype(BF).reshape(micro, size, length, width)
    sums = scatter_seq(terms)
    sum_attn.rest()
    attn_total = sum_attn.total()
    out_qkv = to_rows(attn_total[..., : 3 * cols], 3)
    out_out = attn_total[..., 3 * cols :].transpose(1, 0, 2).reshape(rows, width)
    activations = (tokens.astype(F32) + sums + (bias_out + bias_two)).astype(BF)
    _, norm_back = jax.vjp(layer_norm, tokens.astype(F32), gain, shift)
    input_grad, gain_grad, shift_grad = norm_back(normed_grad)
    input_grad = input_grad + upstream.astype(F32)
    vectors = early.at[:2].add(jnp.stack([gain_grad, shift_grad]))
    vectors = lax.psum(vectors, ("seq", "fsdp"))

    return activations, input_grad, out_qkv, out_out, vectors, out_one, out_two


def per_device(
    tokens,
    ln_gain,
    ln_bias,
    w_qkv,
    b_qkv,
    w_out,
    b_out,
    w_fc1,
    b_fc1,
    w_fc2,
    b_fc2,
    piece_starts,
    cotangent,
):
    size, depth = lax.axis_size("seq"), lax.axis_size("fsdp")
    me = lax.axis_index("seq")
    micro, _, length, width = tokens.shape
    rows = width // (size * depth)
    hidden_rows = w_fc2.shape[0]
    cols = width // size
    units = hidden_rows * depth
    count = micro * size * length
    tokens = tokens[:, 0]
    upstream = cotangent[:, 0]

    index = me * depth + lax.axis_index("fsdp")
    packed = []
    for vector in (ln_gain, ln_bias, b_qkv, b_out, b_fc1, b_fc2):
        mine = jnp.arange(size * depth, dtype=jnp.int32)[:, None] == index
        packed.append(jnp.where(mine, vector[None, :], 0).astype(BF).reshape(-1, width))
    packed = jnp.concatenate(packed, axis=0)
    packed = jnp.pad(packed, ((0, -packed.shape[0] % 16), (0, 0)))
    starts = piece_starts[:, 0]
    loaded = load_all(tokens, upstream, w_fc1, w_fc2, packed)
    if (size, depth, micro) == (8, 4, 2):
        normed, up, one, two_near, full = loaded
        part_grad, part_act, attn, grad_two, grad_one, land_two, land_one, bone = feed_forward(
            normed, up, one, two_near, w_qkv, w_out, full
        )
        wide = (micro, size, length, -1)
        part_act = part_act.reshape(wide)
        turned, mixed, grads, spread_one, _, _, bqkv, out_two, first_act = attention_layer(
            starts,
            normed,
            up,
            attn,
            grad_two,
            grad_one,
            land_two,
            land_one,
            part_act,
            tokens,
            full,
        )
        activations, input_grad, out_out, vectors, spread_qkv = close_layer(
            tokens,
            upstream,
            grads,
            attn,
            turned.reshape(wide),
            mixed.reshape(wide),
            part_grad.reshape(wide),
            part_act,
            full,
            bqkv,
            bone,
            first_act,
        )

        found = results(
            activations, input_grad, out_out, out_two, spread_one, spread_qkv, vectors, index
        )
        found = [v.reshape(-1) if n in (2, 3, 5, 6, 8, 10, 12) else v for n, v in enumerate(found)]
        return (found[0][:, None], found[1][:, None]) + tuple(found[2:])

    activations, input_grad, out_qkv, out_out, vectors, out_one, out_two = staged_layer(
        tokens, upstream, w_fc2, w_qkv, w_out, starts, *loaded, index
    )
    ratio = w_fc1.shape[1] // width

    def own(values):
        values = values.reshape(-1)
        extent = values.shape[0] // (size * depth)
        return lax.dynamic_slice_in_dim(values, index * extent, extent, 0)

    grad_b_two = own(vectors[5])
    return (
        activations[:, None],
        input_grad[:, None],
        own(vectors[0]),
        own(vectors[1]),
        out_qkv,
        own(vectors[2:4]),
        own(vectors[4]),
        out_out,
        grad_b_two,
        out_one,
        own(vectors[6 : 6 + ratio]),
        out_two,
        grad_b_two,
    )


def solution(mesh):
    both = ("seq", "fsdp")
    row = P(both)
    matrix = P(both, None)
    tokens = P(None, "fsdp", "seq", None)
    weights = (row, row, matrix, row, matrix, row, matrix, row, matrix, row)
    grads = (row, row, matrix, row, row, matrix, row, matrix, row, matrix, row)
    return jax.shard_map(
        per_device,
        mesh=mesh,
        in_specs=(tokens,) + weights + (P(None, "fsdp", None), tokens),
        out_specs=(tokens, tokens) + grads,
        check_vma=False,
    )
```

```python
import functools
import math

import jax
import jax.numpy as jnp
import numpy as np
from jax import lax
from jax.experimental import pallas as pl
from jax.experimental.pallas import tpu as pltpu
from jax.sharding import PartitionSpec as P

HEADS = 32
HEAD_DIM = 64
ROT = 32
IMG = 256
PIECES = 2
EPSILON = 1e-05
BF = jnp.bfloat16
F32 = jnp.float32
SCALE = 1.0 / math.sqrt(HEAD_DIM)
LANES = 2 * HEAD_DIM


def swap(value, bit):
    size = lax.axis_size("seq")
    return lax.ppermute(value, "seq", [(i, i ^ bit) for i in range(size)])


def store_index(block):
    half = lax.axis_size("seq") // 2
    if isinstance(block, int):
        return block % 2 * half + block // 2
    return (block & 1) * half + (block >> 1)


def scatter_seq(terms):
    size = lax.axis_size("seq")
    me = lax.axis_index("seq")
    count = size.bit_length() - 1
    micro, _, length, width = terms.shape
    half = width // 2
    bits = list(range(1, count))

    def exchange(held, bit, axis):
        held = held.astype(BF)
        mine = (me >> bit) & 1
        away = lax.dynamic_index_in_dim(held, 1 - mine, axis, keepdims=False)
        kept = lax.dynamic_index_in_dim(held, mine, axis, keepdims=False)
        return kept.astype(F32) + swap(away, 1 << bit).astype(F32)

    sums = []
    for cols, order in ((slice(0, half), bits), (slice(half, width), bits[::-1])):
        held = terms[..., cols].reshape((micro,) + (2,) * count + (length, half))
        left = [0] + bits[::-1]
        for bit in [0] + order:
            held = exchange(held, bit, 1 + left.index(bit))
            left.remove(bit)
        sums.append(held)
    return jnp.concatenate(sums, axis=-1)


def attention_kernel(
    blocks,
    length,
    starts_ref,
    cos_ref,
    sin_ref,
    q_ref,
    k_ref,
    v_ref,
    do_ref,
    mixed_ref,
    dq_ref,
    dk_ref,
    dv_ref,
    q_s,
    k_s,
    v_s,
    do_s,
    dk_s,
    dv_s,
    bias_s,
):
    micro = pl.program_id(0)
    total = blocks * length
    tile = 256
    lane = lax.broadcasted_iota(jnp.int32, (1, LANES), 1)
    low_lane = (lane % HEAD_DIM) < (ROT // 2)

    def turn(value, cosine, sine):
        other = jnp.where(
            low_lane,
            pltpu.roll(value, LANES - ROT // 2, 1),
            pltpu.roll(value, ROT // 2, 1),
        )
        return value * cosine + other * sine

    for block in range(blocks):
        source = store_index(block)
        at = slice(block * length, (block + 1) * length)
        cosine, sine = cos_ref[at, :], sin_ref[at, :]
        q_s[at, :] = (turn(q_ref[0, source], cosine, sine)).astype(BF) * jnp.asarray(SCALE, BF)
        k_s[at, :] = turn(k_ref[0, source], cosine, sine).astype(BF)
        v_s[at, :] = v_ref[0, source].astype(BF)
        do_s[at, :] = do_ref[0, source]
    dk_s[...] = jnp.zeros_like(dk_s)
    dv_s[...] = jnp.zeros_like(dv_s)

    def label(positions):
        found = jnp.full(positions.shape, -1, jnp.int32)
        for piece in range(PIECES):
            start = starts_ref[micro, piece]
            found = jnp.where((positions >= start) & (positions < start + IMG), piece, found)
        return found

    for first in range(0, total, tile):
        last = min(total, first + tile + IMG)
        qpos = first + lax.broadcasted_iota(jnp.int32, (tile, 1), 0)
        kpos = first + lax.broadcasted_iota(jnp.int32, (1, last - first), 1)
        qlab, klab = label(qpos), label(kpos)
        allowed = (kpos <= qpos) | ((qlab == klab) & (qlab >= 0))
        bias_s[:, : last - first] = jnp.where(allowed, 0.0, -1e30)
        rows = slice(first, first + tile)
        keys = k_s[:last, :]
        values = v_s[:last, :]
        mixed = jnp.zeros((tile, LANES), F32)
        dq = jnp.zeros((tile, LANES), F32)
        for head in range(LANES // HEAD_DIM):
            mine = (lane // HEAD_DIM) == head
            q = jnp.where(mine, q_s[rows, :], 0)
            do = jnp.where(mine, do_s[rows, :], 0)
            dims = (((1,), (1,)), ((), ()))
            s = lax.dot_general(q, keys, dims, preferred_element_type=F32)
            if first:
                s = jnp.concatenate(
                    [s[:, :first], s[:, first:] + bias_s[:, : last - first]], axis=1
                )
            else:
                s = s + bias_s[:, : last - first]
            p = jnp.exp(s - jnp.max(s, axis=1, keepdims=True))
            p = p * (1.0 / jnp.sum(p, axis=1, keepdims=True))
            probs = p.astype(BF)
            att = jnp.dot(probs, values, preferred_element_type=F32)
            mixed = jnp.where(mine, att, mixed)
            dp = lax.dot_general(do, values, dims, preferred_element_type=F32)
            delta = jnp.sum(p * dp, axis=1, keepdims=True)
            ds = (p * (dp - delta)).astype(BF)
            dq = jnp.where(mine, jnp.dot(ds, keys, preferred_element_type=F32), dq)
            over = (((0,), (0,)), ((), ()))
            dk_s[:last, :] += lax.dot_general(ds, q, over, preferred_element_type=F32)
            dv_s[:last, :] += lax.dot_general(probs, do, over, preferred_element_type=F32)
        dq = dq * SCALE
        for part in range(tile // length):
            block = first // length + part
            here = slice(part * length, (part + 1) * length)
            at = slice(block * length, (block + 1) * length)
            mixed_ref[0, store_index(block)] = mixed[here].astype(BF)
            dq_ref[0, store_index(block)] = turn(dq[here], cos_ref[at, :], -sin_ref[at, :]).astype(BF)
    for block in range(blocks):
        at = slice(block * length, (block + 1) * length)
        dk_ref[0, store_index(block)] = turn(dk_s[at, :], cos_ref[at, :], -sin_ref[at, :]).astype(BF)
        dv_ref[0, store_index(block)] = dv_s[at, :].astype(BF)


def tables(total):
    half = ROT // 2
    frequency = (10000.0 ** (-2.0 * np.arange(half) / ROT)).astype(np.float32)
    angles = np.arange(total, dtype=np.float32)[:, None] * frequency[None, :]
    cosine, sine = np.cos(angles), np.sin(angles)
    ones = np.ones((total, HEAD_DIM - ROT), np.float32)
    cosine = np.concatenate([cosine, cosine, ones] * 2, axis=1)
    sine = np.concatenate([-sine, sine, 0 * ones] * 2, axis=1)
    return jnp.asarray(cosine), jnp.asarray(sine)


def attention(starts, projected, mixed_grad):
    micro, blocks, length, cols = mixed_grad.shape
    total = blocks * length
    groups = cols // LANES
    cosine, sine = tables(total)

    def spec(offset):
        return pl.BlockSpec(
            (1, blocks, length, LANES), lambda m, g, offset=offset: (m, 0, 0, offset * groups + g)
        )

    table = pl.BlockSpec((total, LANES), lambda m, g: (0, 0))
    shape = jax.ShapeDtypeStruct(mixed_grad.shape, BF)
    return pl.pallas_call(
        functools.partial(attention_kernel, blocks, length),
        grid=(micro, groups),
        in_specs=[
            pl.BlockSpec(memory_space=pltpu.SMEM),
            table,
            table,
            spec(0),
            spec(1),
            spec(2),
            spec(0),
        ],
        out_specs=[spec(0)] * 4,
        out_shape=[shape] * 4,
        scratch_shapes=[pltpu.VMEM((total, LANES), BF)] * 4
        + [pltpu.VMEM((total, LANES), F32)] * 2
        + [pltpu.VMEM((256, 512), F32)],
        compiler_params=pltpu.CompilerParams(vmem_limit_bytes=48 * 1024 * 1024),
        cost_estimate=pl.CostEstimate(
            flops=micro * groups * 40 * total * total * HEAD_DIM,
            bytes_accessed=micro * groups * total * LANES * 22,
            transcendentals=micro * groups * 2 * total * total,
        ),
    )(starts, cosine, sine, projected, projected, projected, mixed_grad)


MESH = pl.DeviceIdType.MESH


def remote(src, dst, send, recv, device):
    return pltpu.make_async_remote_copy(
        src_ref=src,
        dst_ref=dst,
        send_sem=send,
        recv_sem=recv,
        device_id=device,
        device_id_type=MESH,
    )


def greet(size, depth):
    me, at = lax.axis_index("seq"), lax.axis_index("fsdp")
    barrier = pltpu.get_barrier_semaphore()
    for step in range(1, size):
        pl.semaphore_signal(barrier, inc=1, device_id={"seq": me ^ step}, device_id_type=MESH)
    for step in range(1, depth):
        pl.semaphore_signal(
            barrier, inc=1, device_id={"fsdp": lax.rem(at + step, depth)}, device_id_type=MESH
        )
    pl.semaphore_wait(barrier, size + depth - 2)


class LineGather:
    def __init__(self, depth, source, target, send, recv):
        self.depth, self.source, self.target = depth, source, target
        self.send, self.recv = send, recv

    def copy(self, step, way):
        at = lax.axis_index("fsdp")
        origin = jnp.clip(at - way * (step - 1), 0, self.depth - 1)
        number = step * 2 + (way > 0)
        return remote(
            self.source(origin, step),
            self.target(origin),
            self.send.at[number],
            self.recv.at[number],
            {"fsdp": jnp.clip(at + way, 0, self.depth - 1)},
        )

    def sends(self, step, way):
        at = lax.axis_index("fsdp")
        origin = at - way * (step - 1)
        return (at + way >= 0) & (at + way < self.depth) & (origin >= 0) & (origin < self.depth)

    def start(self, step):
        for way in (1, -1):

            @pl.when(self.sends(step, way))
            def _():
                self.copy(step, way).start()

    def arrive(self, step):
        at = lax.axis_index("fsdp")
        for way in (1, -1):
            origin = at - way * step

            @pl.when((origin >= 0) & (origin < self.depth))
            def _():
                self.copy(step, way).wait_recv()

    def sent(self, step):
        for way in (1, -1):

            @pl.when(self.sends(step, way))
            def _():
                self.copy(step, way).wait_send()


class LineSum:
    def __init__(self, depth, chunk, landing, own, held, out, load, send, recv):
        self.depth, self.chunk, self.landing = depth, chunk, landing
        self.own, self.held, self.out = own, held, out
        self.load, self.send, self.recv = load, send, recv

    def place(self, way):
        at = lax.axis_index("fsdp")
        return at if way > 0 else self.depth - 1 - at

    def copy(self, step, way, src):
        number = step * 2 + (way > 0)
        at = lax.axis_index("fsdp")
        return remote(
            src,
            self.landing(step, way),
            self.send.at[number],
            self.recv.at[number],
            {"fsdp": jnp.clip(at + way, 0, self.depth - 1)},
        )

    def origin(self, step, way):
        away = jnp.clip(self.depth - step + self.place(way), 0, self.depth - 1)
        return away if way > 0 else self.depth - 1 - away

    def source(self, step):
        for way in (1, -1):

            @pl.when(self.place(way) == 0)
            def _():
                self.copy(step, way, self.chunk(self.origin(step, way))).start()

    def forward(self, step, here=True):
        for way in (1, -1):
            place = self.place(way)

            @pl.when((place >= 1) & (place <= step - 1) & (place < self.depth - 1))
            def _():
                mine = pltpu.make_async_copy(
                    self.chunk(self.origin(step, way)), self.own, self.load.at[0]
                )
                mine.start()
                if here:
                    self.copy(step - 1, way, self.out(step, way)).wait_recv()
                came = pltpu.make_async_copy(
                    self.landing(step - 1, way), self.held, self.load.at[1]
                )
                came.start()
                mine.wait()
                came.wait()
                target = self.out(step, way)
                target[...] = (self.own[...].astype(F32) + self.held[...].astype(F32)).astype(BF)
                self.copy(step, way, target).start()

    def arrive(self, step, consumed):
        for way in (1, -1):
            place = self.place(way)
            ok = (place >= 1) & (place <= step)
            if consumed:
                ok = ok & (place == self.depth - 1)

            @pl.when(ok)
            def _():
                self.copy(step, way, self.out(step, way)).wait_recv()

    def total(self, last, right, left):
        mine = pltpu.make_async_copy(self.chunk(lax.axis_index("fsdp")), self.own, self.load.at[0])
        mine.start()
        for way, target in ((1, right), (-1, left)):
            place = self.place(way)

            @pl.when(place >= 1)
            def _():
                self.copy(last, way, self.out(last, way)).wait_recv()
                came = pltpu.make_async_copy(self.landing(last, way), target, self.load.at[1])
                came.start()
                came.wait()

            @pl.when(place == 0)
            def _():
                target[...] = jnp.zeros_like(target)

        mine.wait()
        return self.own[...].astype(F32) + right[...].astype(F32) + left[...].astype(F32)

    def sent_first(self, step):
        for way in (1, -1):

            @pl.when(self.place(way) == 0)
            def _():
                self.copy(step, way, self.out(step, way)).wait_send()

    def sent_on(self, step):
        for way in (1, -1):
            place = self.place(way)

            @pl.when((place >= 1) & (place <= step - 1) & (place < self.depth - 1))
            def _():
                self.copy(step, way, self.out(step, way)).wait_send()

    def sent(self, step):
        self.sent_first(step)
        self.sent_on(step)


class SeqSum:
    def __init__(self, size, width, to_core, sums, coming, core_sems, axis_sems, base):
        self.size, self.width = size, width
        self.to_core, self.sums, self.coming = to_core, sums, coming
        self.core_sems, self.axis_sems, self.base = core_sems, axis_sems, base
        self.chips = size // 2
        self.bits = size.bit_length() - 2
        bits = list(range(self.bits))
        self.orders = (bits, bits[::-1])

    def core_copy(self):
        me = lax.axis_index("seq")
        send, recv = self.core_sems
        return remote(self.to_core, self.sums, send, recv, {"seq": me ^ 1})

    def away(self, terms):
        def write(columns, y):
            self.to_core[:, :, columns] = y.astype(BF)

        terms(1 - (lax.axis_index("seq") & 1), write)
        self.core_copy().start()

    def here(self, terms):
        self.core_copy().wait_recv()

        def write(columns, y):
            self.sums[:, :, columns] = (y + self.sums[:, :, columns].astype(F32)).astype(BF)

        terms(lax.axis_index("seq") & 1, write)
        self.start(0)

    def copies(self, part, stage):
        me = lax.axis_index("seq")
        half = self.width // 2
        bit = self.orders[part][stage]
        done = sum(1 << b for b in self.orders[part][:stage])
        first = self.chips - (self.chips >> stage)
        columns = slice(part * half, (part + 1) * half)
        send, recv = self.axis_sems
        found = []
        for mask in range(self.chips):
            if mask & (done | (1 << bit)):
                continue
            slot = first + len(found)
            number = self.base + part * (self.chips - 1) + slot
            copy = remote(
                self.sums.at[(me >> 1) ^ (mask | (1 << bit)), :, columns],
                self.coming.at[slot, :, columns],
                send.at[number],
                recv.at[number],
                {"seq": me ^ (2 << bit)},
            )
            found.append((mask, slot, copy))
        return found

    def start(self, stage):
        for part in range(2):
            for _, _, copy in self.copies(part, stage):
                copy.start()

    def add(self, stage):
        half = self.width // 2
        for part in range(2):
            columns = slice(part * half, (part + 1) * half)
            for mask, slot, copy in self.copies(part, stage):
                copy.wait_recv()
                if stage < self.bits - 1:
                    block = (lax.axis_index("seq") >> 1) ^ mask
                    self.sums[block, :, columns] = (
                        self.sums[block, :, columns].astype(F32)
                        + self.coming[slot, :, columns].astype(F32)
                    ).astype(BF)

    def step(self, stage):
        self.add(stage)
        if stage + 1 < self.bits:
            self.start(stage + 1)

    def last(self):
        chip = lax.axis_index("seq") >> 1
        return self.sums[chip].astype(F32) + self.coming[self.chips - 2].astype(F32)

    def core_sent(self):
        self.core_copy().wait_send()

    def sent(self):
        for part in range(2):
            for stage in range(self.bits):
                for _, _, copy in self.copies(part, stage):
                    copy.wait_send()


def load_kernel(
    dims,
    tokens_ref,
    up_ref,
    one_ref,
    two_ref,
    vec_ref,
    normed_ref,
    all_up_ref,
    my_one_ref,
    my_two_ref,
    full_ref,
    gathered,
    normed_v,
    vec_seq,
    vec_sum,
    vec_all,
    local_sem,
    vec_send,
    vec_recv,
    a2a_send,
    a2a_recv,
    line_send,
    line_recv,
    row_send,
    row_recv,
):
    size, depth, micro, length, width, units, cols = dims
    me, at = lax.axis_index("seq"), lax.axis_index("fsdp")
    count = size.bit_length() - 1
    half = width // 2

    def seq(step):
        return {"seq": me ^ step}

    def line(step):
        return {"fsdp": lax.rem(at + step, depth)}

    greet(size, depth)

    def vec_seq_copy(step):
        return remote(
            vec_sum.at[step],
            vec_seq.at[step],
            vec_send.at[step],
            vec_recv.at[step],
            seq(1 << step),
        )

    def vec_line_copy(step):
        number = size + step
        return remote(
            vec_sum.at[count], vec_all.at[step], vec_send.at[number], vec_recv.at[number], line(step)
        )

    def one_copy(step):
        peer = me ^ step
        return remote(
            one_ref.at[:, pl.ds(pl.multiple_of(peer * units, 128), units)],
            my_one_ref.at[me, at],
            a2a_send.at[step],
            a2a_recv.at[step],
            seq(step),
        )

    local = [
        pltpu.make_async_copy(
            one_ref.at[:, pl.ds(pl.multiple_of(me * units, 128), units)],
            my_one_ref.at[me, at],
            local_sem.at[0],
        ),
        pltpu.make_async_copy(
            tokens_ref,
            gathered.at[:, store_index(me)],
            local_sem.at[1],
        ),
        pltpu.make_async_copy(
            up_ref,
            all_up_ref.at[:, store_index(me)],
            local_sem.at[2],
        ),
    ]
    local.append(pltpu.make_async_copy(two_ref, my_two_ref.at[at], local_sem.at[3]))

    def one_line(step, way):
        origin = jnp.clip(at - way * (step - 1), 0, depth - 1)
        number = 2 * step + (way > 0)
        piece = my_one_ref.at[:, origin]
        ok = (at + way >= 0) & (at + way < depth)
        ok = ok & (at - way * (step - 1) >= 0) & (at - way * (step - 1) < depth)
        return ok, remote(
            piece,
            piece,
            line_send.at[number],
            line_recv.at[number],
            {"fsdp": jnp.clip(at + way, 0, depth - 1)},
        )

    def one_arrives(step, way):
        ok = (at - way * step >= 0) & (at - way * step < depth)
        return ok, one_line(step, way)[1]

    def two_line(way):
        ok = (at + way >= 0) & (at + way < depth)
        number = way > 0
        return ok, remote(
            two_ref,
            my_two_ref.at[at],
            line_send.at[int(number)],
            line_recv.at[int(number)],
            {"fsdp": jnp.clip(at + way, 0, depth - 1)},
        )

    def two_arrives(way):
        return (at - way >= 0) & (at - way < depth), two_line(way)[1]

    def start(pair):
        ok, copy = pair

        @pl.when(ok)
        def _():
            copy.start()

    def wait_recv(pair):
        ok, copy = pair

        @pl.when(ok)
        def _():
            copy.wait_recv()

    def wait_send(pair):
        ok, copy = pair

        @pl.when(ok)
        def _():
            copy.wait_send()

    sources = (tokens_ref, up_ref)
    targets = (gathered, all_up_ref)
    orders = (list(range(1, count)), list(range(1, count))[::-1])

    def row_copy(which, part, mask, bit):
        columns = slice(part * half, (part + 1) * half)
        block = store_index(me ^ mask)
        if mask == 0:
            src = sources[which].at[:, :, columns]
        else:
            src = targets[which].at[:, block, :, columns]
        number = (which * 2 + part) * size + (mask | (1 << bit))
        return remote(
            src,
            targets[which].at[:, block, :, columns],
            row_send.at[number],
            row_recv.at[number],
            seq(1 << bit),
        )

    def row_stage(which, part, stage):
        order = orders[part]
        masks = [0]
        for bit in order[:stage]:
            masks = masks + [mask | (1 << bit) for mask in masks]
        return [row_copy(which, part, mask, order[stage]) for mask in masks]

    def row_cores(which, part, stage):
        order = orders[part]
        masks = [0]
        new = [0]
        for bit in order[: stage + 1]:
            new = [mask | (1 << bit) for mask in masks]
            masks = masks + new
        return [row_copy(which, part, mask, 0) for mask in new]

    def both_parts(function, which, stage):
        return function(which, 0, stage) + function(which, 1, stage)

    def issue(copies):
        for copy in copies:
            copy.start()

    def arrive(copies):
        for copy in copies:
            copy.wait_recv()

    def vec_stage(step):
        vec_seq_copy(step).wait_recv()
        total = vec_sum[step].astype(F32) + vec_seq[step].astype(F32)
        vec_sum[step + 1] = total.astype(BF)

    issue(one_copy(step) for step in range(1, size))
    for way in (1, -1):
        start(two_line(way))
    issue(local)
    vec_sum[0] = vec_ref[...]
    vec_seq_copy(0).start()
    issue(both_parts(row_cores, 0, -1))
    vec_stage(0)
    vec_seq_copy(1).start()
    arrive(one_copy(step) for step in range(1, size))
    local[0].wait()
    for way in (1, -1):
        start(one_line(1, way))
    for which in range(2):
        issue(both_parts(row_stage, which, 0))
    for step in range(1, count):
        vec_stage(step)
        if step + 1 < count:
            vec_seq_copy(step + 1).start()
    issue(vec_line_copy(step) for step in range(1, depth))

    def line_on(step):
        for way in (1, -1):
            wait_recv(one_arrives(step, way))
            start(one_line(step + 1, way))

    line_step = 1
    for stage in range(count - 1):
        for which in range(2):
            arrive(both_parts(row_stage, which, stage))
            if stage + 1 < count - 1:
                issue(both_parts(row_stage, which, stage + 1))
            issue(both_parts(row_cores, which, stage))
            if stage == 0 and which == 0:
                issue(both_parts(row_cores, 1, -1))
                arrive(vec_line_copy(step) for step in range(1, depth))
                summed = vec_sum[count].astype(F32)
                for step in range(1, depth):
                    summed = summed + vec_all[step].astype(F32)
                full_ref[...] = summed
            elif which == 0 or stage == 0:
                if line_step < depth - 1:
                    line_on(line_step)
                    line_step += 1
            if stage == count - 2 and which == 0:
                while line_step < depth - 1:
                    line_on(line_step)
                    line_step += 1
                local[1].wait()
                for step in range(-1, count - 1):
                    arrive(both_parts(row_cores, 0, step))
                gain = full_ref[0:1, :]
                shift = full_ref[1:2, :]

                @pl.loop(0, micro * size)
                def _(index):
                    m, block = index // size, lax.rem(index, size)
                    x = gathered[m, block].astype(F32)
                    center = x - jnp.mean(x, axis=-1, keepdims=True)
                    spread = jnp.mean(center * center, axis=-1, keepdims=True)
                    y = center * lax.rsqrt(spread + EPSILON) * gain + shift
                    normed_v[m, block] = y.astype(BF)

                normed_out = pltpu.make_async_copy(normed_v, normed_ref, local_sem.at[4])
                normed_out.start()

    for copy in local[2:]:
        copy.wait()
    normed_out.wait()
    for stage in range(-1, count - 1):
        arrive(both_parts(row_cores, 1, stage))
    for way in (1, -1):
        wait_recv(two_arrives(way))
        wait_recv(one_arrives(depth - 1, way))

    for step in range(count):
        vec_seq_copy(step).wait_send()
    for step in range(1, size):
        one_copy(step).wait_send()
    for step in range(1, depth):
        vec_line_copy(step).wait_send()
        for way in (1, -1):
            wait_send(one_line(step, way))
    for way in (1, -1):
        wait_send(two_line(way))
    for which in range(2):
        for stage in range(-1, count - 1):
            for copy in both_parts(row_cores, which, stage):
                copy.wait_send()
            if stage >= 0:
                for copy in both_parts(row_stage, which, stage):
                    copy.wait_send()


def load_all(tokens, upstream, w_fc1, w_fc2, vectors):
    size, depth = lax.axis_size("seq"), lax.axis_size("fsdp")
    micro, length, width = tokens.shape
    rows, units, cols = w_fc1.shape[0], w_fc1.shape[1] // size, width // size
    dims = (size, depth, micro, length, width, units, cols)
    hbm = pl.BlockSpec(memory_space=pl.ANY)
    vmem = pl.BlockSpec(memory_space=pltpu.VMEM)
    gathered = (micro, size, length, width)
    dma = pltpu.SemaphoreType.DMA
    return pl.pallas_call(
        functools.partial(load_kernel, dims),
        in_specs=[hbm] * 4 + [vmem],
        out_specs=[hbm] * 4 + [vmem],
        out_shape=[
            jax.ShapeDtypeStruct(gathered, BF),
            jax.ShapeDtypeStruct(gathered, BF),
            jax.ShapeDtypeStruct((size, depth, rows, units), BF),
            jax.ShapeDtypeStruct((depth,) + w_fc2.shape, BF),
            jax.ShapeDtypeStruct(vectors.shape, F32),
        ],
        scratch_shapes=[
            pltpu.VMEM(gathered, BF),
            pltpu.VMEM(gathered, BF),
            pltpu.VMEM((size,) + vectors.shape, BF),
            pltpu.VMEM((size,) + vectors.shape, BF),
            pltpu.VMEM((depth,) + vectors.shape, BF),
            dma((5,)),
            dma((size + depth,)),
            dma((size + depth,)),
            dma((size,)),
            dma((size,)),
            dma((2 * depth + 2,)),
            dma((2 * depth + 2,)),
            dma((4 * size,)),
            dma((4 * size,)),
        ],
        compiler_params=pltpu.CompilerParams(
            collective_id=1, has_side_effects=True, vmem_limit_bytes=60 * 1024 * 1024
        ),
        cost_estimate=pl.CostEstimate(
            flops=1000, bytes_accessed=300 * 1000 * 1000, transcendentals=0
        ),
    )(tokens, upstream, w_fc1, w_fc2, vectors)


def ffn_kernel(
    dims,
    normed_hbm,
    up_hbm,
    one_hbm,
    two_hbm,
    qkv_hbm,
    out_hbm,
    full_ref,
    part_grad_hbm,
    part_act_hbm,
    attn_hbm,
    grad_two_hbm,
    grad_one_hbm,
    land_two,
    land_one,
    bone_ref,
    btwo_ref,
    normed_v,
    up_v,
    one_v,
    two_v,
    hidden_v,
    pre_v,
    grad_two_v,
    grad_one_v,
    own_one,
    held_one,
    out_one,
    load_sem,
    line_load,
    store_sem,
    two_send,
    two_recv,
    attn_send,
    attn_recv,
    sum_two_send,
    sum_two_recv,
    sum_one_send,
    sum_one_recv,
    a2a_send,
    a2a_recv,
    local_sem,
):
    size, depth, micro, length, width, units, cols = dims
    me, at = lax.axis_index("seq"), lax.axis_index("fsdp")
    count = micro * size * length
    per = width // size
    tile = 512
    group = units // depth

    loads = [
        pltpu.make_async_copy(src, dst, load_sem.at[n])
        for n, (src, dst) in enumerate(
            ((normed_hbm, normed_v), (one_hbm, one_v), (up_hbm, up_v))
        )
    ]
    for load in loads:
        load.start()

    def two_load(way):
        origin = jnp.clip(at + way, 0, depth - 1)
        return (at + way >= 0) & (at + way < depth), pltpu.make_async_copy(
            two_hbm.at[origin], two_v.at[origin], load_sem.at[4 + way]
        )

    for way in (0, 1, -1):
        ok, copy = two_load(way)

        @pl.when(ok)
        def _():
            copy.start()

    def qkv_part(peer, part):
        return qkv_hbm.at[:, pl.ds(pl.multiple_of(part * width + peer * cols, 128), cols)]

    def qkv_copy(step, part):
        number = part * size + step
        return remote(
            qkv_part(me ^ step, part),
            attn_hbm.at[me, at, :, pl.ds(part * cols, cols)],
            a2a_send.at[number],
            a2a_recv.at[number],
            {"seq": me ^ step},
        )

    local = [
        pltpu.make_async_copy(
            qkv_part(me, part), attn_hbm.at[me, at, :, pl.ds(part * cols, cols)], local_sem.at[part]
        )
        for part in range(3)
    ] + [
        pltpu.make_async_copy(
            out_hbm.at[:, pl.ds(peer * cols, cols)],
            attn_hbm.at[peer, at, :, pl.ds(3 * cols, cols)],
            local_sem.at[3 + peer],
        )
        for peer in range(size)
    ]
    for copy in local:
        copy.start()
    greet(size, depth)

    two = LineGather(
        depth,
        lambda o, step: two_hbm.at[o] if step == 2 else two_v.at[o],
        lambda o: two_v.at[o],
        two_send,
        two_recv,
    )
    attn = LineGather(
        depth,
        lambda o, step: attn_hbm.at[:, o],
        lambda o: attn_hbm.at[:, o],
        attn_send,
        attn_recv,
    )
    sum_two = LineSum(
        depth,
        lambda o: grad_two_v.at[o],
        lambda step, way: land_two.at[int(way > 0)],
        own_one,
        held_one,
        lambda step, way: grad_two_v.at[0],
        line_load,
        sum_two_send,
        sum_two_recv,
    )
    sum_one = LineSum(
        depth,
        lambda o: grad_one_v.at[:, o],
        lambda step, way: land_one.at[(step - 1) * 2 + (way > 0)],
        own_one,
        held_one,
        lambda step, way: out_one.at[int(way > 0)],
        line_load,
        sum_one_send,
        sum_one_recv,
    )
    two.start(2)
    for part in range(3):
        for step in range(1, size):
            qkv_copy(step, part).start()

    for load in loads[:2]:
        load.wait()
    root = math.sqrt(2.0 / math.pi)
    flat = me * units
    bias_row = 6 + flat // width
    bias_at = pl.multiple_of(lax.rem(flat, width), units)
    bias = full_ref[pl.ds(bias_row, 1), pl.ds(bias_at, units)]
    bone_ref[...] = bias

    @pl.loop(0, count // tile)
    def _(r):
        rows = pl.ds(pl.multiple_of(r * tile, tile), tile)
        a = normed_v[rows, :]
        for o in range(depth):
            columns = slice(o * group, (o + 1) * group)
            w = one_v[:, :, :, columns].reshape(width, group)
            v = jnp.dot(a, w, preferred_element_type=F32) + bone_ref[:, columns]
            square = v * v
            t = jnp.tanh(root * v * (1.0 + 0.044715 * square))
            hidden_v[rows, columns] = (0.5 * v * (1.0 + t)).astype(BF)
            slope = 0.5 * (1.0 + t) + 0.5 * root * v * (1.0 - t * t) * (
                1.0 + 3 * 0.044715 * square
            )
            pre_v[rows, columns] = slope.astype(BF)

    loads[2].wait()
    over_first = (((0,), (0,)), ((), ()))
    over_last = (((1,), (1,)), ((), ()))

    @pl.loop(0, depth)
    def _(o):
        columns = pl.ds(pl.multiple_of(o * group, group), group)
        y = lax.dot_general(hidden_v[:, columns], up_v[...], over_first, preferred_element_type=F32)
        grad_two_v[o] = y.astype(BF)

    two.arrive(2)
    two.start(3)
    sum_two.source(1)
    grad_two_out = pltpu.make_async_copy(grad_two_v, grad_two_hbm, store_sem.at[2])
    grad_two_out.start()
    bone_ref[...] = jnp.zeros_like(bone_ref)

    def piece(o):
        columns = pl.ds(pl.multiple_of(o * group, group), group)

        @pl.loop(0, count // tile)
        def _(r):
            rows = pl.ds(pl.multiple_of(r * tile, tile), tile)
            y = lax.dot_general(up_v[rows, :], two_v[o], over_last, preferred_element_type=F32)
            y = (y * pre_v[rows, columns].astype(F32)).astype(BF)
            pre_v[rows, columns] = y
            bone_ref[:, columns] += jnp.sum(y.astype(F32), axis=0, keepdims=True)

        wide = 1024

        @pl.loop(0, width // wide)
        def _(d):
            rows = pl.ds(pl.multiple_of(d * wide, wide), wide)
            y = lax.dot_general(
                normed_v[:, rows], pre_v[:, columns], over_first, preferred_element_type=F32
            )
            n = wide // per
            y = y.astype(BF).reshape(n, depth, per // depth, group)
            grad_one_v[pl.ds(d * n, n), :, :, columns] = y

    for way in (0, 1, -1):
        ok, copy = two_load(way)

        @pl.when(ok)
        def _():
            copy.wait()

    @pl.loop(0, 2 * depth - 3)
    def _(number):
        distance = (number + 1) // 2
        origin = jnp.where(lax.rem(number, 2) == 1, at - distance, at + distance)

        @pl.when((origin >= 0) & (origin < depth))
        def _():
            piece(jnp.clip(origin, 0, depth - 1))

    for copy in local:
        copy.wait()
    for part in range(3):
        for step in range(1, size):
            qkv_copy(step, part).wait_recv()
    two.arrive(3)
    attn.start(1)

    @pl.loop(2 * depth - 3, 2 * depth - 1)
    def _(number):
        distance = (number + 1) // 2
        origin = jnp.where(lax.rem(number, 2) == 1, at - distance, at + distance)

        @pl.when((origin >= 0) & (origin < depth))
        def _():
            piece(jnp.clip(origin, 0, depth - 1))

    sum_one.source(1)
    sum_one.source(2)
    grad_one_out = pltpu.make_async_copy(grad_one_v, grad_one_hbm, store_sem.at[5])
    grad_one_out.start()

    btwo_ref[...] = jnp.zeros_like(btwo_ref)
    for m in range(micro):
        mine = pl.multiple_of((m * size + store_index(me)) * length, length)
        rows = up_v[pl.ds(mine, length), :].astype(F32)
        btwo_ref[...] += jnp.sum(rows, axis=0, keepdims=True)

    @pl.loop(0, count // tile)
    def _(r):
        rows = pl.ds(pl.multiple_of(r * tile, tile), tile)
        a = pre_v[rows, :]
        for s in range(size):
            w = one_v[s].reshape(per, units)
            y = lax.dot_general(a, w, over_last, preferred_element_type=F32)
            normed_v[rows, s * per : (s + 1) * per] = y.astype(BF)

    part_grad = pltpu.make_async_copy(normed_v, part_grad_hbm, store_sem.at[3])
    part_grad.start()
    attn.arrive(1)
    attn.start(2)

    @pl.loop(0, count // tile)
    def _(r):
        rows = pl.ds(pl.multiple_of(r * tile, tile), tile)
        a = hidden_v[rows, :]
        for s in range(size):
            columns = slice(s * per, (s + 1) * per)
            w = two_v[:, :, columns].reshape(units, per)
            up_v[rows, columns] = jnp.dot(a, w, preferred_element_type=F32).astype(BF)

    part_act = pltpu.make_async_copy(up_v, part_act_hbm, store_sem.at[4])
    part_act.start()
    attn.arrive(2)
    attn.start(3)
    sum_one.forward(2)
    grad_two_out.wait()
    for store in (grad_one_out, part_grad, part_act):
        store.wait()
    attn.arrive(3)
    sum_two.arrive(1, False)
    sum_one.arrive(1, True)
    sum_one.arrive(2, False)
    for step in (2, 3):
        two.sent(step)
    for step in (1, 2, 3):
        attn.sent(step)
    sum_two.sent(1)
    sum_one.sent(1)
    sum_one.sent(2)
    for part in range(3):
        for step in range(1, size):
            qkv_copy(step, part).wait_send()


def feed_forward(normed, up, one, two, w_qkv, w_out, full):
    size, depth = lax.axis_size("seq"), lax.axis_size("fsdp")
    micro, _, length, width = normed.shape
    units, cols = one.shape[-1], width // size
    rows = width // (size * depth)
    count = micro * size * length
    dims = (size, depth, micro, length, width, units, cols)
    hbm = pl.BlockSpec(memory_space=pl.ANY)
    vmem = pl.BlockSpec(memory_space=pltpu.VMEM)
    dma = pltpu.SemaphoreType.DMA
    sums = dma((2 * depth,))
    shape = jax.ShapeDtypeStruct
    tall, deep = (depth, units // depth, width), (size, depth, rows, units)
    return pl.pallas_call(
        functools.partial(ffn_kernel, dims),
        in_specs=[hbm] * 6 + [vmem],
        out_specs=[hbm] * 7 + [vmem] * 2,
        out_shape=[
            shape((count, width), BF),
            shape((count, width), BF),
            shape((size, depth, rows, 4 * cols), BF),
            shape(tall, BF),
            shape(deep, BF),
            shape((2,) + tall[1:], BF),
            shape((4, size, rows, units), BF),
            shape((1, units), F32),
            shape((1, width), F32),
        ],
        scratch_shapes=[
            pltpu.VMEM((count, width), BF),
            pltpu.VMEM((count, width), BF),
            pltpu.VMEM(deep, BF),
            pltpu.VMEM(tall, BF),
            pltpu.VMEM((count, units), BF),
            pltpu.VMEM((count, units), BF),
            pltpu.VMEM(tall, BF),
            pltpu.VMEM(deep, BF),
            pltpu.VMEM((size, rows, units), BF),
            pltpu.VMEM((size, rows, units), BF),
            pltpu.VMEM((2, size, rows, units), BF),
            dma((6,)),
            dma((2,)),
            dma((6,)),
        ]
        + [sums] * 8
        + [dma((3 * size,)), dma((3 * size,)), dma((3 + size,))],
        compiler_params=pltpu.CompilerParams(
            collective_id=2, has_side_effects=True, vmem_limit_bytes=60 * 1024 * 1024
        ),
        cost_estimate=pl.CostEstimate(
            flops=34 * 1000**3, bytes_accessed=300 * 1000 * 1000, transcendentals=0
        ),
    )(
        normed.reshape(count, width),
        up.reshape(count, width),
        one,
        two,
        w_qkv,
        w_out,
        full,
    )


def attn_layer_kernel(
    dims,
    starts_ref,
    cos_ref,
    sin_ref,
    normed_hbm,
    up_hbm,
    attn_hbm,
    grad_two_hbm,
    grad_one_hbm,
    old_two,
    old_one,
    part_act_hbm,
    tokens_hbm,
    full_ref,
    turned_hbm,
    mixed_hbm,
    grads_hbm,
    spread_hbm,
    land_two,
    land_one,
    bqkv_ref,
    two_ref,
    act_ref,
    normed_v,
    up_v,
    attn_v,
    natural_v,
    turned_v,
    mixed_v,
    grads_v,
    dk_s,
    dv_s,
    bias_s,
    own_two,
    held_two,
    out_two,
    one_total,
    held_one,
    part_act_v,
    tokens_v,
    to_core,
    act_sums,
    act_coming,
    load_sem,
    line_load,
    store_sem,
    sum_two_send,
    sum_two_recv,
    sum_one_send,
    sum_one_recv,
    a2a_send,
    a2a_recv,
    core_sem,
    axis_send,
    axis_recv,
):
    size, depth, micro, length, width, units, cols = dims
    me = lax.axis_index("seq")
    chips = size // 2
    groups = cols // LANES
    total = size * length
    count = micro * total
    per = width // size
    loads = [
        pltpu.make_async_copy(src, dst, load_sem.at[n])
        for n, (src, dst) in enumerate(
            ((normed_hbm, normed_v), (attn_hbm, attn_v), (up_hbm, up_v))
        )
    ]
    for load in loads:
        load.start()
    greet(size, depth)
    sum_two = LineSum(
        depth,
        lambda o: grad_two_hbm.at[o],
        lambda step, way: (
            old_two.at[int(way > 0)] if step < 2 else land_two.at[(step - 2) * 2 + (way > 0)]
        ),
        own_two,
        held_two,
        lambda step, way: out_two.at[int(way > 0)],
        line_load,
        sum_two_send,
        sum_two_recv,
    )
    sum_one = LineSum(
        depth,
        lambda o: grad_one_hbm.at[:, o],
        lambda step, way: (
            old_one.at[(step - 1) * 2 + (way > 0)] if step < 3 else land_one.at[int(way > 0)]
        ),
        one_total,
        held_one.at[0],
        lambda step, way: held_one.at[1 + (way > 0)],
        line_load,
        sum_one_send,
        sum_one_recv,
    )
    sum_one.source(3)
    sum_two.source(2)
    sum_two.source(3)
    sum_one.forward(3, here=False)
    sum_two.forward(2, here=False)
    tokens_load = pltpu.make_async_copy(tokens_hbm.at[0], tokens_v, load_sem.at[4])
    tokens_load.start()

    def part_act_half(parity):
        blocks = pl.ds(parity * chips, chips)
        return pltpu.make_async_copy(part_act_hbm.at[0, blocks], part_act_v, load_sem.at[3])

    part_act_half(1 - (me & 1)).start()

    def spread_copy(step):
        peer = me ^ step
        return remote(
            one_total.at[peer],
            spread_hbm.at[me],
            a2a_send.at[step],
            a2a_recv.at[step],
            {"seq": peer},
        )

    spread_mine = pltpu.make_async_copy(one_total.at[me], spread_hbm.at[me], store_sem.at[3])
    act = SeqSum(
        size,
        width,
        to_core,
        act_sums,
        act_coming,
        (core_sem.at[0], core_sem.at[1]),
        (axis_send, axis_recv),
        0,
    )

    def act_terms(parity, write):
        first = pl.multiple_of(parity * chips * length, chips * length)
        mine = mixed_v[pl.ds(first, chips * length), :]

        @pl.loop(0, size)
        def _(s):
            columns = pl.ds(pl.multiple_of(s * per, per), per)
            w = attn_v[s, :, :, 3 * cols :].reshape(cols, cols)
            y = jnp.dot(mine, w, preferred_element_type=F32).reshape(chips, length, per)
            write(columns, y + part_act_v[:, :, columns].astype(F32))

    for load in loads:
        load.wait()

    lane = lax.broadcasted_iota(jnp.int32, (1, LANES), 1)
    low_lane = (lane % HEAD_DIM) < (ROT // 2)
    over_first = (((0,), (0,)), ((), ()))
    over_last = (((1,), (1,)), ((), ()))

    def turn(value, cosine, sine):
        other = jnp.where(
            low_lane,
            pltpu.roll(value, LANES - ROT // 2, 1),
            pltpu.roll(value, ROT // 2, 1),
        )
        return value * cosine + other * sine

    high = chips * length

    @pl.loop(0, micro * 2)
    def _(r):
        m, parity = r // 2, lax.rem(r, 2)
        rows = pl.ds(pl.multiple_of(r * high, high), high)
        a = normed_v[rows, :]
        u = up_v[rows, :]
        for part in range(3):
            w = attn_v[:, :, :, part * cols : (part + 1) * cols].reshape(width, cols)
            y = jnp.dot(a, w, preferred_element_type=F32)
            y = y + full_ref[2 + part : 3 + part, pl.ds(pl.multiple_of(me * cols, cols), cols)]
            for block in range(chips):
                at = pl.ds(pl.multiple_of((block * 2 + parity) * length, length), length)
                cosine, sine = cos_ref[at, :], sin_ref[at, :]
                for g in range(groups):
                    v = y[block * length : (block + 1) * length, g * LANES : (g + 1) * LANES]
                    if part < 2:
                        v = turn(v, cosine, sine)
                    v = v.astype(BF)
                    if part == 0:
                        v = v * jnp.asarray(SCALE, BF)
                    natural_v[part, m, g, at, :] = v
        y = jnp.zeros((high, cols), F32)
        for s in range(size):
            w = attn_v[s, :, :, 3 * cols :].reshape(cols, cols)
            y = y + lax.dot_general(
                u[:, s * per : (s + 1) * per], w, over_last, preferred_element_type=F32
            )
        for block in range(chips):
            at = pl.ds(pl.multiple_of((block * 2 + parity) * length, length), length)
            for g in range(groups):
                v = y[block * length : (block + 1) * length, g * LANES : (g + 1) * LANES]
                natural_v[3, m, g, at, :] = v.astype(BF)

    tile = 256

    @pl.loop(0, micro * groups)
    def _(index):
        m, g = index // groups, lax.rem(index, groups)

        @pl.when(index == 2)
        def _():
            sum_one.sent(3)
            total = sum_one.total(3, held_one.at[0], held_one.at[1])
            one_total[...] = total.astype(BF)
            for step in range(1, size):
                spread_copy(step).start()
            spread_mine.start()
            tokens_load.wait()

        @pl.when(index == groups)
        def _():
            part_act_half(1 - (me & 1)).wait()
            act.away(act_terms)
            part_act_half(me & 1).start()

        @pl.when(index == micro * groups - 1)
        def _():
            part_act_half(me & 1).wait()
            act.here(act_terms)
            sum_two.sent_on(2)
            sum_two.forward(3)

        def label(positions):
            found = jnp.full(positions.shape, -1, jnp.int32)
            for piece in range(PIECES):
                start = starts_ref[m, piece]
                found = jnp.where((positions >= start) & (positions < start + IMG), piece, found)
            return found

        def put(target, at, columns, value):
            for part in range(value.shape[0] // length):
                block = at // length + part
                rows = m * total + store_index(block) * length
                target[pl.ds(pl.multiple_of(rows, length), length), columns] = value[
                    part * length : (part + 1) * length
                ].astype(BF)

        def columns_of(part):
            return pl.ds(pl.multiple_of(part * cols + g * LANES, LANES), LANES)

        dk_s[...] = jnp.zeros_like(dk_s)
        dv_s[...] = jnp.zeros_like(dv_s)
        for first in range(0, total, tile):
            last = min(total, first + tile + IMG)
            qpos = first + lax.broadcasted_iota(jnp.int32, (tile, 1), 0)
            kpos = first + lax.broadcasted_iota(jnp.int32, (1, last - first), 1)
            qlab, klab = label(qpos), label(kpos)
            allowed = (kpos <= qpos) | ((qlab == klab) & (qlab >= 0))
            bias_s[:, : last - first] = jnp.where(allowed, 0.0, -1e30)
            rows = slice(first, first + tile)
            keys = natural_v[1, m, g, :last, :]
            values = natural_v[2, m, g, :last, :]
            heads = [(lane // HEAD_DIM) == head for head in range(LANES // HEAD_DIM)]
            q = jnp.concatenate([jnp.where(h, natural_v[0, m, g, rows, :], 0) for h in heads])
            do = jnp.concatenate([jnp.where(h, natural_v[3, m, g, rows, :], 0) for h in heads])
            s = lax.dot_general(q, keys, over_last, preferred_element_type=F32)
            bias = jnp.concatenate([bias_s[:, : last - first]] * len(heads))
            if first:
                s = jnp.concatenate([s[:, :first], s[:, first:] + bias], axis=1)
            else:
                s = s + bias
            p = jnp.exp(s - jnp.max(s, axis=1, keepdims=True))
            p = p * (1.0 / jnp.sum(p, axis=1, keepdims=True))
            probs = p.astype(BF)
            dp = lax.dot_general(do, values, over_last, preferred_element_type=F32)
            att = jnp.dot(probs, values, preferred_element_type=F32)
            delta = jnp.sum(p * dp, axis=1, keepdims=True)
            ds = (p * (dp - delta)).astype(BF)
            mixed = jnp.where(heads[0], att[:tile], att[tile:])
            dq = jnp.dot(ds, keys, preferred_element_type=F32)
            dq = jnp.where(heads[0], dq[:tile], dq[tile:])
            dk_s[:last, :] += lax.dot_general(ds, q, over_first, preferred_element_type=F32)
            dv_s[:last, :] += lax.dot_general(probs, do, over_first, preferred_element_type=F32)
            put(mixed_v, first, pl.ds(pl.multiple_of(g * LANES, LANES), LANES), mixed)
            dq = turn(dq * SCALE, cos_ref[rows, :], -sin_ref[rows, :])
            put(turned_v, first, columns_of(0), dq)
        put(turned_v, 0, columns_of(1), turn(dk_s[...], cos_ref[...], -sin_ref[...]))
        put(turned_v, 0, columns_of(2), dv_s[...])

    stores = [
        pltpu.make_async_copy(turned_v, turned_hbm, store_sem.at[0]),
        pltpu.make_async_copy(mixed_v, mixed_hbm, store_sem.at[1]),
    ]
    for store in stores:
        store.start()
    bits = size.bit_length() - 2
    for stage in range(bits - 1):
        act.step(stage)

    wide = 512

    @pl.loop(0, width // wide)
    def _(d):
        rows = pl.ds(pl.multiple_of(d * wide, wide), wide)
        y = lax.dot_general(normed_v[:, rows], turned_v[...], over_first, preferred_element_type=F32)
        n = wide // per
        grads_v[pl.ds(d * n, n), :, :, : 3 * cols] = y.astype(BF).reshape(
            n, depth, per // depth, 3 * cols
        )
        y = lax.dot_general(mixed_v[...], up_v[:, rows], over_first, preferred_element_type=F32)
        y = y.astype(BF)
        for k in range(n):
            grads_v[d * n + k, :, :, 3 * cols :] = y[:, k * per : (k + 1) * per].reshape(
                depth, cols // depth, per
            )

    grads_out = pltpu.make_async_copy(grads_v, grads_hbm, store_sem.at[2])
    grads_out.start()
    bqkv_ref[...] = jnp.sum(turned_v[...].astype(F32), axis=0, keepdims=True)
    act.add(bits - 1)
    bias = full_ref[5:6, :] + full_ref[6 + size * units // width : 7 + size * units // width, :]
    act_ref[...] = (tokens_v[...].astype(F32) + act.last() + bias).astype(BF)
    sum_two.sent_first(2)
    sum_two.sent(3)
    two_ref[...] = sum_two.total(3, held_two, out_two.at[0])
    for store in stores:
        store.wait()
    grads_out.wait()
    spread_mine.wait()
    for step in range(1, size):
        spread_copy(step).wait_recv()
        spread_copy(step).wait_send()
    act.core_sent()
    act.sent()


def attention_layer(
    starts, normed, up, attn, grad_two, grad_one, old_two, old_one, part_act, tokens, full
):
    size, depth, rows, units = grad_one.shape
    micro, _, length, width = normed.shape
    cols = width // size
    count, total = micro * size * length, size * length
    dims = (size, depth, micro, length, width, units, cols)
    cosine, sine = tables(total)
    chips = size // 2
    hbm = pl.BlockSpec(memory_space=pl.ANY)
    vmem = pl.BlockSpec(memory_space=pltpu.VMEM)
    dma = pltpu.SemaphoreType.DMA
    sums = dma((2 * depth,))
    shape = jax.ShapeDtypeStruct
    tall, deep = (units // depth, width), (size, rows, units)
    return pl.pallas_call(
        functools.partial(attn_layer_kernel, dims),
        in_specs=[pl.BlockSpec(memory_space=pltpu.SMEM)] + [vmem] * 2 + [hbm] * 9 + [vmem],
        out_specs=[hbm] * 6 + [vmem] * 3,
        out_shape=[
            shape((count, 3 * cols), BF),
            shape((count, cols), BF),
            shape(attn.shape, BF),
            shape(deep, BF),
            shape((4,) + tall, BF),
            shape((2,) + deep, BF),
            shape((1, 3 * cols), F32),
            shape(tall, F32),
            shape((length, width), BF),
        ],
        scratch_shapes=[
            pltpu.VMEM((count, width), BF),
            pltpu.VMEM((count, width), BF),
            pltpu.VMEM(attn.shape, BF),
            pltpu.VMEM((4, micro, cols // LANES, total, LANES), BF),
            pltpu.VMEM((count, 3 * cols), BF),
            pltpu.VMEM((count, cols), BF),
            pltpu.VMEM(attn.shape, BF),
            pltpu.VMEM((total, LANES), F32),
            pltpu.VMEM((total, LANES), F32),
            pltpu.VMEM((256, 512), F32),
            pltpu.VMEM(tall, BF),
            pltpu.VMEM(tall, BF),
            pltpu.VMEM((2,) + tall, BF),
            pltpu.VMEM(deep, BF),
            pltpu.VMEM((3,) + deep, BF),
            pltpu.VMEM((chips, length, width), BF),
            pltpu.VMEM((length, width), BF),
            pltpu.VMEM((chips, length, width), BF),
            pltpu.VMEM((chips, length, width), BF),
            pltpu.VMEM((chips - 1, length, width), BF),
            dma((5,)),
            dma((2,)),
            dma((4,)),
        ]
        + [sums] * 4
        + [dma((size,)), dma((size,)), dma((2,))]
        + [dma((2 * (chips - 1),))] * 2,
        compiler_params=pltpu.CompilerParams(
            collective_id=3, has_side_effects=True, vmem_limit_bytes=62 * 1024 * 1024
        ),
        cost_estimate=pl.CostEstimate(
            flops=40 * 1000**3, bytes_accessed=300 * 1000 * 1000, transcendentals=0
        ),
    )(
        starts,
        cosine,
        sine,
        normed.reshape(count, width),
        up.reshape(count, width),
        attn,
        grad_two,
        grad_one,
        old_two,
        old_one,
        part_act,
        tokens,
        full,
    )


def close_kernel(
    dims,
    tokens_hbm,
    up_hbm,
    grads_hbm,
    attn_hbm,
    turned_hbm,
    mixed_hbm,
    part_grad_hbm,
    part_act_hbm,
    full_ref,
    bqkv_ref,
    bone_ref,
    btwo_ref,
    first_act_ref,
    act_ref,
    ingrad_ref,
    out_ref,
    vec_ref,
    norm_ref,
    spread_hbm,
    tokens_v,
    up_v,
    attn_v,
    turned_v,
    mixed_v,
    part_grad_v,
    part_act_v,
    to_core,
    sums,
    coming,
    grads_v,
    landing,
    line_out,
    total_v,
    norm_v,
    norm_seq,
    norm_line,
    vec_in,
    load_sem,
    core_send,
    core_recv,
    axis_send,
    axis_recv,
    line_send,
    line_recv,
    a2a_send,
    a2a_recv,
    vec_send,
    vec_recv,
    norm_send,
    norm_recv,
):
    size, depth, micro, length, width, units, cols = dims
    me, at = lax.axis_index("seq"), lax.axis_index("fsdp")
    count = size.bit_length() - 1
    chips = size // 2
    chip, core = me >> 1, me & 1
    half = width // 2
    per = width // size

    loads = [
        pltpu.make_async_copy(src, dst, load_sem.at[n])
        for n, (src, dst) in enumerate(
            (
                (turned_hbm, turned_v),
                (attn_hbm, attn_v),
                (part_grad_hbm, part_grad_v),
                (part_act_hbm.at[pl.ds(1, micro - 1)], part_act_v),
                (mixed_hbm, mixed_v),
                (tokens_hbm, tokens_v),
                (up_hbm, up_v),
                (grads_hbm, grads_v),
            )
        )
    ]
    for load in loads[7:] + loads[:3]:
        load.start()
    greet(size, depth)

    def line_copy(step, way, part, src):
        number = (step * 2 + (way > 0)) * 2 + part
        return remote(
            src,
            landing.at[number],
            line_send.at[number],
            line_recv.at[number],
            {"fsdp": jnp.clip(at + way, 0, depth - 1)},
        )

    def place_of(way):
        return at if way > 0 else depth - 1 - at

    def chunk(origin, part):
        return grads_v.at[pl.ds(part * chips, chips), origin]

    def origin_of(step, way):
        away = jnp.clip(depth - step + place_of(way), 0, depth - 1)
        return away if way > 0 else depth - 1 - away

    def line_source():
        for step in range(1, depth):
            for part in range(2):
                for way in (1, -1):

                    @pl.when(place_of(way) == 0)
                    def _():
                        line_copy(step, way, part, chunk(origin_of(step, way), part)).start()

    def line_forward(step, part):
        for way in (1, -1):
            place = place_of(way)
            slot = (way > 0) * 2 + part

            @pl.when((place >= 1) & (place <= step - 1) & (place < depth - 1))
            def _():
                arrived = line_copy(step - 1, way, part, line_out.at[slot])
                arrived.wait_recv()

                @pl.when(place <= step - 2)
                def _():
                    arrived.wait_send()

                came = landing[((step - 1) * 2 + (way > 0)) * 2 + part]
                mine = chunk(origin_of(step, way), part)[...]
                line_out[slot] = (mine.astype(F32) + came.astype(F32)).astype(BF)
                line_copy(step, way, part, line_out.at[slot]).start()

    def line_finish(part):
        for way in (1, -1):
            place = place_of(way)
            number = ((depth - 1) * 2 + (way > 0)) * 2 + part

            @pl.when(place >= 1)
            def _():
                line_copy(depth - 1, way, part, line_out.at[0]).wait_recv()

            @pl.when(place == 0)
            def _():
                landing[number] = jnp.zeros_like(landing[number])

        first = (depth - 1) * 4 + part
        summed = chunk(at, part)[...].astype(F32)
        summed = summed + landing[first].astype(F32) + landing[first + 2].astype(F32)
        total_v[pl.ds(part * chips, chips)] = summed.astype(BF)
        for block in range(chips):
            out_ref[:, (part * chips + block) * cols : (part * chips + block + 1) * cols] = summed[
                block, :, 3 * cols :
            ]

    def line_sent():
        for part in range(2):
            for way in (1, -1):
                place = place_of(way)

                @pl.when(place == 0)
                def _():
                    for step in range(1, depth):
                        line_copy(step, way, part, line_out.at[0]).wait_send()

                @pl.when((place >= 1) & (place < depth - 1))
                def _():
                    line_copy(depth - 1, way, part, line_out.at[0]).wait_send()

    def back_copy(step):
        peer = me ^ step
        return remote(
            total_v.at[peer, :, pl.ds(0, 3 * cols)],
            spread_hbm.at[me],
            a2a_send.at[step],
            a2a_recv.at[step],
            {"seq": peer},
        )

    orders = [(0, m) for m in range(micro)] + [(1, m) for m in range(1, micro)]
    found = {}
    for number, (array, m) in enumerate(orders):
        found[array, m] = SeqSum(
            size,
            width,
            to_core.at[number],
            sums.at[number],
            coming.at[number],
            (core_send.at[number], core_recv.at[number]),
            (axis_send, axis_recv),
            number * 2 * (chips - 1),
        )

    over_last = (((1,), (1,)), ((), ()))

    def grad_terms(m):
        def terms(parity, write):
            blocks = pl.ds(parity * chips, chips)
            turned = turned_v[m, blocks].reshape(chips * length, 3 * cols)

            @pl.loop(0, size)
            def _(s):
                columns = pl.ds(pl.multiple_of(s * per, per), per)
                w = attn_v[s, :, :, : 3 * cols].reshape(per, 3 * cols)
                y = lax.dot_general(turned, w, over_last, preferred_element_type=F32)
                y = y.reshape(chips, length, per)
                write(columns, y + part_grad_v[m, blocks, :, columns].astype(F32))

        return terms

    def act_terms(m):
        def terms(parity, write):
            blocks = pl.ds(parity * chips, chips)
            mixed = mixed_v[m, blocks].reshape(chips * length, cols)

            @pl.loop(0, size)
            def _(s):
                columns = pl.ds(pl.multiple_of(s * per, per), per)
                w = attn_v[s, :, :, 3 * cols :].reshape(per, cols)
                y = jnp.dot(mixed, w, preferred_element_type=F32).reshape(chips, length, per)
                write(columns, y + part_act_v[m - 1, blocks, :, columns].astype(F32))

        return terms

    gain = full_ref[0:1, :]
    vec_ref[...] = jnp.zeros_like(vec_ref)
    for part in range(3):
        columns = pl.ds(pl.multiple_of(me * cols, cols), cols)
        vec_ref[2 + part : 3 + part, columns] = bqkv_ref[:, part * cols : (part + 1) * cols]
    vec_ref[5:6, :] = btwo_ref[...]
    norm_v[...] = jnp.zeros_like(norm_v)
    bone_at = pl.multiple_of(lax.rem(me * units, width), units)
    vec_ref[pl.ds(6 + me * units // width, 1), pl.ds(bone_at, units)] = bone_ref[...]

    def norm_back(m):
        x = tokens_v[m].astype(F32)
        dy = found[0, m].last()
        center = x - jnp.mean(x, axis=-1, keepdims=True)
        spread = jnp.mean(center * center, axis=-1, keepdims=True)
        r = lax.rsqrt(spread + EPSILON)
        xhat = center * r
        g = dy * gain
        inner = g - jnp.mean(g, axis=-1, keepdims=True)
        inner = inner - xhat * jnp.mean(g * xhat, axis=-1, keepdims=True)
        ingrad_ref[m] = up_v[m].astype(F32) + r * inner
        norm_v[0:1, :] += jnp.sum(dy * xhat, axis=0, keepdims=True)
        norm_v[1:2, :] += jnp.sum(dy, axis=0, keepdims=True)

    def act_out(m):
        bias = full_ref[5:6, :] + full_ref[6 + size * units // width : 7 + size * units // width, :]
        total = tokens_v[m].astype(F32) + found[1, m].last() + bias
        act_ref[m] = total.astype(BF)

    def norm_seq_copy(step):
        peer = me ^ step
        return remote(
            norm_v.at[:, pl.ds(pl.multiple_of(peer * per, per), per)],
            norm_seq.at[step],
            norm_send.at[step],
            norm_recv.at[step],
            {"seq": peer},
        )

    def norm_line_copy(step):
        number = size + step
        return remote(
            norm_seq.at[0],
            norm_line.at[step],
            norm_send.at[number],
            norm_recv.at[number],
            {"fsdp": lax.rem(at + step, depth)},
        )

    def norm_line_start():
        total = norm_v[:, pl.ds(pl.multiple_of(me * per, per), per)]
        for step in range(1, size):
            norm_seq_copy(step).wait_recv()
            total = total + norm_seq[step]
        norm_seq[0] = total
        for step in range(1, depth):
            norm_line_copy(step).start()

    def norm_finish():
        total = norm_seq[0]
        for step in range(1, depth):
            norm_line_copy(step).wait_recv()
            total = total + norm_line[step]
        norm_ref[...] = total

    levels = [("fsdp", 1 << bit) for bit in range(depth.bit_length() - 1)]
    levels = levels + [("seq", 1 << bit) for bit in range(count)]

    def vec_copy(level):
        axis, step = levels[level]
        mine = me if axis == "seq" else at
        return remote(
            vec_ref,
            vec_in.at[level],
            vec_send.at[level],
            vec_recv.at[level],
            {axis: mine ^ step},
        )

    def vec_level(level):
        copy = vec_copy(level)
        copy.wait()
        vec_ref[...] += vec_in[level]
        if level + 1 < len(levels):
            vec_copy(level + 1).start()

    vec_copy(0).start()
    loads[7].wait()
    vec_level(0)
    line_source()
    for load in loads[:3]:
        load.wait()
    for load in loads[3:7]:
        load.start()
    found[0, 0].away(grad_terms(0))
    vec_level(1)
    found[0, 1].away(grad_terms(1))
    vec_level(2)
    line_forward(2, 0)
    vec_level(3)
    found[0, 0].here(grad_terms(0))
    vec_level(4)
    found[0, 1].here(grad_terms(1))
    for load in loads[3:7]:
        load.wait()
    act_ref[0] = first_act_ref[...]
    found[1, 1].away(act_terms(1))
    line_forward(2, 1)
    found[1, 1].here(act_terms(1))
    found[0, 0].step(0)
    line_forward(3, 0)
    found[0, 1].step(0)
    found[0, 0].add(1)
    norm_back(0)
    line_forward(3, 1)
    found[0, 1].add(1)
    norm_back(1)
    for step in range(1, size):
        norm_seq_copy(step).start()
    found[1, 1].step(0)
    norm_line_start()

    def finish(part):
        line_finish(part)
        for step in range(1, size):
            peer = me ^ step

            @pl.when((peer >= part * chips) & (peer < (part + 1) * chips))
            def _():
                back_copy(step).start()

    finish(0)
    found[1, 1].add(1)
    act_out(1)
    finish(1)
    norm_finish()

    back_mine = pltpu.make_async_copy(
        total_v.at[me, :, pl.ds(0, 3 * cols)], spread_hbm.at[me], a2a_recv.at[0]
    )
    back_mine.start()
    back_mine.wait()
    for step in range(1, size):
        back_copy(step).wait_recv()

    line_sent()
    for step in range(1, size):
        norm_seq_copy(step).wait_send()
    for step in range(1, depth):
        norm_line_copy(step).wait_send()
    for step in range(1, size):
        back_copy(step).wait_send()
    for terms in found.values():
        terms.core_sent()
        terms.sent()


def close_layer(
    tokens,
    upstream,
    grads,
    attn,
    turned,
    mixed,
    part_grad,
    part_act,
    full,
    bqkv,
    bone,
    btwo,
    first_act,
):
    size, depth = lax.axis_size("seq"), lax.axis_size("fsdp")
    micro, length, width = tokens.shape
    units, cols = bone.shape[-1], width // size
    rows = width // (size * depth)
    dims = (size, depth, micro, length, width, units, cols)
    chips, count = size // 2, size.bit_length() - 1
    hbm = pl.BlockSpec(memory_space=pl.ANY)
    vmem = pl.BlockSpec(memory_space=pltpu.VMEM)
    dma = pltpu.SemaphoreType.DMA
    levels = count + depth.bit_length() - 1
    piece = (chips, rows, 4 * cols)
    arrays = 2 * micro - 1
    shape = jax.ShapeDtypeStruct
    loaded = [v.shape for v in (tokens, upstream, attn, turned, mixed, part_grad)]
    loaded = loaded + [(micro - 1,) + part_act.shape[1:]]
    return pl.pallas_call(
        functools.partial(close_kernel, dims),
        in_specs=[hbm] * 8 + [vmem] * 5,
        out_specs=[vmem] * 5 + [hbm],
        out_shape=[
            shape(tokens.shape, BF),
            shape(tokens.shape, F32),
            shape((rows, width), F32),
            shape(full.shape, F32),
            shape((8, width // size), F32),
            shape((size, rows, 3 * cols), BF),
        ],
        scratch_shapes=[pltpu.VMEM(s, BF) for s in loaded]
        + [
            pltpu.VMEM((arrays, chips, length, width), BF),
            pltpu.VMEM((arrays, chips, length, width), BF),
            pltpu.VMEM((arrays, chips - 1, length, width), BF),
            pltpu.VMEM(grads.shape, BF),
            pltpu.VMEM((4 * depth,) + piece, BF),
            pltpu.VMEM((4,) + piece, BF),
            pltpu.VMEM((size, rows, 4 * cols), BF),
            pltpu.VMEM((8, width), F32),
            pltpu.VMEM((size, 8, width // size), F32),
            pltpu.VMEM((depth, 8, width // size), F32),
            pltpu.VMEM((levels,) + full.shape, F32),
            dma((9,)),
            dma((arrays,)),
            dma((arrays,)),
            dma((2 * arrays * (chips - 1),)),
            dma((2 * arrays * (chips - 1),)),
            dma((4 * depth,)),
            dma((4 * depth,)),
            dma((size,)),
            dma((size,)),
            dma((levels,)),
            dma((levels,)),
            dma((size + depth,)),
            dma((size + depth,)),
        ],
        compiler_params=pltpu.CompilerParams(
            collective_id=4, has_side_effects=True, vmem_limit_bytes=62 * 1024 * 1024
        ),
        cost_estimate=pl.CostEstimate(
            flops=30 * 1000**3, bytes_accessed=300 * 1000 * 1000, transcendentals=0
        ),
    )(
        tokens,
        upstream,
        grads,
        attn,
        turned,
        mixed,
        part_grad,
        part_act,
        full,
        bqkv,
        bone,
        btwo,
        first_act,
    )


def result_kernel(
    dims,
    place_ref,
    act_ref,
    ingrad_ref,
    out_ref,
    two_ref,
    one_ref,
    qkv_ref,
    vec_ref,
    norm_ref,
    act_to,
    ingrad_to,
    gain_ref,
    shift_ref,
    wqkv_ref,
    bqk_ref,
    bv_ref,
    out_to,
    bout_ref,
    one_to,
    bone_ref,
    two_to,
    btwo_ref,
):
    size, depth, width, cols, units = dims
    for source, target in (
        (ingrad_ref, ingrad_to),
        (two_ref, two_to),
        (act_ref, act_to),
        (out_ref, out_to),
    ):
        target[...] = source[...]
    for s in range(size):
        one_to[:, s * units : (s + 1) * units] = one_ref[s].astype(F32)
        for part in range(3):
            start = part * width + s * cols
            wqkv_ref[:, start : start + cols] = qkv_ref[s, :, part * cols : (part + 1) * cols].astype(
                F32
            )
    index = place_ref[0]

    def own(row, total, target):
        extent = total // (size * depth)
        flat = index * extent
        at = lax.rem(flat, width)
        values = vec_ref[pl.ds(row + flat // width, 1), :]
        values = pltpu.roll(values, lax.rem(width - at, width), 1)
        target[...] = values[:, :extent]

    per = width // size
    extent = per // depth
    norms = pltpu.roll(norm_ref[...], lax.rem(per - lax.rem(index, depth) * extent, per), 1)
    gain_ref[...] = norms[0:1, :extent]
    shift_ref[...] = norms[1:2, :extent]
    own(2, 2 * width, bqk_ref)
    own(4, width, bv_ref)
    own(5, width, bout_ref)
    own(5, width, btwo_ref)
    own(6, size * units, bone_ref)


def results(
    activations, input_grad, grad_out, grad_two, spread_one, spread_qkv, vectors, norms, index
):
    size, rows, units = spread_one.shape
    width = vectors.shape[-1]
    depth = width // (size * rows)
    cols = width // size
    dims = (size, depth, width, cols, units)
    vmem = pl.BlockSpec(memory_space=pltpu.VMEM)

    def row(extent):
        return jax.ShapeDtypeStruct((1, extent // (size * depth)), F32)

    def like(value):
        return jax.ShapeDtypeStruct(value.shape, value.dtype)

    wide = jax.ShapeDtypeStruct((rows, size * units), F32)
    shapes = [
        like(activations),
        like(input_grad),
        row(width),
        row(width),
        jax.ShapeDtypeStruct((rows, 3 * width), F32),
        row(2 * width),
        row(width),
        like(grad_out),
        row(width),
        wide,
        row(size * units),
        like(grad_two),
        row(width),
    ]
    return pl.pallas_call(
        functools.partial(result_kernel, dims),
        in_specs=[pl.BlockSpec(memory_space=pltpu.SMEM)] + [vmem] * 8,
        out_specs=[vmem] * len(shapes),
        out_shape=shapes,
        compiler_params=pltpu.CompilerParams(vmem_limit_bytes=60 * 1024 * 1024),
    )(
        index[None],
        activations,
        input_grad,
        grad_out,
        grad_two,
        spread_one,
        spread_qkv,
        vectors,
        norms,
    )


def gelu_tanh(values):
    return jax.nn.gelu(values, approximate=True)


def layer_norm(values, gain, shift):
    center = values - jnp.mean(values, axis=-1, keepdims=True)
    spread = jnp.mean(center * center, axis=-1, keepdims=True)
    return center * lax.rsqrt(spread + EPSILON) * gain + shift


def fence(*values):
    return lax.optimization_barrier(values)


def line_right(value, senders):
    return lax.ppermute(value, "fsdp", [(i, i + 1) for i in senders])


def line_left(value, senders):
    last = lax.axis_size("fsdp") - 1
    return lax.ppermute(value, "fsdp", [(last - i, last - i - 1) for i in senders])


class Gather:
    def __init__(self, mine):
        self.right, self.left = [mine], [mine]

    def step(self):
        size = lax.axis_size("fsdp")
        number = len(self.right)
        if number < size:
            self.right.append(line_right(self.right[-1], range(number - 1, size - 1)))
            self.left.append(line_left(self.left[-1], range(number - 1, size - 1)))

    def fence(self, *others):
        (self.right[-1], self.left[-1]), *others = fence((self.right[-1], self.left[-1]), *others)
        return others

    def rest(self):
        while len(self.right) < lax.axis_size("fsdp"):
            self.step()

    def pieces(self):
        size = lax.axis_size("fsdp")
        at = lax.axis_index("fsdp")
        found = [(self.right[0], at)]
        for step in range(1, size):
            piece = jnp.where(at >= step, self.right[step], self.left[size - step])
            found.append((piece, lax.rem(at - step + size, size)))
        return found


class Scatter:
    def __init__(self, chunk):
        self.chunk = chunk
        self.number = 0
        self.right = self.left = None

    def step(self):
        size = lax.axis_size("fsdp")
        at = lax.axis_index("fsdp")
        if self.number == size - 1:
            return
        self.number += 1
        going = self.chunk(jnp.minimum(size - self.number + at, size - 1))
        coming = self.chunk(jnp.maximum(self.number - size + at, 0))
        if self.number > 1:
            going = (going.astype(F32) + self.right.astype(F32)).astype(BF)
            coming = (coming.astype(F32) + self.left.astype(F32)).astype(BF)
        self.right = line_right(going, range(self.number))
        self.left = line_left(coming, range(self.number))

    def rest(self):
        while self.number < lax.axis_size("fsdp") - 1:
            self.step()

    def fence(self, *others):
        (self.right, self.left), *others = fence((self.right, self.left), *others)
        return others

    def total(self):
        mine = self.chunk(lax.axis_index("fsdp")).astype(F32)
        return mine + self.right.astype(F32) + self.left.astype(F32)


def staged_layer(
    tokens, upstream, w_fc2, w_qkv, w_out, starts, normed, up, my_one, two_near, full, index
):
    size, depth = lax.axis_size("seq"), lax.axis_size("fsdp")
    me = lax.axis_index("seq")
    micro, length, width = tokens.shape
    rows = width // (size * depth)
    hidden_rows = w_fc2.shape[0]
    cols = width // size
    units = hidden_rows * depth
    count = micro * size * length

    def contract_last(left, right):
        return lax.dot_general(left, right, (((1,), (1,)), ((), ())), preferred_element_type=F32)

    def contract_first(left, right):
        return lax.dot_general(left, right, (((0,), (0,)), ((), ())), preferred_element_type=F32)

    def place_columns(pieces):
        out = jnp.zeros((size, depth) + pieces[0][0].shape[1:], BF)
        for piece, origin in pieces:
            out = lax.dynamic_update_slice_in_dim(out, piece[:, None], origin, 1)
        return out

    def place_rows(pieces):
        out = jnp.zeros((depth,) + pieces[0][0].shape, BF)
        for piece, origin in pieces:
            out = lax.dynamic_update_slice_in_dim(out, piece[None], origin, 0)
        return out

    normed = normed.reshape(count, width)
    up = up.reshape(count, width)
    my_one = my_one.reshape(width, units)
    two = Gather(w_fc2)
    at = lax.axis_index("fsdp")
    for way, found in ((-1, two.right), (1, two.left)):
        origin = jnp.clip(at + way, 0, depth - 1)
        found.append(lax.dynamic_index_in_dim(two_near, origin, 0, keepdims=False))
    gain, shift, bias_out = full[0], full[1], full[5]
    bias_qkv = lax.dynamic_slice_in_dim(full[2:5], me * cols, cols, 1).reshape(-1)
    ratio = size * units // width
    bias_one = lax.dynamic_slice_in_dim(full[6 : 6 + ratio].reshape(-1), me * units, units, 0)
    bias_two = full[6 + ratio]
    two.step()
    split = w_qkv.reshape(rows, 3, size, cols).transpose(2, 0, 1, 3).reshape(size, rows, 3 * cols)
    attn_cols = lax.all_to_all(split, "seq", 0, 0, tiled=True)
    out_cols = w_out.reshape(rows, size, cols).transpose(1, 0, 2)
    attn_cols = jnp.concatenate([attn_cols, out_cols], axis=-1)
    pre = jnp.dot(normed, my_one, preferred_element_type=F32) + bias_one
    hidden, back = jax.vjp(gelu_tanh, pre)
    hidden = hidden.astype(BF)
    grad_two = contract_first(hidden, up).astype(BF).reshape(depth, hidden_rows, width)
    hidden, grad_two = two.fence(hidden, grad_two)
    two.step()
    sum_two = Scatter(lambda o: lax.dynamic_index_in_dim(grad_two, o, 0, keepdims=False))
    sum_two.step()
    (two.right, two.left), (sum_two.right, sum_two.left), attn_cols = fence(
        (two.right, two.left), (sum_two.right, sum_two.left), attn_cols
    )
    attn = Gather(attn_cols)
    attn.step()
    two.rest()
    my_two = place_rows(two.pieces()).reshape(units, width)
    pre_grad = back(contract_last(up, my_two))[0].astype(BF)
    grad_one = contract_first(normed, pre_grad).astype(BF).reshape(size, depth, rows, units)
    pre_grad, grad_one = attn.fence(pre_grad, grad_one)
    attn.step()
    sum_one = Scatter(lambda o: lax.dynamic_index_in_dim(grad_one, o, 1, keepdims=False))
    sum_one.step()
    (sum_one.right, sum_one.left), (sum_two.right, sum_two.left) = attn.fence(
        (sum_one.right, sum_one.left), (sum_two.right, sum_two.left)
    )
    attn.step()
    sum_two.step()
    (sum_two.right, sum_two.left), normed, up = attn.fence(
        (sum_two.right, sum_two.left), normed, up
    )
    sum_two.step()
    attn.rest()
    attn_weights = place_columns(attn.pieces())
    my_qkv = attn_weights[..., : 3 * cols].reshape(width, 3 * cols)
    my_out = attn_weights[..., 3 * cols :].transpose(1, 2, 0, 3).reshape(cols, width)
    projected = jnp.dot(normed, my_qkv, preferred_element_type=F32) + bias_qkv
    projected = projected.reshape(micro, size, length, 3 * cols)
    mixed_grad = contract_last(up, my_out).astype(BF).reshape(micro, size, length, cols)
    parts = [attention(starts[:1], projected[:1], mixed_grad[:1])]
    (sum_one.right, sum_one.left), (projected, mixed_grad), parts = sum_two.fence(
        (sum_one.right, sum_one.left), (projected, mixed_grad), parts
    )
    sum_one.step()
    for m in range(1, micro):
        parts.append(attention(starts[m:][:1], projected[m:][:1], mixed_grad[m:][:1]))
    mixed = jnp.concatenate([part[0] for part in parts]).reshape(count, cols)
    projected_grad = jnp.concatenate(
        [jnp.concatenate(part[1:], axis=-1) for part in parts]
    ).reshape(count, 3 * cols)
    projected_grad, mixed = sum_one.fence(projected_grad, mixed)
    sum_one.step()
    grad_qkv = contract_first(normed, projected_grad).astype(BF).reshape(size, depth, rows, 3 * cols)
    grad_out = contract_first(mixed, up).astype(BF).reshape(depth, rows, size, cols)
    grad_qkv, grad_out, (sum_two.right, sum_two.left) = sum_one.fence(
        grad_qkv, grad_out, (sum_two.right, sum_two.left)
    )
    grad_attn = jnp.concatenate([grad_qkv, grad_out.transpose(2, 0, 1, 3)], axis=-1)

    def to_rows(mine, parts):
        mine = lax.all_to_all(mine.astype(BF), "seq", 0, 0, tiled=True).astype(F32)
        return mine.reshape(size, rows, parts, -1).transpose(1, 2, 0, 3).reshape(rows, -1)

    sum_one.rest()
    sum_two.rest()
    out_two = sum_two.total()
    out_one = to_rows(sum_one.total(), 1)

    def put(values, extent, at):
        return lax.dynamic_update_slice_in_dim(jnp.zeros(extent, F32), values, at, -1)

    bqkv = jnp.sum(projected_grad.astype(F32), axis=0).reshape(3, cols)
    bqkv = put(bqkv, (3, width), me * cols)
    bone = put(jnp.sum(pre_grad.astype(F32), axis=0), (size * units,), me * units)
    btwo = jnp.sum(upstream.astype(F32), axis=(0, 1))[None]
    early = [jnp.zeros((2, width), F32), bqkv, btwo, bone.reshape(ratio, width)]
    early = jnp.pad(jnp.concatenate(early), ((0, full.shape[0] - 6 - ratio), (0, 0)))

    sum_attn = Scatter(lambda o: lax.dynamic_index_in_dim(grad_attn, o, 1, keepdims=False))
    sum_attn.step()
    grad_terms = contract_last(projected_grad, my_qkv) + contract_last(pre_grad, my_one)
    grad_terms = grad_terms.astype(BF).reshape(micro, size, length, width)
    (grad_terms,) = sum_attn.fence(grad_terms)
    sum_attn.step()
    normed_grad = scatter_seq(grad_terms)
    terms = jnp.dot(mixed, my_out, preferred_element_type=F32)
    terms = terms + jnp.dot(hidden, my_two, preferred_element_type=F32)
    terms = terms.astype(BF).reshape(micro, size, length, width)
    sums = scatter_seq(terms)
    sum_attn.rest()
    attn_total = sum_attn.total()
    out_qkv = to_rows(attn_total[..., : 3 * cols], 3)
    out_out = attn_total[..., 3 * cols :].transpose(1, 0, 2).reshape(rows, width)
    activations = (tokens.astype(F32) + sums + (bias_out + bias_two)).astype(BF)
    _, norm_back = jax.vjp(layer_norm, tokens.astype(F32), gain, shift)
    input_grad, gain_grad, shift_grad = norm_back(normed_grad)
    input_grad = input_grad + upstream.astype(F32)
    vectors = early.at[:2].add(jnp.stack([gain_grad, shift_grad]))
    vectors = lax.psum(vectors, ("seq", "fsdp"))

    return activations, input_grad, out_qkv, out_out, vectors, out_one, out_two


def per_device(
    tokens,
    ln_gain,
    ln_bias,
    w_qkv,
    b_qkv,
    w_out,
    b_out,
    w_fc1,
    b_fc1,
    w_fc2,
    b_fc2,
    piece_starts,
    cotangent,
):
    size, depth = lax.axis_size("seq"), lax.axis_size("fsdp")
    me = lax.axis_index("seq")
    micro, _, length, width = tokens.shape
    rows = width // (size * depth)
    hidden_rows = w_fc2.shape[0]
    cols = width // size
    units = hidden_rows * depth
    count = micro * size * length
    tokens = tokens[:, 0]
    upstream = cotangent[:, 0]

    index = me * depth + lax.axis_index("fsdp")
    packed = []
    for vector in (ln_gain, ln_bias, b_qkv, b_out, b_fc1, b_fc2):
        mine = jnp.arange(size * depth, dtype=jnp.int32)[:, None] == index
        packed.append(jnp.where(mine, vector[None, :], 0).astype(BF).reshape(-1, width))
    packed = jnp.concatenate(packed, axis=0)
    packed = jnp.pad(packed, ((0, -packed.shape[0] % 16), (0, 0)))
    starts = piece_starts[:, 0]
    loaded = load_all(tokens, upstream, w_fc1, w_fc2, packed)
    if (size, depth, micro) == (8, 4, 2):
        normed, up, one, two_near, full = loaded
        part_grad, part_act, attn, grad_two, grad_one, land_two, land_one, *sums = feed_forward(
            normed, up, one, two_near, w_qkv, w_out, full
        )
        wide = (micro, size, length, -1)
        part_act = part_act.reshape(wide)
        turned, mixed, grads, spread_one, _, _, bqkv, out_two, first_act = attention_layer(
            starts,
            normed,
            up,
            attn,
            grad_two,
            grad_one,
            land_two,
            land_one,
            part_act,
            tokens,
            full,
        )
        activations, input_grad, out_out, vectors, norms, spread_qkv = close_layer(
            tokens,
            upstream,
            grads,
            attn,
            turned.reshape(wide),
            mixed.reshape(wide),
            part_grad.reshape(wide),
            part_act,
            full,
            bqkv,
            *sums,
            first_act,
        )

        found = results(
            activations, input_grad, out_out, out_two, spread_one, spread_qkv, vectors, norms, index
        )
        found = [v.reshape(-1) if n in (2, 3, 5, 6, 8, 10, 12) else v for n, v in enumerate(found)]
        return (found[0][:, None], found[1][:, None]) + tuple(found[2:])

    activations, input_grad, out_qkv, out_out, vectors, out_one, out_two = staged_layer(
        tokens, upstream, w_fc2, w_qkv, w_out, starts, *loaded, index
    )
    ratio = w_fc1.shape[1] // width

    def own(values):
        values = values.reshape(-1)
        extent = values.shape[0] // (size * depth)
        return lax.dynamic_slice_in_dim(values, index * extent, extent, 0)

    grad_b_two = own(vectors[5])
    return (
        activations[:, None],
        input_grad[:, None],
        own(vectors[0]),
        own(vectors[1]),
        out_qkv,
        own(vectors[2:4]),
        own(vectors[4]),
        out_out,
        grad_b_two,
        out_one,
        own(vectors[6 : 6 + ratio]),
        out_two,
        grad_b_two,
    )


def solution(mesh):
    both = ("seq", "fsdp")
    row = P(both)
    matrix = P(both, None)
    tokens = P(None, "fsdp", "seq", None)
    weights = (row, row, matrix, row, matrix, row, matrix, row, matrix, row)
    grads = (row, row, matrix, row, row, matrix, row, matrix, row, matrix, row)
    return jax.shard_map(
        per_device,
        mesh=mesh,
        in_specs=(tokens,) + weights + (P(None, "fsdp", None), tokens),
        out_specs=(tokens, tokens) + grads,
        check_vma=False,
    )
```

```python
import functools
import math

import jax
import jax.numpy as jnp
import numpy as np
from jax import lax
from jax.experimental import pallas as pl
from jax.experimental.pallas import tpu as pltpu
from jax.sharding import PartitionSpec as P

HEADS = 32
HEAD_DIM = 64
ROT = 32
IMG = 256
PIECES = 2
EPSILON = 1e-05
BF = jnp.bfloat16
F32 = jnp.float32
SCALE = 1.0 / math.sqrt(HEAD_DIM)
LANES = 2 * HEAD_DIM


def swap(value, bit):
    size = lax.axis_size("seq")
    return lax.ppermute(value, "seq", [(i, i ^ bit) for i in range(size)])


def store_index(block):
    half = lax.axis_size("seq") // 2
    if isinstance(block, int):
        return block % 2 * half + block // 2
    return (block & 1) * half + (block >> 1)


def scatter_seq(terms):
    size = lax.axis_size("seq")
    me = lax.axis_index("seq")
    count = size.bit_length() - 1
    micro, _, length, width = terms.shape
    half = width // 2
    bits = list(range(1, count))

    def exchange(held, bit, axis):
        held = held.astype(BF)
        mine = (me >> bit) & 1
        away = lax.dynamic_index_in_dim(held, 1 - mine, axis, keepdims=False)
        kept = lax.dynamic_index_in_dim(held, mine, axis, keepdims=False)
        return kept.astype(F32) + swap(away, 1 << bit).astype(F32)

    sums = []
    for cols, order in ((slice(0, half), bits), (slice(half, width), bits[::-1])):
        held = terms[..., cols].reshape((micro,) + (2,) * count + (length, half))
        left = [0] + bits[::-1]
        for bit in [0] + order:
            held = exchange(held, bit, 1 + left.index(bit))
            left.remove(bit)
        sums.append(held)
    return jnp.concatenate(sums, axis=-1)


def attention_kernel(
    blocks,
    length,
    starts_ref,
    cos_ref,
    sin_ref,
    q_ref,
    k_ref,
    v_ref,
    do_ref,
    mixed_ref,
    dq_ref,
    dk_ref,
    dv_ref,
    q_s,
    k_s,
    v_s,
    do_s,
    dk_s,
    dv_s,
    bias_s,
):
    micro = pl.program_id(0)
    total = blocks * length
    tile = 256
    lane = lax.broadcasted_iota(jnp.int32, (1, LANES), 1)
    low_lane = (lane % HEAD_DIM) < (ROT // 2)

    def turn(value, cosine, sine):
        other = jnp.where(
            low_lane,
            pltpu.roll(value, LANES - ROT // 2, 1),
            pltpu.roll(value, ROT // 2, 1),
        )
        return value * cosine + other * sine

    for block in range(blocks):
        source = store_index(block)
        at = slice(block * length, (block + 1) * length)
        cosine, sine = cos_ref[at, :], sin_ref[at, :]
        q_s[at, :] = (turn(q_ref[0, source], cosine, sine)).astype(BF) * jnp.asarray(SCALE, BF)
        k_s[at, :] = turn(k_ref[0, source], cosine, sine).astype(BF)
        v_s[at, :] = v_ref[0, source].astype(BF)
        do_s[at, :] = do_ref[0, source]
    dk_s[...] = jnp.zeros_like(dk_s)
    dv_s[...] = jnp.zeros_like(dv_s)

    def label(positions):
        found = jnp.full(positions.shape, -1, jnp.int32)
        for piece in range(PIECES):
            start = starts_ref[micro, piece]
            found = jnp.where((positions >= start) & (positions < start + IMG), piece, found)
        return found

    for first in range(0, total, tile):
        last = min(total, first + tile + IMG)
        qpos = first + lax.broadcasted_iota(jnp.int32, (tile, 1), 0)
        kpos = first + lax.broadcasted_iota(jnp.int32, (1, last - first), 1)
        qlab, klab = label(qpos), label(kpos)
        allowed = (kpos <= qpos) | ((qlab == klab) & (qlab >= 0))
        bias_s[:, : last - first] = jnp.where(allowed, 0.0, -1e30)
        rows = slice(first, first + tile)
        keys = k_s[:last, :]
        values = v_s[:last, :]
        mixed = jnp.zeros((tile, LANES), F32)
        dq = jnp.zeros((tile, LANES), F32)
        for head in range(LANES // HEAD_DIM):
            mine = (lane // HEAD_DIM) == head
            q = jnp.where(mine, q_s[rows, :], 0)
            do = jnp.where(mine, do_s[rows, :], 0)
            dims = (((1,), (1,)), ((), ()))
            s = lax.dot_general(q, keys, dims, preferred_element_type=F32)
            if first:
                s = jnp.concatenate(
                    [s[:, :first], s[:, first:] + bias_s[:, : last - first]], axis=1
                )
            else:
                s = s + bias_s[:, : last - first]
            p = jnp.exp(s - jnp.max(s, axis=1, keepdims=True))
            p = p * (1.0 / jnp.sum(p, axis=1, keepdims=True))
            probs = p.astype(BF)
            att = jnp.dot(probs, values, preferred_element_type=F32)
            mixed = jnp.where(mine, att, mixed)
            dp = lax.dot_general(do, values, dims, preferred_element_type=F32)
            delta = jnp.sum(p * dp, axis=1, keepdims=True)
            ds = (p * (dp - delta)).astype(BF)
            dq = jnp.where(mine, jnp.dot(ds, keys, preferred_element_type=F32), dq)
            over = (((0,), (0,)), ((), ()))
            dk_s[:last, :] += lax.dot_general(ds, q, over, preferred_element_type=F32)
            dv_s[:last, :] += lax.dot_general(probs, do, over, preferred_element_type=F32)
        dq = dq * SCALE
        for part in range(tile // length):
            block = first // length + part
            here = slice(part * length, (part + 1) * length)
            at = slice(block * length, (block + 1) * length)
            mixed_ref[0, store_index(block)] = mixed[here].astype(BF)
            dq_ref[0, store_index(block)] = turn(dq[here], cos_ref[at, :], -sin_ref[at, :]).astype(BF)
    for block in range(blocks):
        at = slice(block * length, (block + 1) * length)
        dk_ref[0, store_index(block)] = turn(dk_s[at, :], cos_ref[at, :], -sin_ref[at, :]).astype(BF)
        dv_ref[0, store_index(block)] = dv_s[at, :].astype(BF)


def tables(total):
    half = ROT // 2
    frequency = (10000.0 ** (-2.0 * np.arange(half) / ROT)).astype(np.float32)
    angles = np.arange(total, dtype=np.float32)[:, None] * frequency[None, :]
    cosine, sine = np.cos(angles), np.sin(angles)
    ones = np.ones((total, HEAD_DIM - ROT), np.float32)
    cosine = np.concatenate([cosine, cosine, ones] * 2, axis=1)
    sine = np.concatenate([-sine, sine, 0 * ones] * 2, axis=1)
    return jnp.asarray(cosine), jnp.asarray(sine)


def attention(starts, projected, mixed_grad):
    micro, blocks, length, cols = mixed_grad.shape
    total = blocks * length
    groups = cols // LANES
    cosine, sine = tables(total)

    def spec(offset):
        return pl.BlockSpec(
            (1, blocks, length, LANES), lambda m, g, offset=offset: (m, 0, 0, offset * groups + g)
        )

    table = pl.BlockSpec((total, LANES), lambda m, g: (0, 0))
    shape = jax.ShapeDtypeStruct(mixed_grad.shape, BF)
    return pl.pallas_call(
        functools.partial(attention_kernel, blocks, length),
        grid=(micro, groups),
        in_specs=[
            pl.BlockSpec(memory_space=pltpu.SMEM),
            table,
            table,
            spec(0),
            spec(1),
            spec(2),
            spec(0),
        ],
        out_specs=[spec(0)] * 4,
        out_shape=[shape] * 4,
        scratch_shapes=[pltpu.VMEM((total, LANES), BF)] * 4
        + [pltpu.VMEM((total, LANES), F32)] * 2
        + [pltpu.VMEM((256, 512), F32)],
        compiler_params=pltpu.CompilerParams(vmem_limit_bytes=48 * 1024 * 1024),
        cost_estimate=pl.CostEstimate(
            flops=micro * groups * 40 * total * total * HEAD_DIM,
            bytes_accessed=micro * groups * total * LANES * 22,
            transcendentals=micro * groups * 2 * total * total,
        ),
    )(starts, cosine, sine, projected, projected, projected, mixed_grad)


MESH = pl.DeviceIdType.MESH


def remote(src, dst, send, recv, device):
    return pltpu.make_async_remote_copy(
        src_ref=src,
        dst_ref=dst,
        send_sem=send,
        recv_sem=recv,
        device_id=device,
        device_id_type=MESH,
    )


def greet(size, depth):
    me, at = lax.axis_index("seq"), lax.axis_index("fsdp")
    barrier = pltpu.get_barrier_semaphore()
    for step in range(1, size):
        pl.semaphore_signal(barrier, inc=1, device_id={"seq": me ^ step}, device_id_type=MESH)
    for step in range(1, depth):
        pl.semaphore_signal(
            barrier, inc=1, device_id={"fsdp": lax.rem(at + step, depth)}, device_id_type=MESH
        )
    pl.semaphore_wait(barrier, size + depth - 2)


class LineGather:
    def __init__(self, depth, source, target, send, recv):
        self.depth, self.source, self.target = depth, source, target
        self.send, self.recv = send, recv

    def copy(self, step, way):
        at = lax.axis_index("fsdp")
        origin = jnp.clip(at - way * (step - 1), 0, self.depth - 1)
        number = step * 2 + (way > 0)
        return remote(
            self.source(origin, step),
            self.target(origin),
            self.send.at[number],
            self.recv.at[number],
            {"fsdp": jnp.clip(at + way, 0, self.depth - 1)},
        )

    def sends(self, step, way):
        at = lax.axis_index("fsdp")
        origin = at - way * (step - 1)
        return (at + way >= 0) & (at + way < self.depth) & (origin >= 0) & (origin < self.depth)

    def start(self, step):
        for way in (1, -1):

            @pl.when(self.sends(step, way))
            def _():
                self.copy(step, way).start()

    def arrive(self, step):
        at = lax.axis_index("fsdp")
        for way in (1, -1):
            origin = at - way * step

            @pl.when((origin >= 0) & (origin < self.depth))
            def _():
                self.copy(step, way).wait_recv()

    def sent(self, step):
        for way in (1, -1):

            @pl.when(self.sends(step, way))
            def _():
                self.copy(step, way).wait_send()


class LineSum:
    def __init__(self, depth, chunk, landing, own, held, out, load, send, recv):
        self.depth, self.chunk, self.landing = depth, chunk, landing
        self.own, self.held, self.out = own, held, out
        self.load, self.send, self.recv = load, send, recv

    def place(self, way):
        at = lax.axis_index("fsdp")
        return at if way > 0 else self.depth - 1 - at

    def copy(self, step, way, src):
        number = step * 2 + (way > 0)
        at = lax.axis_index("fsdp")
        return remote(
            src,
            self.landing(step, way),
            self.send.at[number],
            self.recv.at[number],
            {"fsdp": jnp.clip(at + way, 0, self.depth - 1)},
        )

    def origin(self, step, way):
        away = jnp.clip(self.depth - step + self.place(way), 0, self.depth - 1)
        return away if way > 0 else self.depth - 1 - away

    def source(self, step):
        for way in (1, -1):

            @pl.when(self.place(way) == 0)
            def _():
                self.copy(step, way, self.chunk(self.origin(step, way))).start()

    def forward(self, step, here=True):
        for way in (1, -1):
            place = self.place(way)

            @pl.when((place >= 1) & (place <= step - 1) & (place < self.depth - 1))
            def _():
                mine = pltpu.make_async_copy(
                    self.chunk(self.origin(step, way)), self.own, self.load.at[0]
                )
                mine.start()
                if here:
                    self.copy(step - 1, way, self.out(step, way)).wait_recv()
                came = pltpu.make_async_copy(
                    self.landing(step - 1, way), self.held, self.load.at[1]
                )
                came.start()
                mine.wait()
                came.wait()
                target = self.out(step, way)
                target[...] = (self.own[...].astype(F32) + self.held[...].astype(F32)).astype(BF)
                self.copy(step, way, target).start()

    def arrive(self, step, consumed):
        for way in (1, -1):
            place = self.place(way)
            ok = (place >= 1) & (place <= step)
            if consumed:
                ok = ok & (place == self.depth - 1)

            @pl.when(ok)
            def _():
                self.copy(step, way, self.out(step, way)).wait_recv()

    def total(self, last, right, left):
        mine = pltpu.make_async_copy(self.chunk(lax.axis_index("fsdp")), self.own, self.load.at[0])
        mine.start()
        for way, target in ((1, right), (-1, left)):
            place = self.place(way)

            @pl.when(place >= 1)
            def _():
                self.copy(last, way, self.out(last, way)).wait_recv()
                came = pltpu.make_async_copy(self.landing(last, way), target, self.load.at[1])
                came.start()
                came.wait()

            @pl.when(place == 0)
            def _():
                target[...] = jnp.zeros_like(target)

        mine.wait()
        return self.own[...].astype(F32) + right[...].astype(F32) + left[...].astype(F32)

    def sent_first(self, step):
        for way in (1, -1):

            @pl.when(self.place(way) == 0)
            def _():
                self.copy(step, way, self.out(step, way)).wait_send()

    def sent_on(self, step):
        for way in (1, -1):
            place = self.place(way)

            @pl.when((place >= 1) & (place <= step - 1) & (place < self.depth - 1))
            def _():
                self.copy(step, way, self.out(step, way)).wait_send()

    def sent(self, step):
        self.sent_first(step)
        self.sent_on(step)


class SeqSum:
    def __init__(self, size, width, to_core, sums, coming, core_sems, axis_sems, base):
        self.size, self.width = size, width
        self.to_core, self.sums, self.coming = to_core, sums, coming
        self.core_sems, self.axis_sems, self.base = core_sems, axis_sems, base
        self.chips = size // 2
        self.bits = size.bit_length() - 2
        bits = list(range(self.bits))
        self.orders = (bits, bits[::-1])

    def core_copy(self):
        me = lax.axis_index("seq")
        send, recv = self.core_sems
        return remote(self.to_core, self.sums, send, recv, {"seq": me ^ 1})

    def away(self, terms):
        def write(columns, y):
            self.to_core[:, :, columns] = y.astype(BF)

        terms(1 - (lax.axis_index("seq") & 1), write)
        self.core_copy().start()

    def here(self, terms):
        self.core_copy().wait_recv()

        def write(columns, y):
            self.sums[:, :, columns] = (y + self.sums[:, :, columns].astype(F32)).astype(BF)

        terms(lax.axis_index("seq") & 1, write)
        self.start(0)

    def copies(self, part, stage):
        me = lax.axis_index("seq")
        half = self.width // 2
        bit = self.orders[part][stage]
        done = sum(1 << b for b in self.orders[part][:stage])
        first = self.chips - (self.chips >> stage)
        columns = slice(part * half, (part + 1) * half)
        send, recv = self.axis_sems
        found = []
        for mask in range(self.chips):
            if mask & (done | (1 << bit)):
                continue
            slot = first + len(found)
            number = self.base + part * (self.chips - 1) + slot
            copy = remote(
                self.sums.at[(me >> 1) ^ (mask | (1 << bit)), :, columns],
                self.coming.at[slot, :, columns],
                send.at[number],
                recv.at[number],
                {"seq": me ^ (2 << bit)},
            )
            found.append((mask, slot, copy))
        return found

    def start(self, stage):
        for part in range(2):
            for _, _, copy in self.copies(part, stage):
                copy.start()

    def add(self, stage):
        half = self.width // 2
        for part in range(2):
            columns = slice(part * half, (part + 1) * half)
            for mask, slot, copy in self.copies(part, stage):
                copy.wait_recv()
                if stage < self.bits - 1:
                    block = (lax.axis_index("seq") >> 1) ^ mask
                    self.sums[block, :, columns] = (
                        self.sums[block, :, columns].astype(F32)
                        + self.coming[slot, :, columns].astype(F32)
                    ).astype(BF)

    def step(self, stage):
        self.add(stage)
        if stage + 1 < self.bits:
            self.start(stage + 1)

    def last(self):
        chip = lax.axis_index("seq") >> 1
        return self.sums[chip].astype(F32) + self.coming[self.chips - 2].astype(F32)

    def core_sent(self):
        self.core_copy().wait_send()

    def sent(self):
        for part in range(2):
            for stage in range(self.bits):
                for _, _, copy in self.copies(part, stage):
                    copy.wait_send()


def load_kernel(
    dims,
    tokens_ref,
    up_ref,
    one_ref,
    two_ref,
    vec_ref,
    normed_ref,
    all_up_ref,
    my_one_ref,
    my_two_ref,
    full_ref,
    gathered,
    normed_v,
    vec_seq,
    vec_sum,
    vec_all,
    local_sem,
    vec_send,
    vec_recv,
    a2a_send,
    a2a_recv,
    line_send,
    line_recv,
    row_send,
    row_recv,
):
    size, depth, micro, length, width, units, cols = dims
    me, at = lax.axis_index("seq"), lax.axis_index("fsdp")
    count = size.bit_length() - 1
    half = width // 2

    def seq(step):
        return {"seq": me ^ step}

    def line(step):
        return {"fsdp": lax.rem(at + step, depth)}

    greet(size, depth)

    def vec_seq_copy(step):
        return remote(
            vec_sum.at[step],
            vec_seq.at[step],
            vec_send.at[step],
            vec_recv.at[step],
            seq(1 << step),
        )

    def vec_line_copy(step):
        number = size + step
        return remote(
            vec_sum.at[count], vec_all.at[step], vec_send.at[number], vec_recv.at[number], line(step)
        )

    def one_copy(step):
        peer = me ^ step
        return remote(
            one_ref.at[:, pl.ds(pl.multiple_of(peer * units, 128), units)],
            my_one_ref.at[me, at],
            a2a_send.at[step],
            a2a_recv.at[step],
            seq(step),
        )

    local = [
        pltpu.make_async_copy(
            one_ref.at[:, pl.ds(pl.multiple_of(me * units, 128), units)],
            my_one_ref.at[me, at],
            local_sem.at[0],
        ),
        pltpu.make_async_copy(
            tokens_ref,
            gathered.at[:, store_index(me)],
            local_sem.at[1],
        ),
        pltpu.make_async_copy(
            up_ref,
            all_up_ref.at[:, store_index(me)],
            local_sem.at[2],
        ),
    ]
    local.append(pltpu.make_async_copy(two_ref, my_two_ref.at[at], local_sem.at[3]))

    def one_line(step, way):
        origin = jnp.clip(at - way * (step - 1), 0, depth - 1)
        number = 2 * step + (way > 0)
        piece = my_one_ref.at[:, origin]
        ok = (at + way >= 0) & (at + way < depth)
        ok = ok & (at - way * (step - 1) >= 0) & (at - way * (step - 1) < depth)
        return ok, remote(
            piece,
            piece,
            line_send.at[number],
            line_recv.at[number],
            {"fsdp": jnp.clip(at + way, 0, depth - 1)},
        )

    def one_arrives(step, way):
        ok = (at - way * step >= 0) & (at - way * step < depth)
        return ok, one_line(step, way)[1]

    def two_line(way):
        ok = (at + way >= 0) & (at + way < depth)
        number = way > 0
        return ok, remote(
            two_ref,
            my_two_ref.at[at],
            line_send.at[int(number)],
            line_recv.at[int(number)],
            {"fsdp": jnp.clip(at + way, 0, depth - 1)},
        )

    def two_arrives(way):
        return (at - way >= 0) & (at - way < depth), two_line(way)[1]

    def start(pair):
        ok, copy = pair

        @pl.when(ok)
        def _():
            copy.start()

    def wait_recv(pair):
        ok, copy = pair

        @pl.when(ok)
        def _():
            copy.wait_recv()

    def wait_send(pair):
        ok, copy = pair

        @pl.when(ok)
        def _():
            copy.wait_send()

    sources = (tokens_ref, up_ref)
    targets = (gathered, all_up_ref)
    orders = (list(range(1, count)), list(range(1, count))[::-1])

    def row_copy(which, part, mask, bit):
        columns = slice(part * half, (part + 1) * half)
        block = store_index(me ^ mask)
        if mask == 0:
            src = sources[which].at[:, :, columns]
        else:
            src = targets[which].at[:, block, :, columns]
        number = (which * 2 + part) * size + (mask | (1 << bit))
        return remote(
            src,
            targets[which].at[:, block, :, columns],
            row_send.at[number],
            row_recv.at[number],
            seq(1 << bit),
        )

    def row_stage(which, part, stage):
        order = orders[part]
        masks = [0]
        for bit in order[:stage]:
            masks = masks + [mask | (1 << bit) for mask in masks]
        return [row_copy(which, part, mask, order[stage]) for mask in masks]

    def row_cores(which, part, stage):
        order = orders[part]
        masks = [0]
        new = [0]
        for bit in order[: stage + 1]:
            new = [mask | (1 << bit) for mask in masks]
            masks = masks + new
        return [row_copy(which, part, mask, 0) for mask in new]

    def both_parts(function, which, stage):
        return function(which, 0, stage) + function(which, 1, stage)

    def issue(copies):
        for copy in copies:
            copy.start()

    def arrive(copies):
        for copy in copies:
            copy.wait_recv()

    def vec_stage(step):
        vec_seq_copy(step).wait_recv()
        total = vec_sum[step].astype(F32) + vec_seq[step].astype(F32)
        vec_sum[step + 1] = total.astype(BF)

    issue(one_copy(step) for step in range(1, size))
    for way in (1, -1):
        start(two_line(way))
    issue(local)
    vec_sum[0] = vec_ref[...]
    vec_seq_copy(0).start()
    issue(both_parts(row_cores, 0, -1))
    vec_stage(0)
    vec_seq_copy(1).start()
    arrive(one_copy(step) for step in range(1, size))
    local[0].wait()
    for way in (1, -1):
        start(one_line(1, way))
    for which in range(2):
        issue(both_parts(row_stage, which, 0))
    for step in range(1, count):
        vec_stage(step)
        if step + 1 < count:
            vec_seq_copy(step + 1).start()
    issue(vec_line_copy(step) for step in range(1, depth))

    def line_on(step):
        for way in (1, -1):
            wait_recv(one_arrives(step, way))
            start(one_line(step + 1, way))

    line_step = 1
    for stage in range(count - 1):
        for which in range(2):
            arrive(both_parts(row_stage, which, stage))
            if stage + 1 < count - 1:
                issue(both_parts(row_stage, which, stage + 1))
            issue(both_parts(row_cores, which, stage))
            if stage == 0 and which == 0:
                issue(both_parts(row_cores, 1, -1))
                arrive(vec_line_copy(step) for step in range(1, depth))
                summed = vec_sum[count].astype(F32)
                for step in range(1, depth):
                    summed = summed + vec_all[step].astype(F32)
                full_ref[...] = summed
            elif which == 0 or stage == 0:
                if line_step < depth - 1:
                    line_on(line_step)
                    line_step += 1
            if stage == count - 2 and which == 0:
                while line_step < depth - 1:
                    line_on(line_step)
                    line_step += 1
                local[1].wait()
                for step in range(-1, count - 1):
                    arrive(both_parts(row_cores, 0, step))
                gain = full_ref[0:1, :]
                shift = full_ref[1:2, :]

                @pl.loop(0, micro * size)
                def _(index):
                    m, block = index // size, lax.rem(index, size)
                    x = gathered[m, block].astype(F32)
                    center = x - jnp.mean(x, axis=-1, keepdims=True)
                    spread = jnp.mean(center * center, axis=-1, keepdims=True)
                    y = center * lax.rsqrt(spread + EPSILON) * gain + shift
                    normed_v[m, block] = y.astype(BF)

                normed_out = pltpu.make_async_copy(normed_v, normed_ref, local_sem.at[4])
                normed_out.start()

    for copy in local[2:]:
        copy.wait()
    normed_out.wait()
    for stage in range(-1, count - 1):
        arrive(both_parts(row_cores, 1, stage))
    for way in (1, -1):
        wait_recv(two_arrives(way))
        wait_recv(one_arrives(depth - 1, way))

    for step in range(count):
        vec_seq_copy(step).wait_send()
    for step in range(1, size):
        one_copy(step).wait_send()
    for step in range(1, depth):
        vec_line_copy(step).wait_send()
        for way in (1, -1):
            wait_send(one_line(step, way))
    for way in (1, -1):
        wait_send(two_line(way))
    for which in range(2):
        for stage in range(-1, count - 1):
            for copy in both_parts(row_cores, which, stage):
                copy.wait_send()
            if stage >= 0:
                for copy in both_parts(row_stage, which, stage):
                    copy.wait_send()


def load_all(tokens, upstream, w_fc1, w_fc2, vectors):
    size, depth = lax.axis_size("seq"), lax.axis_size("fsdp")
    micro, length, width = tokens.shape
    rows, units, cols = w_fc1.shape[0], w_fc1.shape[1] // size, width // size
    dims = (size, depth, micro, length, width, units, cols)
    hbm = pl.BlockSpec(memory_space=pl.ANY)
    vmem = pl.BlockSpec(memory_space=pltpu.VMEM)
    gathered = (micro, size, length, width)
    dma = pltpu.SemaphoreType.DMA
    return pl.pallas_call(
        functools.partial(load_kernel, dims),
        in_specs=[hbm] * 4 + [vmem],
        out_specs=[hbm] * 4 + [vmem],
        out_shape=[
            jax.ShapeDtypeStruct(gathered, BF),
            jax.ShapeDtypeStruct(gathered, BF),
            jax.ShapeDtypeStruct((size, depth, rows, units), BF),
            jax.ShapeDtypeStruct((depth,) + w_fc2.shape, BF),
            jax.ShapeDtypeStruct(vectors.shape, F32),
        ],
        scratch_shapes=[
            pltpu.VMEM(gathered, BF),
            pltpu.VMEM(gathered, BF),
            pltpu.VMEM((size,) + vectors.shape, BF),
            pltpu.VMEM((size,) + vectors.shape, BF),
            pltpu.VMEM((depth,) + vectors.shape, BF),
            dma((5,)),
            dma((size + depth,)),
            dma((size + depth,)),
            dma((size,)),
            dma((size,)),
            dma((2 * depth + 2,)),
            dma((2 * depth + 2,)),
            dma((4 * size,)),
            dma((4 * size,)),
        ],
        compiler_params=pltpu.CompilerParams(
            collective_id=1, has_side_effects=True, vmem_limit_bytes=60 * 1024 * 1024
        ),
        cost_estimate=pl.CostEstimate(
            flops=1000, bytes_accessed=300 * 1000 * 1000, transcendentals=0
        ),
    )(tokens, upstream, w_fc1, w_fc2, vectors)


def ffn_kernel(
    dims,
    normed_hbm,
    up_hbm,
    one_hbm,
    two_hbm,
    qkv_hbm,
    out_hbm,
    full_ref,
    part_grad_hbm,
    part_act_hbm,
    attn_hbm,
    grad_two_hbm,
    grad_one_hbm,
    land_two,
    land_one,
    bone_ref,
    btwo_ref,
    normed_v,
    up_v,
    one_v,
    two_v,
    hidden_v,
    pre_v,
    grad_two_v,
    grad_one_v,
    own_one,
    held_one,
    out_one,
    load_sem,
    line_load,
    store_sem,
    two_send,
    two_recv,
    attn_send,
    attn_recv,
    sum_two_send,
    sum_two_recv,
    sum_one_send,
    sum_one_recv,
    a2a_send,
    a2a_recv,
    local_sem,
):
    size, depth, micro, length, width, units, cols = dims
    me, at = lax.axis_index("seq"), lax.axis_index("fsdp")
    count = micro * size * length
    per = width // size
    tile = 512
    group = units // depth

    loads = [
        pltpu.make_async_copy(src, dst, load_sem.at[n])
        for n, (src, dst) in enumerate(
            ((normed_hbm, normed_v), (one_hbm, one_v), (up_hbm, up_v))
        )
    ]
    for load in loads:
        load.start()

    def two_load(way):
        origin = jnp.clip(at + way, 0, depth - 1)
        return (at + way >= 0) & (at + way < depth), pltpu.make_async_copy(
            two_hbm.at[origin], two_v.at[origin], load_sem.at[4 + way]
        )

    for way in (0, 1, -1):
        ok, copy = two_load(way)

        @pl.when(ok)
        def _():
            copy.start()

    def qkv_part(peer, part):
        return qkv_hbm.at[:, pl.ds(pl.multiple_of(part * width + peer * cols, 128), cols)]

    def qkv_copy(step, part):
        number = part * size + step
        return remote(
            qkv_part(me ^ step, part),
            attn_hbm.at[me, at, :, pl.ds(part * cols, cols)],
            a2a_send.at[number],
            a2a_recv.at[number],
            {"seq": me ^ step},
        )

    local = [
        pltpu.make_async_copy(
            qkv_part(me, part), attn_hbm.at[me, at, :, pl.ds(part * cols, cols)], local_sem.at[part]
        )
        for part in range(3)
    ] + [
        pltpu.make_async_copy(
            out_hbm.at[:, pl.ds(peer * cols, cols)],
            attn_hbm.at[peer, at, :, pl.ds(3 * cols, cols)],
            local_sem.at[3 + peer],
        )
        for peer in range(size)
    ]
    for copy in local:
        copy.start()
    greet(size, depth)

    two = LineGather(
        depth,
        lambda o, step: two_hbm.at[o] if step == 2 else two_v.at[o],
        lambda o: two_v.at[o],
        two_send,
        two_recv,
    )
    attn = LineGather(
        depth,
        lambda o, step: attn_hbm.at[:, o],
        lambda o: attn_hbm.at[:, o],
        attn_send,
        attn_recv,
    )
    sum_two = LineSum(
        depth,
        lambda o: grad_two_v.at[o],
        lambda step, way: land_two.at[int(way > 0)],
        own_one,
        held_one,
        lambda step, way: grad_two_v.at[0],
        line_load,
        sum_two_send,
        sum_two_recv,
    )
    sum_one = LineSum(
        depth,
        lambda o: grad_one_v.at[:, o],
        lambda step, way: land_one.at[(step - 1) * 2 + (way > 0)],
        own_one,
        held_one,
        lambda step, way: out_one.at[int(way > 0)],
        line_load,
        sum_one_send,
        sum_one_recv,
    )
    two.start(2)
    for part in range(3):
        for step in range(1, size):
            qkv_copy(step, part).start()

    for load in loads[:2]:
        load.wait()
    root = math.sqrt(2.0 / math.pi)
    flat = me * units
    bias_row = 6 + flat // width
    bias_at = pl.multiple_of(lax.rem(flat, width), units)
    bias = full_ref[pl.ds(bias_row, 1), pl.ds(bias_at, units)]
    bone_ref[...] = bias

    @pl.loop(0, count // tile)
    def _(r):
        rows = pl.ds(pl.multiple_of(r * tile, tile), tile)
        a = normed_v[rows, :]
        for o in range(depth):
            columns = slice(o * group, (o + 1) * group)
            w = one_v[:, :, :, columns].reshape(width, group)
            v = jnp.dot(a, w, preferred_element_type=F32) + bone_ref[:, columns]
            square = v * v
            t = jnp.tanh(root * v * (1.0 + 0.044715 * square))
            hidden_v[rows, columns] = (0.5 * v * (1.0 + t)).astype(BF)
            slope = 0.5 * (1.0 + t) + 0.5 * root * v * (1.0 - t * t) * (
                1.0 + 3 * 0.044715 * square
            )
            pre_v[rows, columns] = slope.astype(BF)

    loads[2].wait()
    over_first = (((0,), (0,)), ((), ()))
    over_last = (((1,), (1,)), ((), ()))

    @pl.loop(0, depth)
    def _(o):
        columns = pl.ds(pl.multiple_of(o * group, group), group)
        y = lax.dot_general(hidden_v[:, columns], up_v[...], over_first, preferred_element_type=F32)
        grad_two_v[o] = y.astype(BF)

    two.arrive(2)
    two.start(3)
    sum_two.source(1)
    grad_two_out = pltpu.make_async_copy(grad_two_v, grad_two_hbm, store_sem.at[2])
    grad_two_out.start()
    bone_ref[...] = jnp.zeros_like(bone_ref)

    def piece(o):
        columns = pl.ds(pl.multiple_of(o * group, group), group)

        @pl.loop(0, count // tile)
        def _(r):
            rows = pl.ds(pl.multiple_of(r * tile, tile), tile)
            y = lax.dot_general(up_v[rows, :], two_v[o], over_last, preferred_element_type=F32)
            y = (y * pre_v[rows, columns].astype(F32)).astype(BF)
            pre_v[rows, columns] = y
            bone_ref[:, columns] += jnp.sum(y.astype(F32), axis=0, keepdims=True)

        wide = 1024

        @pl.loop(0, width // wide)
        def _(d):
            rows = pl.ds(pl.multiple_of(d * wide, wide), wide)
            y = lax.dot_general(
                normed_v[:, rows], pre_v[:, columns], over_first, preferred_element_type=F32
            )
            n = wide // per
            y = y.astype(BF).reshape(n, depth, per // depth, group)
            grad_one_v[pl.ds(d * n, n), :, :, columns] = y

    for way in (0, 1, -1):
        ok, copy = two_load(way)

        @pl.when(ok)
        def _():
            copy.wait()

    @pl.loop(0, 2 * depth - 3)
    def _(number):
        distance = (number + 1) // 2
        origin = jnp.where(lax.rem(number, 2) == 1, at - distance, at + distance)

        @pl.when((origin >= 0) & (origin < depth))
        def _():
            piece(jnp.clip(origin, 0, depth - 1))

    for copy in local:
        copy.wait()
    for part in range(3):
        for step in range(1, size):
            qkv_copy(step, part).wait_recv()
    two.arrive(3)
    attn.start(1)

    @pl.loop(2 * depth - 3, 2 * depth - 1)
    def _(number):
        distance = (number + 1) // 2
        origin = jnp.where(lax.rem(number, 2) == 1, at - distance, at + distance)

        @pl.when((origin >= 0) & (origin < depth))
        def _():
            piece(jnp.clip(origin, 0, depth - 1))

    sum_one.source(1)
    sum_one.source(2)
    grad_one_out = pltpu.make_async_copy(grad_one_v, grad_one_hbm, store_sem.at[5])
    grad_one_out.start()

    btwo_ref[...] = jnp.zeros_like(btwo_ref)
    for m in range(micro):
        mine = pl.multiple_of((m * size + store_index(me)) * length, length)
        rows = up_v[pl.ds(mine, length), :].astype(F32)
        btwo_ref[...] += jnp.sum(rows, axis=0, keepdims=True)

    @pl.loop(0, count // tile)
    def _(r):
        rows = pl.ds(pl.multiple_of(r * tile, tile), tile)
        a = pre_v[rows, :]
        for s in range(size):
            w = one_v[s].reshape(per, units)
            y = lax.dot_general(a, w, over_last, preferred_element_type=F32)
            normed_v[rows, s * per : (s + 1) * per] = y.astype(BF)

    part_grad = pltpu.make_async_copy(normed_v, part_grad_hbm, store_sem.at[3])
    part_grad.start()
    attn.arrive(1)
    attn.start(2)

    @pl.loop(0, count // tile)
    def _(r):
        rows = pl.ds(pl.multiple_of(r * tile, tile), tile)
        a = hidden_v[rows, :]
        for s in range(size):
            columns = slice(s * per, (s + 1) * per)
            w = two_v[:, :, columns].reshape(units, per)
            up_v[rows, columns] = jnp.dot(a, w, preferred_element_type=F32).astype(BF)

    part_act = pltpu.make_async_copy(up_v, part_act_hbm, store_sem.at[4])
    part_act.start()
    attn.arrive(2)
    attn.start(3)
    sum_one.forward(2)
    grad_two_out.wait()
    for store in (grad_one_out, part_grad, part_act):
        store.wait()
    attn.arrive(3)
    sum_two.arrive(1, False)
    sum_one.arrive(1, True)
    sum_one.arrive(2, False)
    for step in (2, 3):
        two.sent(step)
    for step in (1, 2, 3):
        attn.sent(step)
    sum_two.sent(1)
    sum_one.sent(1)
    sum_one.sent(2)
    for part in range(3):
        for step in range(1, size):
            qkv_copy(step, part).wait_send()


def feed_forward(normed, up, one, two, w_qkv, w_out, full):
    size, depth = lax.axis_size("seq"), lax.axis_size("fsdp")
    micro, _, length, width = normed.shape
    units, cols = one.shape[-1], width // size
    rows = width // (size * depth)
    count = micro * size * length
    dims = (size, depth, micro, length, width, units, cols)
    hbm = pl.BlockSpec(memory_space=pl.ANY)
    vmem = pl.BlockSpec(memory_space=pltpu.VMEM)
    dma = pltpu.SemaphoreType.DMA
    sums = dma((2 * depth,))
    shape = jax.ShapeDtypeStruct
    tall, deep = (depth, units // depth, width), (size, depth, rows, units)
    return pl.pallas_call(
        functools.partial(ffn_kernel, dims),
        in_specs=[hbm] * 6 + [vmem],
        out_specs=[hbm] * 7 + [vmem] * 2,
        out_shape=[
            shape((count, width), BF),
            shape((count, width), BF),
            shape((size, depth, rows, 4 * cols), BF),
            shape(tall, BF),
            shape(deep, BF),
            shape((2,) + tall[1:], BF),
            shape((4, size, rows, units), BF),
            shape((1, units), F32),
            shape((1, width), F32),
        ],
        scratch_shapes=[
            pltpu.VMEM((count, width), BF),
            pltpu.VMEM((count, width), BF),
            pltpu.VMEM(deep, BF),
            pltpu.VMEM(tall, BF),
            pltpu.VMEM((count, units), BF),
            pltpu.VMEM((count, units), BF),
            pltpu.VMEM(tall, BF),
            pltpu.VMEM(deep, BF),
            pltpu.VMEM((size, rows, units), BF),
            pltpu.VMEM((size, rows, units), BF),
            pltpu.VMEM((2, size, rows, units), BF),
            dma((6,)),
            dma((2,)),
            dma((6,)),
        ]
        + [sums] * 8
        + [dma((3 * size,)), dma((3 * size,)), dma((3 + size,))],
        compiler_params=pltpu.CompilerParams(
            collective_id=2, has_side_effects=True, vmem_limit_bytes=60 * 1024 * 1024
        ),
        cost_estimate=pl.CostEstimate(
            flops=34 * 1000**3, bytes_accessed=300 * 1000 * 1000, transcendentals=0
        ),
    )(
        normed.reshape(count, width),
        up.reshape(count, width),
        one,
        two,
        w_qkv,
        w_out,
        full,
    )


def attn_layer_kernel(
    dims,
    starts_ref,
    cos_ref,
    sin_ref,
    normed_hbm,
    up_hbm,
    attn_hbm,
    grad_two_hbm,
    grad_one_hbm,
    old_two,
    old_one,
    part_act_hbm,
    tokens_hbm,
    full_ref,
    turned_hbm,
    mixed_hbm,
    grads_hbm,
    spread_hbm,
    land_two,
    land_one,
    bqkv_ref,
    two_ref,
    act_ref,
    normed_v,
    up_v,
    attn_v,
    natural_v,
    turned_v,
    mixed_v,
    grads_v,
    dk_s,
    dv_s,
    bias_s,
    own_two,
    held_two,
    out_two,
    one_total,
    held_one,
    part_act_v,
    tokens_v,
    to_core,
    act_sums,
    act_coming,
    load_sem,
    line_load,
    store_sem,
    sum_two_send,
    sum_two_recv,
    sum_one_send,
    sum_one_recv,
    a2a_send,
    a2a_recv,
    core_sem,
    axis_send,
    axis_recv,
):
    size, depth, micro, length, width, units, cols = dims
    me = lax.axis_index("seq")
    chips = size // 2
    groups = cols // LANES
    total = size * length
    count = micro * total
    per = width // size
    loads = [
        pltpu.make_async_copy(src, dst, load_sem.at[n])
        for n, (src, dst) in enumerate(
            ((normed_hbm, normed_v), (attn_hbm, attn_v), (up_hbm, up_v))
        )
    ]
    for load in loads:
        load.start()
    greet(size, depth)
    sum_two = LineSum(
        depth,
        lambda o: grad_two_hbm.at[o],
        lambda step, way: (
            old_two.at[int(way > 0)] if step < 2 else land_two.at[(step - 2) * 2 + (way > 0)]
        ),
        own_two,
        held_two,
        lambda step, way: out_two.at[int(way > 0)],
        line_load,
        sum_two_send,
        sum_two_recv,
    )
    sum_one = LineSum(
        depth,
        lambda o: grad_one_hbm.at[:, o],
        lambda step, way: (
            old_one.at[(step - 1) * 2 + (way > 0)] if step < 3 else land_one.at[int(way > 0)]
        ),
        one_total,
        held_one.at[0],
        lambda step, way: held_one.at[1 + (way > 0)],
        line_load,
        sum_one_send,
        sum_one_recv,
    )
    sum_one.source(3)
    sum_two.source(2)
    sum_two.source(3)
    sum_one.forward(3, here=False)
    sum_two.forward(2, here=False)
    tokens_load = pltpu.make_async_copy(tokens_hbm.at[0], tokens_v, load_sem.at[4])
    tokens_load.start()

    def part_act_half(parity):
        blocks = pl.ds(parity * chips, chips)
        return pltpu.make_async_copy(part_act_hbm.at[0, blocks], part_act_v, load_sem.at[3])

    part_act_half(1 - (me & 1)).start()

    def spread_copy(step):
        peer = me ^ step
        return remote(
            one_total.at[peer],
            spread_hbm.at[me],
            a2a_send.at[step],
            a2a_recv.at[step],
            {"seq": peer},
        )

    spread_mine = pltpu.make_async_copy(one_total.at[me], spread_hbm.at[me], store_sem.at[3])
    act = SeqSum(
        size,
        width,
        to_core,
        act_sums,
        act_coming,
        (core_sem.at[0], core_sem.at[1]),
        (axis_send, axis_recv),
        0,
    )

    def act_terms(parity, write):
        first = pl.multiple_of(parity * chips * length, chips * length)
        mine = mixed_v[pl.ds(first, chips * length), :]

        @pl.loop(0, size)
        def _(s):
            columns = pl.ds(pl.multiple_of(s * per, per), per)
            w = attn_v[s, :, :, 3 * cols :].reshape(cols, cols)
            y = jnp.dot(mine, w, preferred_element_type=F32).reshape(chips, length, per)
            write(columns, y + part_act_v[:, :, columns].astype(F32))

    for load in loads:
        load.wait()

    lane = lax.broadcasted_iota(jnp.int32, (1, LANES), 1)
    low_lane = (lane % HEAD_DIM) < (ROT // 2)
    over_first = (((0,), (0,)), ((), ()))
    over_last = (((1,), (1,)), ((), ()))

    def turn(value, cosine, sine):
        other = jnp.where(
            low_lane,
            pltpu.roll(value, LANES - ROT // 2, 1),
            pltpu.roll(value, ROT // 2, 1),
        )
        return value * cosine + other * sine

    high = chips * length

    @pl.loop(0, micro * 2)
    def _(r):
        m, parity = r // 2, lax.rem(r, 2)
        rows = pl.ds(pl.multiple_of(r * high, high), high)
        a = normed_v[rows, :]
        u = up_v[rows, :]
        for part in range(3):
            w = attn_v[:, :, :, part * cols : (part + 1) * cols].reshape(width, cols)
            y = jnp.dot(a, w, preferred_element_type=F32)
            y = y + full_ref[2 + part : 3 + part, pl.ds(pl.multiple_of(me * cols, cols), cols)]
            for block in range(chips):
                at = pl.ds(pl.multiple_of((block * 2 + parity) * length, length), length)
                cosine, sine = cos_ref[at, :], sin_ref[at, :]
                for g in range(groups):
                    v = y[block * length : (block + 1) * length, g * LANES : (g + 1) * LANES]
                    if part < 2:
                        v = turn(v, cosine, sine)
                    v = v.astype(BF)
                    if part == 0:
                        v = v * jnp.asarray(SCALE, BF)
                    natural_v[part, m, g, at, :] = v
        y = jnp.zeros((high, cols), F32)
        for s in range(size):
            w = attn_v[s, :, :, 3 * cols :].reshape(cols, cols)
            y = y + lax.dot_general(
                u[:, s * per : (s + 1) * per], w, over_last, preferred_element_type=F32
            )
        for block in range(chips):
            at = pl.ds(pl.multiple_of((block * 2 + parity) * length, length), length)
            for g in range(groups):
                v = y[block * length : (block + 1) * length, g * LANES : (g + 1) * LANES]
                natural_v[3, m, g, at, :] = v.astype(BF)

    tile = 256

    @pl.loop(0, micro * groups)
    def _(index):
        m, g = index // groups, lax.rem(index, groups)

        @pl.when(index == 2)
        def _():
            sum_one.sent(3)
            total = sum_one.total(3, held_one.at[0], held_one.at[1])
            one_total[...] = total.astype(BF)
            for step in range(1, size):
                spread_copy(step).start()
            spread_mine.start()
            tokens_load.wait()

        @pl.when(index == groups)
        def _():
            part_act_half(1 - (me & 1)).wait()
            act.away(act_terms)
            part_act_half(me & 1).start()

        @pl.when(index == micro * groups - 1)
        def _():
            part_act_half(me & 1).wait()
            act.here(act_terms)
            sum_two.sent_on(2)
            sum_two.forward(3)

        def label(positions):
            found = jnp.full(positions.shape, -1, jnp.int32)
            for piece in range(PIECES):
                start = starts_ref[m, piece]
                found = jnp.where((positions >= start) & (positions < start + IMG), piece, found)
            return found

        def put(target, at, columns, value):
            for part in range(value.shape[0] // length):
                block = at // length + part
                rows = m * total + store_index(block) * length
                target[pl.ds(pl.multiple_of(rows, length), length), columns] = value[
                    part * length : (part + 1) * length
                ].astype(BF)

        def columns_of(part):
            return pl.ds(pl.multiple_of(part * cols + g * LANES, LANES), LANES)

        dk_s[...] = jnp.zeros_like(dk_s)
        dv_s[...] = jnp.zeros_like(dv_s)
        for first in range(0, total, tile):
            last = min(total, first + tile + IMG)
            qpos = first + lax.broadcasted_iota(jnp.int32, (tile, 1), 0)
            kpos = first + lax.broadcasted_iota(jnp.int32, (1, last - first), 1)
            qlab, klab = label(qpos), label(kpos)
            allowed = (kpos <= qpos) | ((qlab == klab) & (qlab >= 0))
            bias_s[:, : last - first] = jnp.where(allowed, 0.0, -1e30)
            rows = slice(first, first + tile)
            keys = natural_v[1, m, g, :last, :]
            values = natural_v[2, m, g, :last, :]
            heads = [(lane // HEAD_DIM) == head for head in range(LANES // HEAD_DIM)]
            q = jnp.concatenate([jnp.where(h, natural_v[0, m, g, rows, :], 0) for h in heads])
            do = jnp.concatenate([jnp.where(h, natural_v[3, m, g, rows, :], 0) for h in heads])
            s = lax.dot_general(q, keys, over_last, preferred_element_type=F32)
            bias = jnp.concatenate([bias_s[:, : last - first]] * len(heads))
            if first:
                s = jnp.concatenate([s[:, :first], s[:, first:] + bias], axis=1)
            else:
                s = s + bias
            p = jnp.exp(s - jnp.max(s, axis=1, keepdims=True))
            p = p * (1.0 / jnp.sum(p, axis=1, keepdims=True))
            probs = p.astype(BF)
            dp = lax.dot_general(do, values, over_last, preferred_element_type=F32)
            att = jnp.dot(probs, values, preferred_element_type=F32)
            delta = jnp.sum(p * dp, axis=1, keepdims=True)
            ds = (p * (dp - delta)).astype(BF)
            mixed = jnp.where(heads[0], att[:tile], att[tile:])
            dq = jnp.dot(ds, keys, preferred_element_type=F32)
            dq = jnp.where(heads[0], dq[:tile], dq[tile:])
            dk_s[:last, :] += lax.dot_general(ds, q, over_first, preferred_element_type=F32)
            dv_s[:last, :] += lax.dot_general(probs, do, over_first, preferred_element_type=F32)
            put(mixed_v, first, pl.ds(pl.multiple_of(g * LANES, LANES), LANES), mixed)
            dq = turn(dq * SCALE, cos_ref[rows, :], -sin_ref[rows, :])
            put(turned_v, first, columns_of(0), dq)
        put(turned_v, 0, columns_of(1), turn(dk_s[...], cos_ref[...], -sin_ref[...]))
        put(turned_v, 0, columns_of(2), dv_s[...])

    stores = [
        pltpu.make_async_copy(turned_v, turned_hbm, store_sem.at[0]),
        pltpu.make_async_copy(mixed_v, mixed_hbm, store_sem.at[1]),
    ]
    for store in stores:
        store.start()
    bits = size.bit_length() - 2
    for stage in range(bits - 1):
        act.step(stage)

    wide = 512

    @pl.loop(0, width // wide)
    def _(d):
        rows = pl.ds(pl.multiple_of(d * wide, wide), wide)
        y = lax.dot_general(normed_v[:, rows], turned_v[...], over_first, preferred_element_type=F32)
        n = wide // per
        grads_v[pl.ds(d * n, n), :, :, : 3 * cols] = y.astype(BF).reshape(
            n, depth, per // depth, 3 * cols
        )
        y = lax.dot_general(mixed_v[...], up_v[:, rows], over_first, preferred_element_type=F32)
        y = y.astype(BF)
        for k in range(n):
            grads_v[d * n + k, :, :, 3 * cols :] = y[:, k * per : (k + 1) * per].reshape(
                depth, cols // depth, per
            )

    grads_out = pltpu.make_async_copy(grads_v, grads_hbm, store_sem.at[2])
    grads_out.start()
    bqkv_ref[...] = jnp.sum(turned_v[...].astype(F32), axis=0, keepdims=True)
    act.add(bits - 1)
    bias = full_ref[5:6, :] + full_ref[6 + size * units // width : 7 + size * units // width, :]
    act_ref[...] = (tokens_v[...].astype(F32) + act.last() + bias).astype(BF)
    sum_two.sent_first(2)
    sum_two.sent(3)
    two_ref[...] = sum_two.total(3, held_two, out_two.at[0])
    for store in stores:
        store.wait()
    grads_out.wait()
    spread_mine.wait()
    for step in range(1, size):
        spread_copy(step).wait_recv()
        spread_copy(step).wait_send()
    act.core_sent()
    act.sent()


def attention_layer(
    starts, normed, up, attn, grad_two, grad_one, old_two, old_one, part_act, tokens, full
):
    size, depth, rows, units = grad_one.shape
    micro, _, length, width = normed.shape
    cols = width // size
    count, total = micro * size * length, size * length
    dims = (size, depth, micro, length, width, units, cols)
    cosine, sine = tables(total)
    chips = size // 2
    hbm = pl.BlockSpec(memory_space=pl.ANY)
    vmem = pl.BlockSpec(memory_space=pltpu.VMEM)
    dma = pltpu.SemaphoreType.DMA
    sums = dma((2 * depth,))
    shape = jax.ShapeDtypeStruct
    tall, deep = (units // depth, width), (size, rows, units)
    return pl.pallas_call(
        functools.partial(attn_layer_kernel, dims),
        in_specs=[pl.BlockSpec(memory_space=pltpu.SMEM)] + [vmem] * 2 + [hbm] * 9 + [vmem],
        out_specs=[hbm] * 6 + [vmem] * 3,
        out_shape=[
            shape((count, 3 * cols), BF),
            shape((count, cols), BF),
            shape(attn.shape, BF),
            shape(deep, BF),
            shape((4,) + tall, BF),
            shape((2,) + deep, BF),
            shape((1, 3 * cols), F32),
            shape(tall, F32),
            shape((length, width), BF),
        ],
        scratch_shapes=[
            pltpu.VMEM((count, width), BF),
            pltpu.VMEM((count, width), BF),
            pltpu.VMEM(attn.shape, BF),
            pltpu.VMEM((4, micro, cols // LANES, total, LANES), BF),
            pltpu.VMEM((count, 3 * cols), BF),
            pltpu.VMEM((count, cols), BF),
            pltpu.VMEM(attn.shape, BF),
            pltpu.VMEM((total, LANES), F32),
            pltpu.VMEM((total, LANES), F32),
            pltpu.VMEM((256, 512), F32),
            pltpu.VMEM(tall, BF),
            pltpu.VMEM(tall, BF),
            pltpu.VMEM((2,) + tall, BF),
            pltpu.VMEM(deep, BF),
            pltpu.VMEM((3,) + deep, BF),
            pltpu.VMEM((chips, length, width), BF),
            pltpu.VMEM((length, width), BF),
            pltpu.VMEM((chips, length, width), BF),
            pltpu.VMEM((chips, length, width), BF),
            pltpu.VMEM((chips - 1, length, width), BF),
            dma((5,)),
            dma((2,)),
            dma((4,)),
        ]
        + [sums] * 4
        + [dma((size,)), dma((size,)), dma((2,))]
        + [dma((2 * (chips - 1),))] * 2,
        compiler_params=pltpu.CompilerParams(
            collective_id=3, has_side_effects=True, vmem_limit_bytes=62 * 1024 * 1024
        ),
        cost_estimate=pl.CostEstimate(
            flops=40 * 1000**3, bytes_accessed=300 * 1000 * 1000, transcendentals=0
        ),
    )(
        starts,
        cosine,
        sine,
        normed.reshape(count, width),
        up.reshape(count, width),
        attn,
        grad_two,
        grad_one,
        old_two,
        old_one,
        part_act,
        tokens,
        full,
    )


def close_kernel(
    dims,
    tokens_hbm,
    up_hbm,
    grads_hbm,
    attn_hbm,
    turned_hbm,
    mixed_hbm,
    part_grad_hbm,
    part_act_hbm,
    full_ref,
    bqkv_ref,
    bone_ref,
    btwo_ref,
    first_act_ref,
    act_ref,
    ingrad_ref,
    out_ref,
    vec_ref,
    norm_ref,
    spread_hbm,
    tokens_v,
    up_v,
    attn_v,
    turned_v,
    mixed_v,
    part_grad_v,
    part_act_v,
    to_core,
    sums,
    coming,
    grads_v,
    landing,
    line_out,
    total_v,
    norm_v,
    norm_seq,
    norm_line,
    vec_in,
    load_sem,
    core_send,
    core_recv,
    axis_send,
    axis_recv,
    line_send,
    line_recv,
    a2a_send,
    a2a_recv,
    vec_send,
    vec_recv,
    norm_send,
    norm_recv,
):
    size, depth, micro, length, width, units, cols = dims
    me, at = lax.axis_index("seq"), lax.axis_index("fsdp")
    count = size.bit_length() - 1
    chips = size // 2
    chip, core = me >> 1, me & 1
    half = width // 2
    per = width // size

    loads = [
        pltpu.make_async_copy(src, dst, load_sem.at[n])
        for n, (src, dst) in enumerate(
            (
                (turned_hbm, turned_v),
                (attn_hbm, attn_v),
                (part_grad_hbm, part_grad_v),
                (part_act_hbm.at[pl.ds(1, micro - 1)], part_act_v),
                (mixed_hbm, mixed_v),
                (tokens_hbm, tokens_v),
                (up_hbm, up_v),
                (grads_hbm, grads_v),
            )
        )
    ]
    for load in loads[7:] + loads[:3]:
        load.start()
    greet(size, depth)

    def line_copy(step, way, part, src):
        number = (step * 2 + (way > 0)) * 2 + part
        return remote(
            src,
            landing.at[number],
            line_send.at[number],
            line_recv.at[number],
            {"fsdp": jnp.clip(at + way, 0, depth - 1)},
        )

    def place_of(way):
        return at if way > 0 else depth - 1 - at

    def chunk(origin, part):
        return grads_v.at[pl.ds(part * chips, chips), origin]

    def origin_of(step, way):
        away = jnp.clip(depth - step + place_of(way), 0, depth - 1)
        return away if way > 0 else depth - 1 - away

    def line_source():
        for step in range(1, depth):
            for part in range(2):
                for way in (1, -1):

                    @pl.when(place_of(way) == 0)
                    def _():
                        line_copy(step, way, part, chunk(origin_of(step, way), part)).start()

    def line_forward(step, part):
        for way in (1, -1):
            place = place_of(way)
            slot = (way > 0) * 2 + part

            @pl.when((place >= 1) & (place <= step - 1) & (place < depth - 1))
            def _():
                arrived = line_copy(step - 1, way, part, line_out.at[slot])
                arrived.wait_recv()

                @pl.when(place <= step - 2)
                def _():
                    arrived.wait_send()

                came = landing[((step - 1) * 2 + (way > 0)) * 2 + part]
                mine = chunk(origin_of(step, way), part)[...]
                line_out[slot] = (mine.astype(F32) + came.astype(F32)).astype(BF)
                line_copy(step, way, part, line_out.at[slot]).start()

    def line_finish(part):
        for way in (1, -1):
            place = place_of(way)
            number = ((depth - 1) * 2 + (way > 0)) * 2 + part

            @pl.when(place >= 1)
            def _():
                line_copy(depth - 1, way, part, line_out.at[0]).wait_recv()

            @pl.when(place == 0)
            def _():
                landing[number] = jnp.zeros_like(landing[number])

        first = (depth - 1) * 4 + part
        summed = chunk(at, part)[...].astype(F32)
        summed = summed + landing[first].astype(F32) + landing[first + 2].astype(F32)
        total_v[pl.ds(part * chips, chips)] = summed.astype(BF)
        for block in range(chips):
            out_ref[:, (part * chips + block) * cols : (part * chips + block + 1) * cols] = summed[
                block, :, 3 * cols :
            ]

    def line_sent():
        for part in range(2):
            for way in (1, -1):
                place = place_of(way)

                @pl.when(place == 0)
                def _():
                    for step in range(1, depth):
                        line_copy(step, way, part, line_out.at[0]).wait_send()

                @pl.when((place >= 1) & (place < depth - 1))
                def _():
                    line_copy(depth - 1, way, part, line_out.at[0]).wait_send()

    def back_copy(step):
        peer = me ^ step
        return remote(
            total_v.at[peer, :, pl.ds(0, 3 * cols)],
            spread_hbm.at[me],
            a2a_send.at[step],
            a2a_recv.at[step],
            {"seq": peer},
        )

    orders = [(0, m) for m in range(micro)] + [(1, m) for m in range(1, micro)]
    found = {}
    for number, (array, m) in enumerate(orders):
        found[array, m] = SeqSum(
            size,
            width,
            to_core.at[number],
            sums.at[number],
            coming.at[number],
            (core_send.at[number], core_recv.at[number]),
            (axis_send, axis_recv),
            number * 2 * (chips - 1),
        )

    over_last = (((1,), (1,)), ((), ()))

    def grad_terms(m):
        def terms(parity, write):
            blocks = pl.ds(parity * chips, chips)
            turned = turned_v[m, blocks].reshape(chips * length, 3 * cols)

            @pl.loop(0, size)
            def _(s):
                columns = pl.ds(pl.multiple_of(s * per, per), per)
                w = attn_v[s, :, :, : 3 * cols].reshape(per, 3 * cols)
                y = lax.dot_general(turned, w, over_last, preferred_element_type=F32)
                y = y.reshape(chips, length, per)
                write(columns, y + part_grad_v[m, blocks, :, columns].astype(F32))

        return terms

    def act_terms(m):
        def terms(parity, write):
            blocks = pl.ds(parity * chips, chips)
            mixed = mixed_v[m, blocks].reshape(chips * length, cols)

            @pl.loop(0, size)
            def _(s):
                columns = pl.ds(pl.multiple_of(s * per, per), per)
                w = attn_v[s, :, :, 3 * cols :].reshape(per, cols)
                y = jnp.dot(mixed, w, preferred_element_type=F32).reshape(chips, length, per)
                write(columns, y + part_act_v[m - 1, blocks, :, columns].astype(F32))

        return terms

    gain = full_ref[0:1, :]
    vec_ref[...] = jnp.zeros_like(vec_ref)
    for part in range(3):
        columns = pl.ds(pl.multiple_of(me * cols, cols), cols)
        vec_ref[2 + part : 3 + part, columns] = bqkv_ref[:, part * cols : (part + 1) * cols]
    vec_ref[5:6, :] = btwo_ref[...]
    norm_v[...] = jnp.zeros_like(norm_v)
    bone_at = pl.multiple_of(lax.rem(me * units, width), units)
    vec_ref[pl.ds(6 + me * units // width, 1), pl.ds(bone_at, units)] = bone_ref[...]

    def norm_back(m):
        x = tokens_v[m].astype(F32)
        dy = found[0, m].last()
        center = x - jnp.mean(x, axis=-1, keepdims=True)
        spread = jnp.mean(center * center, axis=-1, keepdims=True)
        r = lax.rsqrt(spread + EPSILON)
        xhat = center * r
        g = dy * gain
        inner = g - jnp.mean(g, axis=-1, keepdims=True)
        inner = inner - xhat * jnp.mean(g * xhat, axis=-1, keepdims=True)
        ingrad_ref[m] = up_v[m].astype(F32) + r * inner
        norm_v[0:1, :] += jnp.sum(dy * xhat, axis=0, keepdims=True)
        norm_v[1:2, :] += jnp.sum(dy, axis=0, keepdims=True)

    def act_out(m):
        bias = full_ref[5:6, :] + full_ref[6 + size * units // width : 7 + size * units // width, :]
        total = tokens_v[m].astype(F32) + found[1, m].last() + bias
        act_ref[m] = total.astype(BF)

    def norm_seq_copy(step):
        peer = me ^ step
        return remote(
            norm_v.at[:, pl.ds(pl.multiple_of(peer * per, per), per)],
            norm_seq.at[step],
            norm_send.at[step],
            norm_recv.at[step],
            {"seq": peer},
        )

    def norm_line_copy(step):
        number = size + step
        return remote(
            norm_seq.at[0],
            norm_line.at[step],
            norm_send.at[number],
            norm_recv.at[number],
            {"fsdp": lax.rem(at + step, depth)},
        )

    def norm_line_start():
        total = norm_v[:, pl.ds(pl.multiple_of(me * per, per), per)]
        for step in range(1, size):
            norm_seq_copy(step).wait_recv()
            total = total + norm_seq[step]
        norm_seq[0] = total
        for step in range(1, depth):
            norm_line_copy(step).start()

    def norm_finish():
        total = norm_seq[0]
        for step in range(1, depth):
            norm_line_copy(step).wait_recv()
            total = total + norm_line[step]
        norm_ref[...] = total

    levels = [("seq", 1 << bit) for bit in range(count)]

    def vec_line_copy(step):
        number = count + step
        return remote(
            vec_in.at[count],
            vec_in.at[number],
            vec_send.at[number],
            vec_recv.at[number],
            {"fsdp": lax.rem(at + step, depth)},
        )

    def vec_line_start():
        vec_in[count] = vec_ref[...]
        for step in range(1, depth):
            vec_line_copy(step).start()

    def vec_finish():
        for step in range(1, depth):
            copy = vec_line_copy(step)
            copy.wait()
            vec_ref[...] += vec_in[count + step]


    def vec_copy(level):
        axis, step = levels[level]
        mine = me if axis == "seq" else at
        return remote(
            vec_ref,
            vec_in.at[level],
            vec_send.at[level],
            vec_recv.at[level],
            {axis: mine ^ step},
        )

    def vec_level(level):
        copy = vec_copy(level)
        copy.wait()
        vec_ref[...] += vec_in[level]
        if level + 1 < len(levels):
            vec_copy(level + 1).start()

    vec_copy(0).start()
    loads[7].wait()
    line_source()
    vec_level(0)
    for load in loads[:3]:
        load.wait()
    for load in loads[3:7]:
        load.start()
    found[0, 0].away(grad_terms(0))
    vec_level(1)
    found[0, 1].away(grad_terms(1))
    vec_level(2)
    line_forward(2, 0)
    vec_line_start()
    found[0, 0].here(grad_terms(0))
    found[0, 1].here(grad_terms(1))
    for load in loads[3:7]:
        load.wait()
    act_ref[0] = first_act_ref[...]
    found[1, 1].away(act_terms(1))
    line_forward(2, 1)
    found[1, 1].here(act_terms(1))
    found[0, 0].step(0)
    line_forward(3, 0)
    found[0, 1].step(0)
    found[0, 0].add(1)
    norm_back(0)
    line_forward(3, 1)
    found[0, 1].add(1)
    norm_back(1)
    for step in range(1, size):
        norm_seq_copy(step).start()
    found[1, 1].step(0)
    norm_line_start()

    def finish(part):
        line_finish(part)
        for step in range(1, size):
            peer = me ^ step

            @pl.when((peer >= part * chips) & (peer < (part + 1) * chips))
            def _():
                back_copy(step).start()

    finish(0)
    found[1, 1].add(1)
    act_out(1)
    finish(1)
    norm_finish()
    vec_finish()

    back_mine = pltpu.make_async_copy(
        total_v.at[me, :, pl.ds(0, 3 * cols)], spread_hbm.at[me], a2a_recv.at[0]
    )
    back_mine.start()
    back_mine.wait()
    for step in range(1, size):
        back_copy(step).wait_recv()

    line_sent()
    for step in range(1, size):
        norm_seq_copy(step).wait_send()
    for step in range(1, depth):
        norm_line_copy(step).wait_send()
    for step in range(1, size):
        back_copy(step).wait_send()
    for terms in found.values():
        terms.core_sent()
        terms.sent()


def close_layer(
    tokens,
    upstream,
    grads,
    attn,
    turned,
    mixed,
    part_grad,
    part_act,
    full,
    bqkv,
    bone,
    btwo,
    first_act,
):
    size, depth = lax.axis_size("seq"), lax.axis_size("fsdp")
    micro, length, width = tokens.shape
    units, cols = bone.shape[-1], width // size
    rows = width // (size * depth)
    dims = (size, depth, micro, length, width, units, cols)
    chips, count = size // 2, size.bit_length() - 1
    hbm = pl.BlockSpec(memory_space=pl.ANY)
    vmem = pl.BlockSpec(memory_space=pltpu.VMEM)
    dma = pltpu.SemaphoreType.DMA
    levels = count + depth
    piece = (chips, rows, 4 * cols)
    arrays = 2 * micro - 1
    shape = jax.ShapeDtypeStruct
    loaded = [v.shape for v in (tokens, upstream, attn, turned, mixed, part_grad)]
    loaded = loaded + [(micro - 1,) + part_act.shape[1:]]
    return pl.pallas_call(
        functools.partial(close_kernel, dims),
        in_specs=[hbm] * 8 + [vmem] * 5,
        out_specs=[vmem] * 5 + [hbm],
        out_shape=[
            shape(tokens.shape, BF),
            shape(tokens.shape, F32),
            shape((rows, width), F32),
            shape(full.shape, F32),
            shape((8, width // size), F32),
            shape((size, rows, 3 * cols), BF),
        ],
        scratch_shapes=[pltpu.VMEM(s, BF) for s in loaded]
        + [
            pltpu.VMEM((arrays, chips, length, width), BF),
            pltpu.VMEM((arrays, chips, length, width), BF),
            pltpu.VMEM((arrays, chips - 1, length, width), BF),
            pltpu.VMEM(grads.shape, BF),
            pltpu.VMEM((4 * depth,) + piece, BF),
            pltpu.VMEM((4,) + piece, BF),
            pltpu.VMEM((size, rows, 4 * cols), BF),
            pltpu.VMEM((8, width), F32),
            pltpu.VMEM((size, 8, width // size), F32),
            pltpu.VMEM((depth, 8, width // size), F32),
            pltpu.VMEM((levels,) + full.shape, F32),
            dma((9,)),
            dma((arrays,)),
            dma((arrays,)),
            dma((2 * arrays * (chips - 1),)),
            dma((2 * arrays * (chips - 1),)),
            dma((4 * depth,)),
            dma((4 * depth,)),
            dma((size,)),
            dma((size,)),
            dma((levels,)),
            dma((levels,)),
            dma((size + depth,)),
            dma((size + depth,)),
        ],
        compiler_params=pltpu.CompilerParams(
            collective_id=4, has_side_effects=True, vmem_limit_bytes=63 * 1024 * 1024
        ),
        cost_estimate=pl.CostEstimate(
            flops=30 * 1000**3, bytes_accessed=300 * 1000 * 1000, transcendentals=0
        ),
    )(
        tokens,
        upstream,
        grads,
        attn,
        turned,
        mixed,
        part_grad,
        part_act,
        full,
        bqkv,
        bone,
        btwo,
        first_act,
    )


def result_kernel(
    dims,
    place_ref,
    act_ref,
    ingrad_ref,
    out_ref,
    two_ref,
    one_ref,
    qkv_ref,
    vec_ref,
    norm_ref,
    act_to,
    ingrad_to,
    gain_ref,
    shift_ref,
    wqkv_ref,
    bqk_ref,
    bv_ref,
    out_to,
    bout_ref,
    one_to,
    bone_ref,
    two_to,
    btwo_ref,
):
    size, depth, width, cols, units = dims
    for source, target in (
        (ingrad_ref, ingrad_to),
        (two_ref, two_to),
        (act_ref, act_to),
        (out_ref, out_to),
    ):
        target[...] = source[...]
    for s in range(size):
        one_to[:, s * units : (s + 1) * units] = one_ref[s].astype(F32)
        for part in range(3):
            start = part * width + s * cols
            wqkv_ref[:, start : start + cols] = qkv_ref[s, :, part * cols : (part + 1) * cols].astype(
                F32
            )
    index = place_ref[0]

    def own(row, total, target):
        extent = total // (size * depth)
        flat = index * extent
        at = lax.rem(flat, width)
        values = vec_ref[pl.ds(row + flat // width, 1), :]
        values = pltpu.roll(values, lax.rem(width - at, width), 1)
        target[...] = values[:, :extent]

    per = width // size
    extent = per // depth
    norms = pltpu.roll(norm_ref[...], lax.rem(per - lax.rem(index, depth) * extent, per), 1)
    gain_ref[...] = norms[0:1, :extent]
    shift_ref[...] = norms[1:2, :extent]
    own(2, 2 * width, bqk_ref)
    own(4, width, bv_ref)
    own(5, width, bout_ref)
    own(5, width, btwo_ref)
    own(6, size * units, bone_ref)


def results(
    activations, input_grad, grad_out, grad_two, spread_one, spread_qkv, vectors, norms, index
):
    size, rows, units = spread_one.shape
    width = vectors.shape[-1]
    depth = width // (size * rows)
    cols = width // size
    dims = (size, depth, width, cols, units)
    vmem = pl.BlockSpec(memory_space=pltpu.VMEM)

    def row(extent):
        return jax.ShapeDtypeStruct((1, extent // (size * depth)), F32)

    def like(value):
        return jax.ShapeDtypeStruct(value.shape, value.dtype)

    wide = jax.ShapeDtypeStruct((rows, size * units), F32)
    shapes = [
        like(activations),
        like(input_grad),
        row(width),
        row(width),
        jax.ShapeDtypeStruct((rows, 3 * width), F32),
        row(2 * width),
        row(width),
        like(grad_out),
        row(width),
        wide,
        row(size * units),
        like(grad_two),
        row(width),
    ]
    return pl.pallas_call(
        functools.partial(result_kernel, dims),
        in_specs=[pl.BlockSpec(memory_space=pltpu.SMEM)] + [vmem] * 8,
        out_specs=[vmem] * len(shapes),
        out_shape=shapes,
        compiler_params=pltpu.CompilerParams(vmem_limit_bytes=60 * 1024 * 1024),
    )(
        index[None],
        activations,
        input_grad,
        grad_out,
        grad_two,
        spread_one,
        spread_qkv,
        vectors,
        norms,
    )


def gelu_tanh(values):
    return jax.nn.gelu(values, approximate=True)


def layer_norm(values, gain, shift):
    center = values - jnp.mean(values, axis=-1, keepdims=True)
    spread = jnp.mean(center * center, axis=-1, keepdims=True)
    return center * lax.rsqrt(spread + EPSILON) * gain + shift


def fence(*values):
    return lax.optimization_barrier(values)


def line_right(value, senders):
    return lax.ppermute(value, "fsdp", [(i, i + 1) for i in senders])


def line_left(value, senders):
    last = lax.axis_size("fsdp") - 1
    return lax.ppermute(value, "fsdp", [(last - i, last - i - 1) for i in senders])


class Gather:
    def __init__(self, mine):
        self.right, self.left = [mine], [mine]

    def step(self):
        size = lax.axis_size("fsdp")
        number = len(self.right)
        if number < size:
            self.right.append(line_right(self.right[-1], range(number - 1, size - 1)))
            self.left.append(line_left(self.left[-1], range(number - 1, size - 1)))

    def fence(self, *others):
        (self.right[-1], self.left[-1]), *others = fence((self.right[-1], self.left[-1]), *others)
        return others

    def rest(self):
        while len(self.right) < lax.axis_size("fsdp"):
            self.step()

    def pieces(self):
        size = lax.axis_size("fsdp")
        at = lax.axis_index("fsdp")
        found = [(self.right[0], at)]
        for step in range(1, size):
            piece = jnp.where(at >= step, self.right[step], self.left[size - step])
            found.append((piece, lax.rem(at - step + size, size)))
        return found


class Scatter:
    def __init__(self, chunk):
        self.chunk = chunk
        self.number = 0
        self.right = self.left = None

    def step(self):
        size = lax.axis_size("fsdp")
        at = lax.axis_index("fsdp")
        if self.number == size - 1:
            return
        self.number += 1
        going = self.chunk(jnp.minimum(size - self.number + at, size - 1))
        coming = self.chunk(jnp.maximum(self.number - size + at, 0))
        if self.number > 1:
            going = (going.astype(F32) + self.right.astype(F32)).astype(BF)
            coming = (coming.astype(F32) + self.left.astype(F32)).astype(BF)
        self.right = line_right(going, range(self.number))
        self.left = line_left(coming, range(self.number))

    def rest(self):
        while self.number < lax.axis_size("fsdp") - 1:
            self.step()

    def fence(self, *others):
        (self.right, self.left), *others = fence((self.right, self.left), *others)
        return others

    def total(self):
        mine = self.chunk(lax.axis_index("fsdp")).astype(F32)
        return mine + self.right.astype(F32) + self.left.astype(F32)


def staged_layer(
    tokens, upstream, w_fc2, w_qkv, w_out, starts, normed, up, my_one, two_near, full, index
):
    size, depth = lax.axis_size("seq"), lax.axis_size("fsdp")
    me = lax.axis_index("seq")
    micro, length, width = tokens.shape
    rows = width // (size * depth)
    hidden_rows = w_fc2.shape[0]
    cols = width // size
    units = hidden_rows * depth
    count = micro * size * length

    def contract_last(left, right):
        return lax.dot_general(left, right, (((1,), (1,)), ((), ())), preferred_element_type=F32)

    def contract_first(left, right):
        return lax.dot_general(left, right, (((0,), (0,)), ((), ())), preferred_element_type=F32)

    def place_columns(pieces):
        out = jnp.zeros((size, depth) + pieces[0][0].shape[1:], BF)
        for piece, origin in pieces:
            out = lax.dynamic_update_slice_in_dim(out, piece[:, None], origin, 1)
        return out

    def place_rows(pieces):
        out = jnp.zeros((depth,) + pieces[0][0].shape, BF)
        for piece, origin in pieces:
            out = lax.dynamic_update_slice_in_dim(out, piece[None], origin, 0)
        return out

    normed = normed.reshape(count, width)
    up = up.reshape(count, width)
    my_one = my_one.reshape(width, units)
    two = Gather(w_fc2)
    at = lax.axis_index("fsdp")
    for way, found in ((-1, two.right), (1, two.left)):
        origin = jnp.clip(at + way, 0, depth - 1)
        found.append(lax.dynamic_index_in_dim(two_near, origin, 0, keepdims=False))
    gain, shift, bias_out = full[0], full[1], full[5]
    bias_qkv = lax.dynamic_slice_in_dim(full[2:5], me * cols, cols, 1).reshape(-1)
    ratio = size * units // width
    bias_one = lax.dynamic_slice_in_dim(full[6 : 6 + ratio].reshape(-1), me * units, units, 0)
    bias_two = full[6 + ratio]
    two.step()
    split = w_qkv.reshape(rows, 3, size, cols).transpose(2, 0, 1, 3).reshape(size, rows, 3 * cols)
    attn_cols = lax.all_to_all(split, "seq", 0, 0, tiled=True)
    out_cols = w_out.reshape(rows, size, cols).transpose(1, 0, 2)
    attn_cols = jnp.concatenate([attn_cols, out_cols], axis=-1)
    pre = jnp.dot(normed, my_one, preferred_element_type=F32) + bias_one
    hidden, back = jax.vjp(gelu_tanh, pre)
    hidden = hidden.astype(BF)
    grad_two = contract_first(hidden, up).astype(BF).reshape(depth, hidden_rows, width)
    hidden, grad_two = two.fence(hidden, grad_two)
    two.step()
    sum_two = Scatter(lambda o: lax.dynamic_index_in_dim(grad_two, o, 0, keepdims=False))
    sum_two.step()
    (two.right, two.left), (sum_two.right, sum_two.left), attn_cols = fence(
        (two.right, two.left), (sum_two.right, sum_two.left), attn_cols
    )
    attn = Gather(attn_cols)
    attn.step()
    two.rest()
    my_two = place_rows(two.pieces()).reshape(units, width)
    pre_grad = back(contract_last(up, my_two))[0].astype(BF)
    grad_one = contract_first(normed, pre_grad).astype(BF).reshape(size, depth, rows, units)
    pre_grad, grad_one = attn.fence(pre_grad, grad_one)
    attn.step()
    sum_one = Scatter(lambda o: lax.dynamic_index_in_dim(grad_one, o, 1, keepdims=False))
    sum_one.step()
    (sum_one.right, sum_one.left), (sum_two.right, sum_two.left) = attn.fence(
        (sum_one.right, sum_one.left), (sum_two.right, sum_two.left)
    )
    attn.step()
    sum_two.step()
    (sum_two.right, sum_two.left), normed, up = attn.fence(
        (sum_two.right, sum_two.left), normed, up
    )
    sum_two.step()
    attn.rest()
    attn_weights = place_columns(attn.pieces())
    my_qkv = attn_weights[..., : 3 * cols].reshape(width, 3 * cols)
    my_out = attn_weights[..., 3 * cols :].transpose(1, 2, 0, 3).reshape(cols, width)
    projected = jnp.dot(normed, my_qkv, preferred_element_type=F32) + bias_qkv
    projected = projected.reshape(micro, size, length, 3 * cols)
    mixed_grad = contract_last(up, my_out).astype(BF).reshape(micro, size, length, cols)
    parts = [attention(starts[:1], projected[:1], mixed_grad[:1])]
    (sum_one.right, sum_one.left), (projected, mixed_grad), parts = sum_two.fence(
        (sum_one.right, sum_one.left), (projected, mixed_grad), parts
    )
    sum_one.step()
    for m in range(1, micro):
        parts.append(attention(starts[m:][:1], projected[m:][:1], mixed_grad[m:][:1]))
    mixed = jnp.concatenate([part[0] for part in parts]).reshape(count, cols)
    projected_grad = jnp.concatenate(
        [jnp.concatenate(part[1:], axis=-1) for part in parts]
    ).reshape(count, 3 * cols)
    projected_grad, mixed = sum_one.fence(projected_grad, mixed)
    sum_one.step()
    grad_qkv = contract_first(normed, projected_grad).astype(BF).reshape(size, depth, rows, 3 * cols)
    grad_out = contract_first(mixed, up).astype(BF).reshape(depth, rows, size, cols)
    grad_qkv, grad_out, (sum_two.right, sum_two.left) = sum_one.fence(
        grad_qkv, grad_out, (sum_two.right, sum_two.left)
    )
    grad_attn = jnp.concatenate([grad_qkv, grad_out.transpose(2, 0, 1, 3)], axis=-1)

    def to_rows(mine, parts):
        mine = lax.all_to_all(mine.astype(BF), "seq", 0, 0, tiled=True).astype(F32)
        return mine.reshape(size, rows, parts, -1).transpose(1, 2, 0, 3).reshape(rows, -1)

    sum_one.rest()
    sum_two.rest()
    out_two = sum_two.total()
    out_one = to_rows(sum_one.total(), 1)

    def put(values, extent, at):
        return lax.dynamic_update_slice_in_dim(jnp.zeros(extent, F32), values, at, -1)

    bqkv = jnp.sum(projected_grad.astype(F32), axis=0).reshape(3, cols)
    bqkv = put(bqkv, (3, width), me * cols)
    bone = put(jnp.sum(pre_grad.astype(F32), axis=0), (size * units,), me * units)
    btwo = jnp.sum(upstream.astype(F32), axis=(0, 1))[None]
    early = [jnp.zeros((2, width), F32), bqkv, btwo, bone.reshape(ratio, width)]
    early = jnp.pad(jnp.concatenate(early), ((0, full.shape[0] - 6 - ratio), (0, 0)))

    sum_attn = Scatter(lambda o: lax.dynamic_index_in_dim(grad_attn, o, 1, keepdims=False))
    sum_attn.step()
    grad_terms = contract_last(projected_grad, my_qkv) + contract_last(pre_grad, my_one)
    grad_terms = grad_terms.astype(BF).reshape(micro, size, length, width)
    (grad_terms,) = sum_attn.fence(grad_terms)
    sum_attn.step()
    normed_grad = scatter_seq(grad_terms)
    terms = jnp.dot(mixed, my_out, preferred_element_type=F32)
    terms = terms + jnp.dot(hidden, my_two, preferred_element_type=F32)
    terms = terms.astype(BF).reshape(micro, size, length, width)
    sums = scatter_seq(terms)
    sum_attn.rest()
    attn_total = sum_attn.total()
    out_qkv = to_rows(attn_total[..., : 3 * cols], 3)
    out_out = attn_total[..., 3 * cols :].transpose(1, 0, 2).reshape(rows, width)
    activations = (tokens.astype(F32) + sums + (bias_out + bias_two)).astype(BF)
    _, norm_back = jax.vjp(layer_norm, tokens.astype(F32), gain, shift)
    input_grad, gain_grad, shift_grad = norm_back(normed_grad)
    input_grad = input_grad + upstream.astype(F32)
    vectors = early.at[:2].add(jnp.stack([gain_grad, shift_grad]))
    vectors = lax.psum(vectors, ("seq", "fsdp"))

    return activations, input_grad, out_qkv, out_out, vectors, out_one, out_two


def per_device(
    tokens,
    ln_gain,
    ln_bias,
    w_qkv,
    b_qkv,
    w_out,
    b_out,
    w_fc1,
    b_fc1,
    w_fc2,
    b_fc2,
    piece_starts,
    cotangent,
):
    size, depth = lax.axis_size("seq"), lax.axis_size("fsdp")
    me = lax.axis_index("seq")
    micro, _, length, width = tokens.shape
    rows = width // (size * depth)
    hidden_rows = w_fc2.shape[0]
    cols = width // size
    units = hidden_rows * depth
    count = micro * size * length
    tokens = tokens[:, 0]
    upstream = cotangent[:, 0]

    index = me * depth + lax.axis_index("fsdp")
    packed = []
    for vector in (ln_gain, ln_bias, b_qkv, b_out, b_fc1, b_fc2):
        mine = jnp.arange(size * depth, dtype=jnp.int32)[:, None] == index
        packed.append(jnp.where(mine, vector[None, :], 0).astype(BF).reshape(-1, width))
    packed = jnp.concatenate(packed, axis=0)
    packed = jnp.pad(packed, ((0, -packed.shape[0] % 16), (0, 0)))
    starts = piece_starts[:, 0]
    loaded = load_all(tokens, upstream, w_fc1, w_fc2, packed)
    if (size, depth, micro) == (8, 4, 2):
        normed, up, one, two_near, full = loaded
        part_grad, part_act, attn, grad_two, grad_one, land_two, land_one, *sums = feed_forward(
            normed, up, one, two_near, w_qkv, w_out, full
        )
        wide = (micro, size, length, -1)
        part_act = part_act.reshape(wide)
        turned, mixed, grads, spread_one, _, _, bqkv, out_two, first_act = attention_layer(
            starts,
            normed,
            up,
            attn,
            grad_two,
            grad_one,
            land_two,
            land_one,
            part_act,
            tokens,
            full,
        )
        activations, input_grad, out_out, vectors, norms, spread_qkv = close_layer(
            tokens,
            upstream,
            grads,
            attn,
            turned.reshape(wide),
            mixed.reshape(wide),
            part_grad.reshape(wide),
            part_act,
            full,
            bqkv,
            *sums,
            first_act,
        )

        found = results(
            activations, input_grad, out_out, out_two, spread_one, spread_qkv, vectors, norms, index
        )
        found = [v.reshape(-1) if n in (2, 3, 5, 6, 8, 10, 12) else v for n, v in enumerate(found)]
        return (found[0][:, None], found[1][:, None]) + tuple(found[2:])

    activations, input_grad, out_qkv, out_out, vectors, out_one, out_two = staged_layer(
        tokens, upstream, w_fc2, w_qkv, w_out, starts, *loaded, index
    )
    ratio = w_fc1.shape[1] // width

    def own(values):
        values = values.reshape(-1)
        extent = values.shape[0] // (size * depth)
        return lax.dynamic_slice_in_dim(values, index * extent, extent, 0)

    grad_b_two = own(vectors[5])
    return (
        activations[:, None],
        input_grad[:, None],
        own(vectors[0]),
        own(vectors[1]),
        out_qkv,
        own(vectors[2:4]),
        own(vectors[4]),
        out_out,
        grad_b_two,
        out_one,
        own(vectors[6 : 6 + ratio]),
        out_two,
        grad_b_two,
    )


def solution(mesh):
    both = ("seq", "fsdp")
    row = P(both)
    matrix = P(both, None)
    tokens = P(None, "fsdp", "seq", None)
    weights = (row, row, matrix, row, matrix, row, matrix, row, matrix, row)
    grads = (row, row, matrix, row, row, matrix, row, matrix, row, matrix, row)
    return jax.shard_map(
        per_device,
        mesh=mesh,
        in_specs=(tokens,) + weights + (P(None, "fsdp", None), tokens),
        out_specs=(tokens, tokens) + grads,
        check_vma=False,
    )
```
